32 devices in a mesh: az: 8 (over z, core), rg: 4 (over y, x).
Axes of the slice: x: 2, y: 2, z: 4, core: 2. Of those that a mesh axis runs over, the one named last changes fastest.
Arguments:
- raw_echoes: float32 [128, 4, 2, 8192], P(('az', 'rg')), may hold values from -6 to 6
- chirp_spectrum: float32 [2, 8192], replicated, may hold values from -5 to 5
- reconstruction: float32 [2, 4, 4, 128], replicated, may hold values from -2 to 2
- delays: int32 [4], replicated, may hold values from 0 to 127
- azimuth_rate: float32 [8192], P(('az', 'rg')), may hold values from 0.5 to 2
- band_halfwidth: int32 [8192], P(('az', 'rg')), may hold values from 64 to 256
- migration: int32 [8192], P(('az', 'rg')), may hold values from 8 to 16
Outputs:
- focused_image: float32 [2, 8192, 512], P(None, ('az', 'rg'))
The draws below stay inside these ranges and needn't reach their ends.
All inputs are finite; a program needn't handle non-finite values.
Results may differ from the reference program's by a relative error of at most 0.00007.
Values sent between devices are 32-bit elements; how exact they have to be, the bound alone decides.
A program may use at most 64 MiB of HBM per device.

```python
import math
import jax
import jax.numpy as jnp
from jax import lax

NCH = 4
NR = 8192
MIG = 16
PULSES = 128
DOPPLER = 512


def set_ends(values, own_key, low, high):
    index_at = [jax.random.randint(jax.random.fold_in(own_key, axis), (), 0, length) for axis, length in enumerate(values.shape)]
    main_axis = values.shape.index(max(values.shape))
    neighbour = index_at[:main_axis] + [(index_at[main_axis] + 1) % values.shape[main_axis]] + index_at[main_axis + 1:]
    return values.at[tuple(index_at)].set(low).at[tuple(neighbour)].set(high)


def levels(own_key, extent, cuts, smallest, top_value):
    def one(axis_at, shards_of):
        steps = jax.random.uniform(jax.random.fold_in(jax.random.fold_in(own_key, 6), axis_at), (shards_of,), jnp.float32, smallest / len(cuts), top_value / len(cuts))
        return jnp.repeat(jnp.exp(steps), extent[axis_at] // shards_of).reshape((-1,) + (1,) * (len(extent) - axis_at - 1))

    factor_of = one(*cuts[0])
    for cut in cuts[1:]:
        factor_of = factor_of * one(*cut)
    return factor_of


def scatter_about(rng, extent, width, most, shards=(), kind=jnp.bfloat16):
    gain = levels(rng, extent, shards, -0.22, 0.18) if shards else 1.0
    values = jax.random.normal(rng, extent, jnp.float32) * width * gain
    return jnp.minimum(jnp.maximum(values, -most), most).astype(kind)


def setup_inputs(seed: int = 0) -> dict:
    splits = jax.random.split(jax.random.key(seed), 8)
    raw_echoes = scatter_about(splits[0], (PULSES, NCH, 2, NR), 1.0, 6.0, ((0, 32),), jnp.float32)
    chirp_spectrum = scatter_about(splits[1], (2, NR), 0.7071, 5.0, (), jnp.float32)
    reconstruction = scatter_about(splits[2], (2, NCH, NCH, PULSES), 0.35, 2.0, (), jnp.float32)
    delays = set_ends(jax.random.randint(splits[3], (NCH,), 0, PULSES), jax.random.fold_in(splits[3], 1), 0, PULSES - 1).astype(jnp.int32)
    azimuth_rate = jnp.clip(jnp.exp(math.log(2.0) - 1.3862944 * jax.random.uniform(splits[4], (NR,), jnp.float32) ** levels(splits[4], (NR,), ((0, 32),), -0.2, 0.2)), 0.5, 2.0)
    band_halfwidth = set_ends(jax.random.randint(splits[5], (NR,), DOPPLER // 8, DOPPLER // 2 + 1), jax.random.fold_in(splits[5], 1), DOPPLER // 8, (DOPPLER // 2 + 1) - 1).astype(jnp.int32)
    migration = set_ends(jax.random.randint(splits[6], (NR,), MIG // 2, MIG + 1), jax.random.fold_in(splits[6], 1), MIG // 2, MIG).astype(jnp.int32)
    return {"raw_echoes": raw_echoes, "chirp_spectrum": chirp_spectrum, "reconstruction": reconstruction, "delays": delays, "azimuth_rate": azimuth_rate, "band_halfwidth": band_halfwidth, "migration": migration}


curvature = 32.0

def reference(raw_echoes, chirp_spectrum, reconstruction, delays, azimuth_rate, band_halfwidth, migration):
    signal = lax.complex(raw_echoes[:, :, 0], raw_echoes[:, :, 1])
    spectrum = jnp.fft.fft(signal, axis=2)
    compressed = jnp.fft.ifft(spectrum * lax.complex(chirp_spectrum[0], -chirp_spectrum[1]), axis=2)
    doppler = jnp.fft.fft(compressed, axis=0) / math.sqrt(PULSES)
    frequency = jnp.arange(PULSES, dtype=jnp.int32)
    angle_turns = frequency[None, :] * delays[:, None] % PULSES
    angles = 2.0 * math.pi / PULSES * angle_turns.astype(jnp.float32)
    alignment = lax.complex(jnp.cos(angles), jnp.sin(angles))
    mixing = lax.complex(reconstruction[0], reconstruction[1]) * alignment[None]
    unfolded = jnp.einsum('bcf,fcr->bfr', mixing, doppler, precision=lax.Precision.HIGHEST)
    unfolded = unfolded.reshape(DOPPLER, NR)
    padded = jnp.pad(unfolded, ((0, 0), (0, MIG)))
    doppler_index = jnp.arange(DOPPLER, dtype=jnp.int32)
    centred = doppler_index - DOPPLER * (doppler_index >= DOPPLER // 2).astype(jnp.int32)
    band_square = band_halfwidth * band_halfwidth
    squared = jnp.minimum((centred * centred)[None, :], band_square[:, None])
    migration_shift = (migration[:, None] * squared + (band_square // 2)[:, None]) // band_square[:, None]
    source_rows = jnp.arange(NR, dtype=jnp.int32)[:, None] + migration_shift
    migrated = jnp.take_along_axis(padded, source_rows.T, axis=1).T
    relative = centred.astype(jnp.float32) / (DOPPLER // 2)
    matched_phase = math.pi * curvature * azimuth_rate[:, None] * (relative * relative)[None, :]
    inside = jnp.abs(centred)[None, :] < band_halfwidth[:, None]
    focused = jnp.where(inside, migrated * lax.complex(jnp.cos(matched_phase), jnp.sin(matched_phase)), 0.0)
    focused_image = jnp.fft.ifft(focused, axis=1) * math.sqrt(DOPPLER)
    return jnp.stack([jnp.real(focused_image), jnp.imag(focused_image)]).astype(jnp.float32)
```

```python
import functools
import math

import jax
import jax.numpy as jnp
import ml_dtypes
import numpy as np
from jax import lax
from jax.experimental import pallas as pl
from jax.experimental.pallas import tpu as pltpu
from jax.sharding import PartitionSpec as P

MIG = 16
LANES = 128
HALO_ROWS = 8


highest = lax.Precision.HIGHEST
curvature = 32.0


def passed_along(value, axis, by):
    size = lax.axis_size(axis)
    pairs = [(i, i + by) for i in range(size) if 0 <= i + by < size]
    return lax.ppermute(value, axis, pairs)


def factor_pair(length):
    largest = 1
    for candidate in range(1, length + 1):
        if candidate * candidate > length:
            break
        if length % candidate == 0:
            largest = candidate
    return (largest, length // largest)


def dft_matrix(length, direction):
    indices = jnp.arange(length, dtype=jnp.int32)
    angles = (
        2.0 * math.pi / length * (indices[:, None] * indices[None, :] % length).astype(jnp.float32)
    )
    cosine = jnp.cos(angles)
    sines = direction * jnp.sin(angles)
    return jnp.stack(
        [jnp.stack([cosine, -sines], axis=1), jnp.stack([sines, cosine], axis=1)], axis=0
    )


def twiddle(lead_size, trail_size, length, direction):
    lead_index = jnp.arange(lead_size, dtype=jnp.int32)
    trail_index = jnp.arange(trail_size, dtype=jnp.int32)
    angles = (
        2.0
        * math.pi
        / length
        * (lead_index[:, None] * trail_index[None, :] % length).astype(jnp.float32)
    )
    return (jnp.cos(angles), direction * jnp.sin(angles))


def complex_mul(values, factor_real, factor_imag, part_axis):
    real_part = lax.index_in_dim(values, 0, part_axis, keepdims=True)
    imag_part = lax.index_in_dim(values, 1, part_axis, keepdims=True)
    return jnp.concatenate(
        [
            real_part * factor_real - imag_part * factor_imag,
            real_part * factor_imag + imag_part * factor_real,
        ],
        axis=part_axis,
    )


def range_focus(raw_echoes, chirp_spectrum):
    local_pulses, channels, _, length = raw_echoes.shape
    lead_size, trail_size = factor_pair(length)
    layout = raw_echoes.reshape(local_pulses, channels, 2, lead_size, trail_size)
    sectioned = jnp.einsum(
        "okci,pqcij->pqokj", dft_matrix(lead_size, -1.0), layout, precision=highest
    )
    twiddle_real, twiddle_imag = twiddle(lead_size, trail_size, length, -1.0)
    sectioned = complex_mul(sectioned, twiddle_real, twiddle_imag, 2)
    spectrum = jnp.einsum(
        "olcj,pqckj->pqolk", dft_matrix(trail_size, -1.0), sectioned, precision=highest
    )
    spectrum = spectrum.reshape(local_pulses, channels, 2, length)
    spectrum = complex_mul(spectrum, chirp_spectrum[0], -chirp_spectrum[1], 2)
    layout = spectrum.reshape(local_pulses, channels, 2, lead_size, trail_size)
    sectioned = jnp.einsum(
        "okci,pqcij->pqokj", dft_matrix(lead_size, 1.0), layout, precision=highest
    )
    twiddle_real, twiddle_imag = twiddle(lead_size, trail_size, length, 1.0)
    sectioned = complex_mul(sectioned, twiddle_real, twiddle_imag, 2)
    restored = jnp.einsum(
        "olcj,pqckj->qoplk", dft_matrix(trail_size, 1.0), sectioned, precision=highest
    )
    return restored.reshape(channels, 2, local_pulses, length) / length


def reconstruct(turned, mixing_real, mixing_imag):
    channels, _, local_pulses, blocks, bin_count = turned.shape
    pulse_total = blocks * local_pulses
    sectioned = jnp.einsum("okcm,qcimb->qobik", dft_matrix(blocks, -1.0), turned, precision=highest)
    twiddle_real, twiddle_imag = twiddle(local_pulses, blocks, pulse_total, -1.0)
    sectioned = complex_mul(sectioned, twiddle_real, twiddle_imag, 1)
    spectrum = jnp.einsum(
        "olci,qcbik->qoblk", dft_matrix(local_pulses, -1.0), sectioned, precision=highest
    )
    spectrum = spectrum.reshape(channels, 2, bin_count, pulse_total) / math.sqrt(pulse_total)
    spec_real = spectrum[:, 0]
    spec_imag = spectrum[:, 1]
    unfolded_real = jnp.einsum(
        "bcf,crf->rbf", mixing_real, spec_real, precision=highest
    ) - jnp.einsum("bcf,crf->rbf", mixing_imag, spec_imag, precision=highest)
    unfolded_imag = jnp.einsum(
        "bcf,crf->rbf", mixing_real, spec_imag, precision=highest
    ) + jnp.einsum("bcf,crf->rbf", mixing_imag, spec_real, precision=highest)
    unfolded = jnp.stack([unfolded_real, unfolded_imag], axis=0)
    return unfolded.reshape(2, bin_count, channels * pulse_total)


def azimuth_focus(unfolded, azimuth_rate, band_halfwidth, migration):
    bin_count = azimuth_rate.shape[0]
    length = unfolded.shape[2]
    doppler_index = jnp.arange(length, dtype=jnp.int32)
    centred = doppler_index - length * (doppler_index >= length // 2).astype(jnp.int32)
    band_square = band_halfwidth * band_halfwidth
    squared = jnp.minimum((centred * centred)[None, :], band_square[:, None])
    migration_shift = (migration[:, None] * squared + (band_square // 2)[:, None]) // band_square[
        :, None
    ]
    migrated = jnp.zeros((2, bin_count, length), jnp.float32)
    for offset in range(MIG + 1):
        window = unfolded[:, offset : offset + bin_count, :]
        migrated = jnp.where((migration_shift == offset)[None], window, migrated)
    relative = centred.astype(jnp.float32) / (length // 2)
    matched_phase = math.pi * curvature * azimuth_rate[:, None] * (relative * relative)[None, :]
    focused = complex_mul(migrated, jnp.cos(matched_phase), jnp.sin(matched_phase), 0)
    inside = jnp.abs(centred)[None, :] < band_halfwidth[:, None]
    focused = jnp.where(inside[None], focused, 0.0)
    lead_size, trail_size = factor_pair(length)
    layout = focused.reshape(2, bin_count, lead_size, trail_size)
    sectioned = jnp.einsum("okci,cbij->obkj", dft_matrix(lead_size, 1.0), layout, precision=highest)
    twiddle_real, twiddle_imag = twiddle(lead_size, trail_size, length, 1.0)
    sectioned = complex_mul(sectioned, twiddle_real, twiddle_imag, 0)
    focused_image = jnp.einsum(
        "olcj,cbkj->oblk", dft_matrix(trail_size, 1.0), sectioned, precision=highest
    )
    return focused_image.reshape(2, bin_count, length) / math.sqrt(length)


def plain_local(
    raw_echoes, chirp_spectrum, reconstruction, delays, azimuth_rate, band_halfwidth, migration
):
    compressed = range_focus(raw_echoes, chirp_spectrum)
    channels, _, local_pulses, length = compressed.shape
    azimuth_count = lax.axis_size("az")
    range_count = lax.axis_size("rg")
    bin_count = length // (azimuth_count * range_count)
    layout = compressed.reshape(channels, 2, local_pulses, azimuth_count, range_count, bin_count)
    layout = lax.all_to_all(layout, "rg", split_axis=4, concat_axis=4, tiled=True)
    layout = lax.all_to_all(layout, "az", split_axis=3, concat_axis=3, tiled=True)
    turned = layout.reshape(channels, 2, local_pulses, azimuth_count * range_count, bin_count)
    pulse_total = azimuth_count * range_count * local_pulses
    frequency = jnp.arange(pulse_total, dtype=jnp.int32)
    angles = (
        2.0
        * math.pi
        / pulse_total
        * (frequency[None, :] * delays[:, None] % pulse_total).astype(jnp.float32)
    )
    align_real = jnp.cos(angles)[None]
    align_imag = jnp.sin(angles)[None]
    mixing_real = reconstruction[0] * align_real - reconstruction[1] * align_imag
    mixing_imag = reconstruction[0] * align_imag + reconstruction[1] * align_real
    unfolded = reconstruct(turned, mixing_real, mixing_imag)
    margin_bins = passed_along(unfolded[:, :MIG, :], ("az", "rg"), -1)
    unfolded = jnp.concatenate([unfolded, margin_bins], axis=1)
    return azimuth_focus(unfolded, azimuth_rate, band_halfwidth, migration)


def split_constant(values):
    high = values.astype(ml_dtypes.bfloat16)
    low = (values - high.astype(np.float64)).astype(ml_dtypes.bfloat16)
    return np.stack([high, low])


def roots(rows, columns, length, direction):
    turns = (rows[:, None] * columns[None, :]) % length
    angles = 2.0 * np.pi / length * turns
    return np.cos(angles), direction * np.sin(angles)


def left_matrix(cosine, sine):
    return np.stack([np.stack([cosine, -sine], 1), np.stack([sine, cosine], 1)], 0)


def right_matrix(cosine, sine):
    return np.stack([np.stack([cosine, sine], 1), np.stack([-sine, cosine], 1)], 0)


def split(values):
    high = values.astype(jnp.bfloat16)
    low = (values - high.astype(jnp.float32)).astype(jnp.bfloat16)
    return high, low


def dot(a, b):
    return jnp.dot(a, b, preferred_element_type=jnp.float32)


def dot_right(values, matrix):
    high, low = split(values)
    return dot(high, matrix[0]) + (dot(low, matrix[0]) + dot(high, matrix[1]))


def dot_left(matrix, values):
    high, low = split(values)
    return dot(matrix[0], high) + (dot(matrix[1], high) + dot(matrix[0], low))


def cos_sin_turns(turns):
    quarter = jnp.floor(turns * 4.0 + 0.5)
    theta = (turns - quarter * 0.25) * (2.0 * math.pi)
    square = theta * theta
    cosine = 1.0 + square * (
        -0.5 + square * (1.0 / 24 + square * (-1.0 / 720 + square * (1.0 / 40320)))
    )
    sine = theta * (
        1.0
        + square
        * (-1.0 / 6 + square * (1.0 / 120 + square * (-1.0 / 5040 + square * (1.0 / 362880))))
    )
    index = quarter.astype(jnp.int32)
    odd = (index & 1) == 1
    cos_negative = ((index + 1) & 2) == 2
    sin_negative = (index & 2) == 2
    cos_size = jnp.where(odd, sine, cosine)
    sin_size = jnp.where(odd, cosine, sine)
    return (
        jnp.where(cos_negative, -cos_size, cos_size),
        jnp.where(sin_negative, -sin_size, sin_size),
    )


def range_kernel(
    sizes, x_ref, chirp_ref, first_ref, twiddle_ref, fwd_ref, inv_ref, last_ref, halo_ref, out_ref
):
    pulses, channels, lead, devices = sizes
    tw_r = jnp.concatenate([twiddle_ref[0]] * channels, axis=0)
    tw_i = jnp.concatenate([twiddle_ref[1]] * channels, axis=0)
    chirp_r = jnp.concatenate([chirp_ref[0]] * channels, axis=0)
    chirp_i = jnp.concatenate([chirp_ref[1]] * channels, axis=0)
    lane = lax.broadcasted_iota(jnp.int32, (2 * lead, LANES), 1)
    groups = pulses * channels * MIG // LANES
    per_group = LANES // MIG
    packs = [jnp.zeros((2 * lead, LANES), jnp.float32) for _ in range(groups)]
    for p in range(pulses):
        x = jnp.concatenate([x_ref[p * channels + c] for c in range(channels)], axis=1)
        y = dot_left(first_ref, x)
        y = jnp.concatenate([y[:, c * LANES : (c + 1) * LANES] for c in range(channels)], axis=0)
        y = y.reshape(channels, 2, lead, LANES)
        y_r = y[:, 0].reshape(channels * lead, LANES)
        y_i = y[:, 1].reshape(channels * lead, LANES)
        y = jnp.concatenate([y_r * tw_r - y_i * tw_i, y_r * tw_i + y_i * tw_r], axis=1)
        s = dot_right(y, fwd_ref)
        s_r, s_i = s[:, :LANES], s[:, LANES:]
        s = jnp.concatenate(
            [s_r * chirp_r + s_i * chirp_i, s_i * chirp_r - s_r * chirp_i], axis=1
        )
        t = dot_right(s, inv_ref)
        t_r, t_i = t[:, :LANES], t[:, LANES:]
        z_r = t_r * tw_r + t_i * tw_i
        z_i = t_i * tw_r - t_r * tw_i
        z = [
            jnp.concatenate(
                [z_r[c * lead : (c + 1) * lead], z_i[c * lead : (c + 1) * lead]], axis=0
            )
            for c in range(channels)
        ]
        pairs = channels // 2
        stacked = jnp.concatenate(
            [jnp.concatenate([z[2 * k], z[2 * k + 1]], axis=0) for k in range(pairs)], axis=1
        )
        w = dot_left(last_ref, stacked)
        for k in range(pairs):
            row = (p * pairs + k) * 8
            out_ref[:, row : row + 8, :] = w[:, k * LANES : (k + 1) * LANES].reshape(
                devices, 8, LANES
            )
        for c in range(channels):
            signal = p * channels + c
            g, place = signal // per_group, signal % per_group
            moved = z[c] if place == 0 else pltpu.roll(z[c], place * MIG, 1)
            packs[g] = jnp.where(lane // MIG == place, moved, packs[g])
    w = dot_left(halo_ref, jnp.concatenate(packs, axis=1))
    row = lax.broadcasted_iota(jnp.int32, (devices * HALO_ROWS, LANES), 0) % HALO_ROWS
    total = w[:, :LANES]
    for g in range(1, groups):
        total = jnp.where(row // 2 == g, w[:, g * LANES : (g + 1) * LANES], total)
    out_ref[:, pulses * channels * 4 :, :] = total.reshape(devices, HALO_ROWS, LANES)


def exchange_kernel(devices, inner, send_ref, recv_ref, local_sem, send_sems, recv_sems):
    mine = lax.axis_index("az") * inner + lax.axis_index("rg")
    barrier = pltpu.get_barrier_semaphore()

    def place(index):
        return (lax.div(index, inner), lax.rem(index, inner))

    for k in range(1, devices):
        pl.semaphore_signal(
            barrier,
            inc=1,
            device_id=place(lax.rem(mine + k, devices)),
            device_id_type=pl.DeviceIdType.MESH,
        )
    own = pltpu.make_async_copy(send_ref.at[mine], recv_ref.at[mine], local_sem)
    own.start()
    pl.semaphore_wait(barrier, devices - 1)
    copies = []
    for k in range(devices // 2, 0, -1):
        for step in sorted({k, devices - k}):
            target = lax.rem(mine + step, devices)
            copy = pltpu.make_async_remote_copy(
                src_ref=send_ref.at[target],
                dst_ref=recv_ref.at[mine],
                send_sem=send_sems.at[step],
                recv_sem=recv_sems.at[step],
                device_id=place(target),
                device_id_type=pl.DeviceIdType.MESH,
            )
            copy.start()
            copies.append(copy)
    own.wait()
    for copy in copies:
        copy.wait()


def azimuth_kernel(
    sizes,
    recv_ref,
    reconstruction_ref,
    delays_ref,
    rate_ref,
    band_ref,
    migration_ref,
    doppler_ref,
    halo_doppler_ref,
    final_hbm,
    out_ref,
    spectra,
    unfolded,
    focused,
    mix,
    final,
    final_sem,
):
    sources, local_pulses, channels, bins = sizes
    pulses = sources * local_pulses
    block = local_pulses * channels * 4 + HALO_ROWS
    length = channels * pulses
    load = pltpu.make_async_copy(final_hbm, final, final_sem)
    load.start()

    row = lax.broadcasted_iota(jnp.int32, (channels * channels, pulses), 0) % channels
    frequency = lax.broadcasted_iota(jnp.int32, (channels * channels, pulses), 1)
    delay = jnp.zeros_like(row)
    for c in range(channels):
        delay = jnp.where(row == c, delays_ref[c], delay)
    turns = lax.rem(frequency * delay, pulses).astype(jnp.float32) * (1.0 / pulses)
    align_r, align_i = cos_sin_turns(turns)
    rec_r, rec_i = reconstruction_ref[0], reconstruction_ref[1]
    mix[0] = rec_r * align_r - rec_i * align_i
    mix[1] = rec_r * align_i + rec_i * align_r

    def rows_of(start):
        return recv_ref[pl.ds(start, sources, stride=block), :]

    for c in range(channels):
        for half in range(bins // LANES):
            z = jnp.concatenate(
                [
                    rows_of(p * channels * 4 + c * 4 + part * 2 + half)
                    for part in range(2)
                    for p in range(local_pulses)
                ],
                axis=0,
            )
            spectra[c, half * LANES : (half + 1) * LANES, :] = dot_right(z.T, doppler_ref)
    groups = local_pulses * channels * MIG // LANES
    per_group = LANES // (MIG * channels)
    h = jnp.concatenate(
        [
            rows_of(local_pulses * channels * 4 + g * 2 + part)
            for g in range(groups)
            for part in range(2)
        ],
        axis=0,
    ).T
    step = channels * MIG
    halo = dot_right(h[:step], halo_doppler_ref.at[0])
    for k in range(1, per_group):
        halo = halo + dot_right(h[k * step : (k + 1) * step], halo_doppler_ref.at[k])
    for c in range(channels):
        spectra[c, bins:, :] = halo[c * MIG : (c + 1) * MIG]

    def mix_rows(index, carry):
        at = pl.ds(pl.multiple_of(index * 8, 8), 8)
        spec = [spectra[c, at, :] for c in range(channels)]
        for b in range(channels):
            total_r = total_i = None
            for c in range(channels):
                m = b * channels + c
                m_r = jnp.broadcast_to(mix[0, m : m + 1, :], (8, pulses))
                m_i = jnp.broadcast_to(mix[1, m : m + 1, :], (8, pulses))
                d_r, d_i = spec[c][:, :pulses], spec[c][:, pulses:]
                r = m_r * d_r - m_i * d_i
                i = m_r * d_i + m_i * d_r
                total_r = r if c == 0 else total_r + r
                total_i = i if c == 0 else total_i + i
            unfolded[at, b * pulses : (b + 1) * pulses] = total_r
            unfolded[at, length + b * pulses : length + (b + 1) * pulses] = total_i
        return carry

    lax.fori_loop(0, (bins + MIG) // 8, mix_rows, 0)

    def focus_band(b, carry):
        lane = pl.multiple_of(b * LANES, LANES)
        at_real = pl.ds(lane, LANES)
        at_imag = pl.ds(pl.multiple_of(length + lane, LANES), LANES)
        doppler = lax.broadcasted_iota(jnp.int32, (8, LANES), 1) + lane
        centred = doppler - jnp.where(doppler >= length // 2, length, 0)
        centred_square = centred * centred
        distance = jnp.abs(centred)
        relative = centred.astype(jnp.float32) * (2.0 / length)
        chirp_turns = relative * relative * (curvature / 2.0)
        for start in range(0, bins, 8):
            at = slice(start, start + 8)
            rate = jnp.broadcast_to(rate_ref[at, :], (8, LANES))
            band = jnp.broadcast_to(band_ref[at, :], (8, LANES))
            move = jnp.broadcast_to(migration_ref[at, :], (8, LANES))
            band_square = band * band
            reach = move * jnp.minimum(centred_square, band_square) + (band_square >> 1)
            real = unfolded[at, at_real]
            imag = unfolded[at, at_imag]
            bound = band_square
            for offset in range(1, MIG + 1):
                moved = reach >= bound
                window = slice(start + offset, start + offset + 8)
                real = jnp.where(moved, unfolded[window, at_real], real)
                imag = jnp.where(moved, unfolded[window, at_imag], imag)
                bound = bound + band_square
            cosine, sine = cos_sin_turns(rate * chirp_turns)
            inside = distance < band
            focused[at, at_real] = jnp.where(inside, real * cosine - imag * sine, 0.0)
            focused[at, at_imag] = jnp.where(inside, real * sine + imag * cosine, 0.0)
        return carry

    lax.fori_loop(0, length // LANES, focus_band, 0)
    load.wait()
    image = dot_right(focused[...], final)
    out_ref[0] = image[:, :length]
    out_ref[1] = image[:, length:]


def fits(pulses, channels, length, devices):
    local_pulses = pulses // devices
    signals = local_pulses * channels
    bins = length // devices
    lead = length // LANES
    return (
        pulses == LANES
        and length % (LANES * devices) == 0
        and bins == 2 * LANES
        and channels % 2 == 0
        and lead % 8 == 0
        and devices % 8 == 0
        and signals * MIG % LANES == 0
        and LANES % (MIG * channels) == 0
        and 2 * (signals * MIG // LANES) <= HALO_ROWS
        and channels * pulses <= 512
    )


def vmem():
    return pl.BlockSpec(memory_space=pltpu.VMEM)


def blocked_local(
    raw_echoes, chirp_spectrum, reconstruction, delays, azimuth_rate, band_halfwidth, migration
):
    local_pulses, channels, _, length = raw_echoes.shape
    inner = lax.axis_size("rg")
    devices = lax.axis_size("az") * inner
    bins = length // devices
    lead = length // LANES
    pulses = local_pulses * devices
    signals = local_pulses * channels
    doppler_bins = channels * pulses
    leads = np.arange(lead)
    lanes = np.arange(LANES)

    first = left_matrix(*roots(leads, leads, lead, -1.0))
    first = first.transpose(0, 1, 3, 2).reshape(2 * lead, 2 * lead)
    forward = right_matrix(*roots(lanes, lanes, LANES, -1.0)).reshape(2 * LANES, 2 * LANES)
    inverse = right_matrix(*roots(lanes, lanes, LANES, 1.0)).reshape(2 * LANES, 2 * LANES)
    last = left_matrix(*roots(leads, leads, lead, 1.0)) / length
    pair = np.zeros((devices, 2, 2, 2, 2, 2 * lead))
    by_device = last.reshape(2, devices, 2, 2 * lead).transpose(1, 0, 2, 3)
    for s in range(2):
        pair[:, s, :, :, s, :] = by_device
    pair = pair.reshape(devices * 8, 4 * lead)
    halo = np.zeros((devices, HALO_ROWS, 2 * lead))
    groups = signals * MIG // LANES
    for g in range(groups):
        halo[:-1, 2 * g : 2 * g + 2] = by_device[1:, :, 0]
    halo = halo.reshape(devices * HALO_ROWS, 2 * lead)
    twiddles = np.stack(roots(leads, lanes, length, -1.0)).astype(np.float32)

    sources = np.arange(devices)
    bins_f = np.arange(pulses)
    order = (np.arange(local_pulses)[:, None] + sources[None, :] * local_pulses).reshape(-1)
    scale = 1.0 / math.sqrt(pulses)
    to_doppler = right_matrix(*roots(order, bins_f, pulses, -1.0)) * scale
    to_doppler = to_doppler.reshape(2 * pulses, 2 * pulses)
    per_group = local_pulses // groups
    halo_doppler = []
    for k in range(per_group):
        by_group = []
        for g in range(groups):
            at = sources * local_pulses + g * per_group + k
            by_group.append(
                (right_matrix(*roots(at, bins_f, pulses, -1.0)) * scale).reshape(
                    2 * devices, 2 * pulses
                )
            )
        halo_doppler.append(split_constant(np.concatenate(by_group, axis=0)))
    halo_doppler = np.stack(halo_doppler)
    indices = np.arange(doppler_bins)
    final = right_matrix(*roots(indices, indices, doppler_bins, 1.0)) / math.sqrt(doppler_bins)
    final = final.reshape(2 * doppler_bins, 2 * doppler_bins)

    x = raw_echoes.reshape(signals, 2, lead, LANES).transpose(0, 2, 1, 3)
    x = x.reshape(signals, 2 * lead, LANES)
    chirp = chirp_spectrum.reshape(2, LANES, lead).transpose(0, 2, 1)
    block = signals * 4 + HALO_ROWS
    send = pl.pallas_call(
        functools.partial(range_kernel, (local_pulses, channels, lead, devices)),
        out_shape=jax.ShapeDtypeStruct((devices, block, LANES), jnp.float32),
        in_specs=[vmem()] * 8,
        out_specs=vmem(),
        compiler_params=pltpu.CompilerParams(vmem_limit_bytes=48 * 1024 * 1024),
        name="range_compress",
    )(
        x,
        chirp,
        split_constant(first),
        twiddles,
        split_constant(forward),
        split_constant(inverse),
        split_constant(pair),
        split_constant(halo),
    )
    received = pl.pallas_call(
        functools.partial(exchange_kernel, devices, inner),
        out_shape=jax.ShapeDtypeStruct((devices, block, LANES), jnp.float32),
        in_specs=[pl.BlockSpec(memory_space=pl.ANY)],
        out_specs=pl.BlockSpec(memory_space=pl.ANY),
        scratch_shapes=[
            pltpu.SemaphoreType.DMA,
            pltpu.SemaphoreType.DMA((devices,)),
            pltpu.SemaphoreType.DMA((devices,)),
        ],
        compiler_params=pltpu.CompilerParams(collective_id=0, has_side_effects=True),
        name="exchange",
    )(send)
    received = received.reshape(devices * block, LANES)
    return pl.pallas_call(
        functools.partial(azimuth_kernel, (devices, local_pulses, channels, bins)),
        out_shape=jax.ShapeDtypeStruct((2, bins, doppler_bins), jnp.float32),
        in_specs=[
            vmem(),
            vmem(),
            pl.BlockSpec(memory_space=pltpu.SMEM),
            vmem(),
            vmem(),
            vmem(),
            vmem(),
            vmem(),
            pl.BlockSpec(memory_space=pl.ANY),
        ],
        out_specs=vmem(),
        scratch_shapes=[
            pltpu.VMEM((channels, bins + MIG, 2 * pulses), jnp.float32),
            pltpu.VMEM((bins + MIG, 2 * doppler_bins), jnp.float32),
            pltpu.VMEM((bins, 2 * doppler_bins), jnp.float32),
            pltpu.VMEM((2, channels * channels, pulses), jnp.float32),
            pltpu.VMEM((2, 2 * doppler_bins, 2 * doppler_bins), jnp.bfloat16),
            pltpu.SemaphoreType.DMA,
        ],
        compiler_params=pltpu.CompilerParams(vmem_limit_bytes=48 * 1024 * 1024),
        name="azimuth_focus",
    )(
        received,
        reconstruction.reshape(2, channels * channels, pulses),
        delays,
        azimuth_rate.reshape(bins, 1),
        band_halfwidth.reshape(bins, 1),
        migration.reshape(bins, 1),
        split_constant(to_doppler),
        halo_doppler,
        split_constant(final),
    )


def local(raw_echoes, chirp_spectrum, reconstruction, *rest):
    local_pulses, channels, _, length = raw_echoes.shape
    devices = lax.axis_size("az") * lax.axis_size("rg")
    if fits(local_pulses * devices, channels, length, devices):
        return blocked_local(raw_echoes, chirp_spectrum, reconstruction, *rest)
    return plain_local(raw_echoes, chirp_spectrum, reconstruction, *rest)


def solution(mesh):
    in_specs = (
        P(("az", "rg"), None, None, None),
        P(),
        P(),
        P(),
        P(("az", "rg")),
        P(("az", "rg")),
        P(("az", "rg")),
    )
    out_specs = P(None, ("az", "rg"), None)
    return jax.shard_map(local, mesh=mesh, in_specs=in_specs, out_specs=out_specs, check_vma=False)
```

```python
import functools
import math

import jax
import jax.numpy as jnp
import ml_dtypes
import numpy as np
from jax import lax
from jax.experimental import pallas as pl
from jax.experimental.pallas import tpu as pltpu
from jax.sharding import PartitionSpec as P

MIG = 16
LANES = 128
HALO_ROWS = 8
KERNEL_VMEM = 62 * 1024 * 1024


highest = lax.Precision.HIGHEST
curvature = 32.0


def passed_along(value, axis, by):
    size = lax.axis_size(axis)
    pairs = [(i, i + by) for i in range(size) if 0 <= i + by < size]
    return lax.ppermute(value, axis, pairs)


def factor_pair(length):
    largest = 1
    for candidate in range(1, length + 1):
        if candidate * candidate > length:
            break
        if length % candidate == 0:
            largest = candidate
    return (largest, length // largest)


def dft_matrix(length, direction):
    indices = jnp.arange(length, dtype=jnp.int32)
    angles = (
        2.0 * math.pi / length * (indices[:, None] * indices[None, :] % length).astype(jnp.float32)
    )
    cosine = jnp.cos(angles)
    sines = direction * jnp.sin(angles)
    return jnp.stack(
        [jnp.stack([cosine, -sines], axis=1), jnp.stack([sines, cosine], axis=1)], axis=0
    )


def twiddle(lead_size, trail_size, length, direction):
    lead_index = jnp.arange(lead_size, dtype=jnp.int32)
    trail_index = jnp.arange(trail_size, dtype=jnp.int32)
    angles = (
        2.0
        * math.pi
        / length
        * (lead_index[:, None] * trail_index[None, :] % length).astype(jnp.float32)
    )
    return (jnp.cos(angles), direction * jnp.sin(angles))


def complex_mul(values, factor_real, factor_imag, part_axis):
    real_part = lax.index_in_dim(values, 0, part_axis, keepdims=True)
    imag_part = lax.index_in_dim(values, 1, part_axis, keepdims=True)
    return jnp.concatenate(
        [
            real_part * factor_real - imag_part * factor_imag,
            real_part * factor_imag + imag_part * factor_real,
        ],
        axis=part_axis,
    )


def range_focus(raw_echoes, chirp_spectrum):
    local_pulses, channels, _, length = raw_echoes.shape
    lead_size, trail_size = factor_pair(length)
    layout = raw_echoes.reshape(local_pulses, channels, 2, lead_size, trail_size)
    sectioned = jnp.einsum(
        "okci,pqcij->pqokj", dft_matrix(lead_size, -1.0), layout, precision=highest
    )
    twiddle_real, twiddle_imag = twiddle(lead_size, trail_size, length, -1.0)
    sectioned = complex_mul(sectioned, twiddle_real, twiddle_imag, 2)
    spectrum = jnp.einsum(
        "olcj,pqckj->pqolk", dft_matrix(trail_size, -1.0), sectioned, precision=highest
    )
    spectrum = spectrum.reshape(local_pulses, channels, 2, length)
    spectrum = complex_mul(spectrum, chirp_spectrum[0], -chirp_spectrum[1], 2)
    layout = spectrum.reshape(local_pulses, channels, 2, lead_size, trail_size)
    sectioned = jnp.einsum(
        "okci,pqcij->pqokj", dft_matrix(lead_size, 1.0), layout, precision=highest
    )
    twiddle_real, twiddle_imag = twiddle(lead_size, trail_size, length, 1.0)
    sectioned = complex_mul(sectioned, twiddle_real, twiddle_imag, 2)
    restored = jnp.einsum(
        "olcj,pqckj->qoplk", dft_matrix(trail_size, 1.0), sectioned, precision=highest
    )
    return restored.reshape(channels, 2, local_pulses, length) / length


def reconstruct(turned, mixing_real, mixing_imag):
    channels, _, local_pulses, blocks, bin_count = turned.shape
    pulse_total = blocks * local_pulses
    sectioned = jnp.einsum("okcm,qcimb->qobik", dft_matrix(blocks, -1.0), turned, precision=highest)
    twiddle_real, twiddle_imag = twiddle(local_pulses, blocks, pulse_total, -1.0)
    sectioned = complex_mul(sectioned, twiddle_real, twiddle_imag, 1)
    spectrum = jnp.einsum(
        "olci,qcbik->qoblk", dft_matrix(local_pulses, -1.0), sectioned, precision=highest
    )
    spectrum = spectrum.reshape(channels, 2, bin_count, pulse_total) / math.sqrt(pulse_total)
    spec_real = spectrum[:, 0]
    spec_imag = spectrum[:, 1]
    unfolded_real = jnp.einsum(
        "bcf,crf->rbf", mixing_real, spec_real, precision=highest
    ) - jnp.einsum("bcf,crf->rbf", mixing_imag, spec_imag, precision=highest)
    unfolded_imag = jnp.einsum(
        "bcf,crf->rbf", mixing_real, spec_imag, precision=highest
    ) + jnp.einsum("bcf,crf->rbf", mixing_imag, spec_real, precision=highest)
    unfolded = jnp.stack([unfolded_real, unfolded_imag], axis=0)
    return unfolded.reshape(2, bin_count, channels * pulse_total)


def azimuth_focus(unfolded, azimuth_rate, band_halfwidth, migration):
    bin_count = azimuth_rate.shape[0]
    length = unfolded.shape[2]
    doppler_index = jnp.arange(length, dtype=jnp.int32)
    centred = doppler_index - length * (doppler_index >= length // 2).astype(jnp.int32)
    band_square = band_halfwidth * band_halfwidth
    squared = jnp.minimum((centred * centred)[None, :], band_square[:, None])
    migration_shift = (migration[:, None] * squared + (band_square // 2)[:, None]) // band_square[
        :, None
    ]
    migrated = jnp.zeros((2, bin_count, length), jnp.float32)
    for offset in range(MIG + 1):
        window = unfolded[:, offset : offset + bin_count, :]
        migrated = jnp.where((migration_shift == offset)[None], window, migrated)
    relative = centred.astype(jnp.float32) / (length // 2)
    matched_phase = math.pi * curvature * azimuth_rate[:, None] * (relative * relative)[None, :]
    focused = complex_mul(migrated, jnp.cos(matched_phase), jnp.sin(matched_phase), 0)
    inside = jnp.abs(centred)[None, :] < band_halfwidth[:, None]
    focused = jnp.where(inside[None], focused, 0.0)
    lead_size, trail_size = factor_pair(length)
    layout = focused.reshape(2, bin_count, lead_size, trail_size)
    sectioned = jnp.einsum("okci,cbij->obkj", dft_matrix(lead_size, 1.0), layout, precision=highest)
    twiddle_real, twiddle_imag = twiddle(lead_size, trail_size, length, 1.0)
    sectioned = complex_mul(sectioned, twiddle_real, twiddle_imag, 0)
    focused_image = jnp.einsum(
        "olcj,cbkj->oblk", dft_matrix(trail_size, 1.0), sectioned, precision=highest
    )
    return focused_image.reshape(2, bin_count, length) / math.sqrt(length)


def plain_local(
    raw_echoes, chirp_spectrum, reconstruction, delays, azimuth_rate, band_halfwidth, migration
):
    compressed = range_focus(raw_echoes, chirp_spectrum)
    channels, _, local_pulses, length = compressed.shape
    azimuth_count = lax.axis_size("az")
    range_count = lax.axis_size("rg")
    bin_count = length // (azimuth_count * range_count)
    layout = compressed.reshape(channels, 2, local_pulses, azimuth_count, range_count, bin_count)
    layout = lax.all_to_all(layout, "rg", split_axis=4, concat_axis=4, tiled=True)
    layout = lax.all_to_all(layout, "az", split_axis=3, concat_axis=3, tiled=True)
    turned = layout.reshape(channels, 2, local_pulses, azimuth_count * range_count, bin_count)
    pulse_total = azimuth_count * range_count * local_pulses
    frequency = jnp.arange(pulse_total, dtype=jnp.int32)
    angles = (
        2.0
        * math.pi
        / pulse_total
        * (frequency[None, :] * delays[:, None] % pulse_total).astype(jnp.float32)
    )
    align_real = jnp.cos(angles)[None]
    align_imag = jnp.sin(angles)[None]
    mixing_real = reconstruction[0] * align_real - reconstruction[1] * align_imag
    mixing_imag = reconstruction[0] * align_imag + reconstruction[1] * align_real
    unfolded = reconstruct(turned, mixing_real, mixing_imag)
    margin_bins = passed_along(unfolded[:, :MIG, :], ("az", "rg"), -1)
    unfolded = jnp.concatenate([unfolded, margin_bins], axis=1)
    return azimuth_focus(unfolded, azimuth_rate, band_halfwidth, migration)


def split_constant(values):
    high = values.astype(ml_dtypes.bfloat16)
    low = (values - high.astype(np.float64)).astype(ml_dtypes.bfloat16)
    return np.stack([high, low])


def roots(rows, columns, length, direction):
    turns = (rows[:, None] * columns[None, :]) % length
    angles = 2.0 * np.pi / length * turns
    return np.cos(angles), direction * np.sin(angles)


def left_matrix(cosine, sine):
    return np.stack([np.stack([cosine, -sine], 1), np.stack([sine, cosine], 1)], 0)


def right_matrix(cosine, sine):
    return np.stack([np.stack([cosine, sine], 1), np.stack([-sine, cosine], 1)], 0)


def split(values):
    high = values.astype(jnp.bfloat16)
    low = (values - high.astype(jnp.float32)).astype(jnp.bfloat16)
    return high, low


def dot(a, b):
    return jnp.dot(a, b, preferred_element_type=jnp.float32)


def dot_right(values, matrix):
    high, low = split(values)
    return dot(high, matrix[0]) + (dot(low, matrix[0]) + dot(high, matrix[1]))


def dot_left(matrix, values):
    high, low = split(values)
    return dot(matrix[0], high) + (dot(matrix[1], high) + dot(matrix[0], low))


def cos_sin_turns(turns):
    quarter = jnp.floor(turns * 4.0 + 0.5)
    theta = (turns - quarter * 0.25) * (2.0 * math.pi)
    square = theta * theta
    cosine = 1.0 + square * (
        -0.5 + square * (1.0 / 24 + square * (-1.0 / 720 + square * (1.0 / 40320)))
    )
    sine = theta * (
        1.0
        + square
        * (-1.0 / 6 + square * (1.0 / 120 + square * (-1.0 / 5040 + square * (1.0 / 362880))))
    )
    index = quarter.astype(jnp.int32)
    odd = (index & 1) == 1
    cos_negative = ((index + 1) & 2) == 2
    sin_negative = (index & 2) == 2
    cos_size = jnp.where(odd, sine, cosine)
    sin_size = jnp.where(odd, cosine, sine)
    return (
        jnp.where(cos_negative, -cos_size, cos_size),
        jnp.where(sin_negative, -sin_size, sin_size),
    )


def spread_rows(values):
    return jnp.concatenate(
        [
            jnp.broadcast_to(values[h : h + 1, :], (LANES, LANES)).T
            for h in range(values.shape[0])
        ],
        axis=0,
    )


def compress_kernel(
    sizes,
    x_hbm,
    chirp_hbm,
    rate_hbm,
    band_hbm,
    migration_hbm,
    first_hbm,
    twiddle_hbm,
    fwd_hbm,
    inv_hbm,
    last_hbm,
    halo_hbm,
    recv_ref,
    cos_hbm,
    sin_hbm,
    reach_hbm,
    square_hbm,
    x_ref,
    chirp_ref,
    rate_ref,
    band_ref,
    migration_ref,
    first_ref,
    twiddle_ref,
    fwd_ref,
    inv_ref,
    last_ref,
    halo_ref,
    send_ref,
    rows_ref,
    cos_ref,
    sin_ref,
    reach_ref,
    square_ref,
    load_sems,
    store_sems,
    local_sem,
    send_sems,
    recv_sems,
):
    pulses, channels, lead, devices, inner, length = sizes
    mine = lax.axis_index("az") * inner + lax.axis_index("rg")
    barrier = pltpu.get_barrier_semaphore()

    def place(index):
        return (lax.div(index, inner), lax.rem(index, inner))

    def greet(k, carry):
        pl.semaphore_signal(
            barrier,
            inc=1,
            device_id=place(lax.rem(mine + k, devices)),
            device_id_type=pl.DeviceIdType.MESH,
        )
        return carry

    loads = []

    def start_load(source, target):
        copy = pltpu.make_async_copy(source, target, load_sems.at[len(loads)])
        copy.start()
        loads.append(copy)
        return copy

    def pulse_load(p):
        at = pl.ds(p * channels, channels)
        return start_load(x_hbm.at[at], x_ref.at[at])

    load_x = [pulse_load(0)]
    load_first = start_load(first_hbm, first_ref)
    load_twiddle = start_load(twiddle_hbm, twiddle_ref)
    load_fwd = start_load(fwd_hbm, fwd_ref)
    load_chirp = start_load(chirp_hbm, chirp_ref)
    load_inv = start_load(inv_hbm, inv_ref)
    load_last = start_load(last_hbm, last_ref)
    load_x += [pulse_load(p) for p in range(1, pulses)]
    load_halo = start_load(halo_hbm, halo_ref)
    load_rate = start_load(rate_hbm, rate_ref)
    load_band = start_load(band_hbm, band_ref)
    load_migration = start_load(migration_hbm, migration_ref)
    lax.fori_loop(1, devices, greet, 0)

    rows = pulses * channels * 4 + HALO_ROWS
    cut = channels * 4

    def remote(chunk, i):
        far = lax.div(i + 1, 2)
        step = devices // 2 + far - 2 * far * lax.rem(i, 2)
        target = lax.rem(mine + step, devices)
        at = pl.ds(0, cut) if chunk == 0 else pl.ds(cut, rows - cut)
        return pltpu.make_async_remote_copy(
            src_ref=send_ref.at[target, at],
            dst_ref=recv_ref.at[mine, at],
            send_sem=send_sems.at[chunk, step],
            recv_sem=recv_sems.at[chunk, step],
            device_id=place(target),
            device_id_type=pl.DeviceIdType.MESH,
        )

    def send(chunk):
        def body(i, carry):
            remote(chunk, i).start()
            return carry

        lax.fori_loop(0, devices - 1, body, 0)

    lane = lax.broadcasted_iota(jnp.int32, (2 * lead, LANES), 1)
    groups = pulses * channels * MIG // LANES
    per_group = LANES // MIG
    pairs = channels // 2
    packs = [jnp.zeros((2 * lead, LANES), jnp.float32) for _ in range(groups)]
    for p in range(pulses):
        load_x[p].wait()
        if p == 0:
            load_first.wait()
        x = jnp.concatenate([x_ref[p * channels + c] for c in range(channels)], axis=1)
        y = dot_left(first_ref, x)
        if p == 0:
            load_twiddle.wait()
            load_fwd.wait()
            load_chirp.wait()
            load_inv.wait()
            tw_r = jnp.concatenate([twiddle_ref[0]] * channels, axis=0)
            tw_i = jnp.concatenate([twiddle_ref[1]] * channels, axis=0)
            chirp = jnp.concatenate(
                [chirp_ref[pl.ds(part, lead, stride=2), :] for part in range(2)], axis=0
            ).T
            top, bottom = chirp[:lead], chirp[lead:]
            left = lane[:lead] < lead
            chirp_r = jnp.where(left, top, pltpu.roll(bottom, lead, 1))
            chirp_i = jnp.where(left, pltpu.roll(top, lead, 1), bottom)
            chirp_r = jnp.concatenate([chirp_r] * channels, axis=0)
            chirp_i = jnp.concatenate([chirp_i] * channels, axis=0)
        y = jnp.concatenate([y[:, c * LANES : (c + 1) * LANES] for c in range(channels)], axis=0)
        y = y.reshape(channels, 2, lead, LANES)
        y_r = y[:, 0].reshape(channels * lead, LANES)
        y_i = y[:, 1].reshape(channels * lead, LANES)
        y = jnp.concatenate([y_r * tw_r - y_i * tw_i, y_r * tw_i + y_i * tw_r], axis=1)
        s = dot_right(y, fwd_ref)
        s_r, s_i = s[:, :LANES], s[:, LANES:]
        s = jnp.concatenate(
            [s_r * chirp_r + s_i * chirp_i, s_i * chirp_r - s_r * chirp_i], axis=1
        )
        t = dot_right(s, inv_ref)
        t_r, t_i = t[:, :LANES], t[:, LANES:]
        z_r = t_r * tw_r + t_i * tw_i
        z_i = t_i * tw_r - t_r * tw_i
        z = [
            jnp.concatenate(
                [z_r[c * lead : (c + 1) * lead], z_i[c * lead : (c + 1) * lead]], axis=0
            )
            for c in range(channels)
        ]
        stacked = jnp.concatenate(
            [jnp.concatenate([z[2 * k], z[2 * k + 1]], axis=0) for k in range(pairs)], axis=1
        )
        if p == 0:
            load_last.wait()
        w = dot_left(last_ref, stacked)
        for k in range(pairs):
            row = (p * pairs + k) * 8
            send_ref[:, row : row + 8, :] = w[:, k * LANES : (k + 1) * LANES].reshape(
                devices, 8, LANES
            )
        for c in range(channels):
            signal = p * channels + c
            g, where = signal // per_group, signal % per_group
            moved = z[c] if where == 0 else pltpu.roll(z[c], where * MIG, 1)
            packs[g] = jnp.where(lane // MIG == where, moved, packs[g])
        if p == 0:
            pl.semaphore_wait(barrier, devices - 1)
            send(0)
    load_halo.wait()
    w = dot_left(halo_ref, jnp.concatenate(packs, axis=1))
    row = lax.broadcasted_iota(jnp.int32, (devices * HALO_ROWS, LANES), 0) % HALO_ROWS
    total = w[:, :LANES]
    for g in range(1, groups):
        total = jnp.where(row // 2 == g, w[:, g * LANES : (g + 1) * LANES], total)
    send_ref[:, pulses * channels * 4 :, :] = total.reshape(devices, HALO_ROWS, LANES)
    send(1)
    own = pltpu.make_async_copy(send_ref.at[mine], recv_ref.at[mine], local_sem)
    own.start()

    load_rate.wait()
    load_band.wait()
    load_migration.wait()
    rows_ref[0] = spread_rows(rate_ref[...])
    rows_ref[1] = spread_rows(band_ref[...].astype(jnp.float32))
    rows_ref[2] = spread_rows(migration_ref[...].astype(jnp.float32))
    bins = rows_ref.shape[1]

    def tables(index, carry):
        at = pl.ds(pl.multiple_of(index * 8, 8), 8)
        rate = rows_ref[0, at, :]
        band = rows_ref[1, at, :].astype(jnp.int32)
        move = rows_ref[2, at, :].astype(jnp.int32)
        band_square = band * band
        square_ref[at, :] = band_square
        for start in range(0, length, LANES):
            doppler = lax.broadcasted_iota(jnp.int32, (8, LANES), 1) + start
            centred = jnp.where(doppler >= length // 2, doppler - length, doppler)
            relative = centred.astype(jnp.float32) * (2.0 / length)
            cosine, sine = cos_sin_turns(rate * (relative * relative * (curvature / 2.0)))
            inside = jnp.abs(centred) < band
            columns = slice(start, start + LANES)
            cos_ref[at, columns] = jnp.where(inside, cosine, 0.0)
            sin_ref[at, columns] = jnp.where(inside, sine, 0.0)
            reach_ref[at, columns] = move * jnp.minimum(centred * centred, band_square) + (
                band_square >> 1
            )
        return carry

    lax.fori_loop(0, bins // 8, tables, 0)
    stores = []
    for source, target in (
        (cos_ref, cos_hbm),
        (sin_ref, sin_hbm),
        (reach_ref, reach_hbm),
        (square_ref, square_hbm),
    ):
        copy = pltpu.make_async_copy(source, target, store_sems.at[len(stores)])
        copy.start()
        stores.append(copy)
    for copy in stores:
        copy.wait()
    own.wait()

    def finish(i, carry):
        for chunk in range(2):
            copy = remote(chunk, i)
            copy.wait_send()
            copy.wait_recv()
        return carry

    lax.fori_loop(0, devices - 1, finish, 0)


def azimuth_kernel(
    sizes,
    recv_hbm,
    reconstruction_ref,
    delays_ref,
    doppler_ref,
    halo_doppler_ref,
    final_hbm,
    cos_hbm,
    sin_hbm,
    reach_hbm,
    square_hbm,
    out_ref,
    recv_ref,
    spectra,
    unfolded,
    focused,
    mix,
    final,
    cos_ref,
    sin_ref,
    reach_ref,
    square_ref,
    load_sems,
    recv_sems,
):
    sources, local_pulses, channels, bins = sizes
    pulses = sources * local_pulses
    block = local_pulses * channels * 4 + HALO_ROWS
    length = channels * pulses
    arrivals = []

    def arrive(row):
        at = pl.ds(row, 8)
        copy = pltpu.make_async_copy(
            recv_hbm.at[:, at], recv_ref.at[:, at], recv_sems.at[len(arrivals)]
        )
        copy.start()
        arrivals.append(copy)

    for pair in range(channels // 2):
        for p in range(local_pulses):
            arrive((p * (channels // 2) + pair) * 8)
    arrive(local_pulses * channels * 4)
    loads = []
    for source, target in (
        (reach_hbm, reach_ref),
        (square_hbm, square_ref),
        (cos_hbm, cos_ref),
        (sin_hbm, sin_ref),
        (final_hbm, final),
    ):
        copy = pltpu.make_async_copy(source, target, load_sems.at[len(loads)])
        copy.start()
        loads.append(copy)

    row = lax.broadcasted_iota(jnp.int32, (channels * channels, pulses), 0) % channels
    frequency = lax.broadcasted_iota(jnp.int32, (channels * channels, pulses), 1)
    delay = jnp.zeros_like(row)
    for c in range(channels):
        delay = jnp.where(row == c, delays_ref[c], delay)
    turns = lax.rem(frequency * delay, pulses).astype(jnp.float32) * (1.0 / pulses)
    align_r, align_i = cos_sin_turns(turns)
    rec_r, rec_i = reconstruction_ref[0], reconstruction_ref[1]
    mix[0] = rec_r * align_r - rec_i * align_i
    mix[1] = rec_r * align_i + rec_i * align_r

    def rows_of(start):
        return flat[pl.ds(start, sources, stride=block), :]

    flat = recv_ref.reshape(sources * block, LANES)
    for c in range(channels):
        if c % 2 == 0:
            for p in range(local_pulses):
                arrivals[c // 2 * local_pulses + p].wait()
        for half in range(bins // LANES):
            z = jnp.concatenate(
                [
                    rows_of(p * channels * 4 + c * 4 + part * 2 + half)
                    for part in range(2)
                    for p in range(local_pulses)
                ],
                axis=0,
            )
            spectra[c, half * LANES : (half + 1) * LANES, :] = dot_right(z.T, doppler_ref)
    groups = local_pulses * channels * MIG // LANES
    per_group = LANES // (MIG * channels)
    arrivals[-1].wait()
    h = jnp.concatenate(
        [
            rows_of(local_pulses * channels * 4 + g * 2 + part)
            for g in range(groups)
            for part in range(2)
        ],
        axis=0,
    ).T
    step = channels * MIG
    halo = dot_right(h[:step], halo_doppler_ref.at[0])
    for k in range(1, per_group):
        halo = halo + dot_right(h[k * step : (k + 1) * step], halo_doppler_ref.at[k])
    for c in range(channels):
        spectra[c, bins:, :] = halo[c * MIG : (c + 1) * MIG]

    def mix_rows(index, carry):
        at = pl.ds(pl.multiple_of(index * 8, 8), 8)
        spec = [spectra[c, at, :] for c in range(channels)]
        for b in range(channels):
            total_r = total_i = None
            for c in range(channels):
                m = b * channels + c
                m_r = jnp.broadcast_to(mix[0, m : m + 1, :], (8, pulses))
                m_i = jnp.broadcast_to(mix[1, m : m + 1, :], (8, pulses))
                d_r, d_i = spec[c][:, :pulses], spec[c][:, pulses:]
                r = m_r * d_r - m_i * d_i
                i = m_r * d_i + m_i * d_r
                total_r = r if c == 0 else total_r + r
                total_i = i if c == 0 else total_i + i
            unfolded[at, b * pulses : (b + 1) * pulses] = total_r
            unfolded[at, length + b * pulses : length + (b + 1) * pulses] = total_i
        return carry

    lax.fori_loop(0, (bins + MIG) // 8, mix_rows, 0)

    for copy in loads[:-1]:
        copy.wait()

    def focus_band(b, carry):
        lane = pl.multiple_of(b * LANES, LANES)
        at_real = pl.ds(lane, LANES)
        at_imag = pl.ds(pl.multiple_of(length + lane, LANES), LANES)
        for start in range(0, bins, 8):
            at = slice(start, start + 8)
            band_square = square_ref[at, :]
            reach = reach_ref[at, at_real]
            real = unfolded[at, at_real]
            imag = unfolded[at, at_imag]
            bound = band_square
            for offset in range(1, MIG + 1):
                moved = reach >= bound
                window = slice(start + offset, start + offset + 8)
                real = jnp.where(moved, unfolded[window, at_real], real)
                imag = jnp.where(moved, unfolded[window, at_imag], imag)
                bound = bound + band_square
            cosine = cos_ref[at, at_real]
            sine = sin_ref[at, at_real]
            focused[at, at_real] = real * cosine - imag * sine
            focused[at, at_imag] = real * sine + imag * cosine
        return carry

    lax.fori_loop(0, length // LANES, focus_band, 0)
    loads[-1].wait()
    image = dot_right(focused[...], final)
    out_ref[0] = image[:, :length]
    out_ref[1] = image[:, length:]


def fits(pulses, channels, length, devices):
    local_pulses = pulses // devices
    signals = local_pulses * channels
    bins = length // devices
    lead = length // LANES
    return (
        pulses == LANES
        and length % (LANES * devices) == 0
        and bins == 2 * LANES
        and channels % 2 == 0
        and 2 * lead == LANES
        and devices % 8 == 0
        and signals * MIG % LANES == 0
        and LANES % (MIG * channels) == 0
        and 2 * (signals * MIG // LANES) <= HALO_ROWS
        and channels * pulses <= 512
    )


def hbm():
    return pl.BlockSpec(memory_space=pltpu.HBM)


def vmem():
    return pl.BlockSpec(memory_space=pltpu.VMEM)


def blocked_local(
    raw_echoes, chirp_spectrum, reconstruction, delays, azimuth_rate, band_halfwidth, migration
):
    local_pulses, channels, _, length = raw_echoes.shape
    inner = lax.axis_size("rg")
    devices = lax.axis_size("az") * inner
    bins = length // devices
    lead = length // LANES
    pulses = local_pulses * devices
    signals = local_pulses * channels
    doppler_bins = channels * pulses
    leads = np.arange(lead)
    lanes = np.arange(LANES)

    first = left_matrix(*roots(leads, leads, lead, -1.0))
    first = first.transpose(0, 1, 3, 2).reshape(2 * lead, 2 * lead)
    turned = np.concatenate([lanes[0::2], lanes[1::2]])
    forward = right_matrix(*roots(lanes, turned, LANES, -1.0)).reshape(2 * LANES, 2 * LANES)
    inverse = right_matrix(*roots(turned, lanes, LANES, 1.0)).reshape(2 * LANES, 2 * LANES)
    last = left_matrix(*roots(leads, leads, lead, 1.0)) / length
    pair = np.zeros((devices, 2, 2, 2, 2, 2 * lead))
    by_device = last.reshape(2, devices, 2, 2 * lead).transpose(1, 0, 2, 3)
    for s in range(2):
        pair[:, s, :, :, s, :] = by_device
    pair = pair.reshape(devices * 8, 4 * lead)
    halo = np.zeros((devices, HALO_ROWS, 2 * lead))
    groups = signals * MIG // LANES
    for g in range(groups):
        halo[:-1, 2 * g : 2 * g + 2] = by_device[1:, :, 0]
    halo = halo.reshape(devices * HALO_ROWS, 2 * lead)
    twiddles = np.stack(roots(leads, lanes, length, -1.0)).astype(np.float32)

    sources = np.arange(devices)
    bins_f = np.arange(pulses)
    order = (np.arange(local_pulses)[:, None] + sources[None, :] * local_pulses).reshape(-1)
    scale = 1.0 / math.sqrt(pulses)
    to_doppler = right_matrix(*roots(order, bins_f, pulses, -1.0)) * scale
    to_doppler = to_doppler.reshape(2 * pulses, 2 * pulses)
    per_group = local_pulses // groups
    halo_doppler = []
    for k in range(per_group):
        by_group = []
        for g in range(groups):
            at = sources * local_pulses + g * per_group + k
            by_group.append(
                (right_matrix(*roots(at, bins_f, pulses, -1.0)) * scale).reshape(
                    2 * devices, 2 * pulses
                )
            )
        halo_doppler.append(split_constant(np.concatenate(by_group, axis=0)))
    halo_doppler = np.stack(halo_doppler)
    indices = np.arange(doppler_bins)
    final = right_matrix(*roots(indices, indices, doppler_bins, 1.0)) / math.sqrt(doppler_bins)
    final = final.reshape(2 * doppler_bins, 2 * doppler_bins)

    x = raw_echoes.reshape(signals, 2, lead, LANES).transpose(0, 2, 1, 3)
    x = x.reshape(signals, 2 * lead, LANES)
    chirp = chirp_spectrum.reshape(2, lead, LANES).transpose(1, 0, 2).reshape(2 * lead, LANES)
    block = signals * 4 + HALO_ROWS
    tables = (bins, doppler_bins)
    by_lane = (bins // LANES, LANES)
    operands = (
        x,
        chirp,
        azimuth_rate.reshape(by_lane),
        band_halfwidth.reshape(by_lane),
        migration.reshape(by_lane),
        split_constant(first),
        twiddles,
        split_constant(forward),
        split_constant(inverse),
        split_constant(pair),
        split_constant(halo),
    )
    received, cosine, sine, reach, square = pl.pallas_call(
        functools.partial(
            compress_kernel, (local_pulses, channels, lead, devices, inner, doppler_bins)
        ),
        out_shape=(
            jax.ShapeDtypeStruct((devices, block, LANES), jnp.float32),
            jax.ShapeDtypeStruct(tables, jnp.float32),
            jax.ShapeDtypeStruct(tables, jnp.float32),
            jax.ShapeDtypeStruct(tables, jnp.int32),
            jax.ShapeDtypeStruct((bins, LANES), jnp.int32),
        ),
        in_specs=[hbm()] * len(operands),
        out_specs=(hbm(),) * 5,
        scratch_shapes=[pltpu.VMEM(value.shape, value.dtype) for value in operands]
        + [
            pltpu.VMEM((devices, block, LANES), jnp.float32),
            pltpu.VMEM((3, bins, LANES), jnp.float32),
            pltpu.VMEM(tables, jnp.float32),
            pltpu.VMEM(tables, jnp.float32),
            pltpu.VMEM(tables, jnp.int32),
            pltpu.VMEM((bins, LANES), jnp.int32),
            pltpu.SemaphoreType.DMA((len(operands) + local_pulses - 1,)),
            pltpu.SemaphoreType.DMA((4,)),
            pltpu.SemaphoreType.DMA,
            pltpu.SemaphoreType.DMA((2, devices)),
            pltpu.SemaphoreType.DMA((2, devices)),
        ],
        compiler_params=pltpu.CompilerParams(
            collective_id=0, has_side_effects=True, vmem_limit_bytes=KERNEL_VMEM
        ),
        name="compress_exchange",
    )(*operands)
    return pl.pallas_call(
        functools.partial(azimuth_kernel, (devices, local_pulses, channels, bins)),
        out_shape=jax.ShapeDtypeStruct((2, bins, doppler_bins), jnp.float32),
        in_specs=[
            hbm(),
            vmem(),
            pl.BlockSpec(memory_space=pltpu.SMEM),
            vmem(),
            vmem(),
            hbm(),
            hbm(),
            hbm(),
            hbm(),
            hbm(),
        ],
        out_specs=vmem(),
        scratch_shapes=[
            pltpu.VMEM((devices, block, LANES), jnp.float32),
            pltpu.VMEM((channels, bins + MIG, 2 * pulses), jnp.float32),
            pltpu.VMEM((bins + MIG, 2 * doppler_bins), jnp.float32),
            pltpu.VMEM((bins, 2 * doppler_bins), jnp.float32),
            pltpu.VMEM((2, channels * channels, pulses), jnp.float32),
            pltpu.VMEM((2, 2 * doppler_bins, 2 * doppler_bins), jnp.bfloat16),
            pltpu.VMEM(tables, jnp.float32),
            pltpu.VMEM(tables, jnp.float32),
            pltpu.VMEM(tables, jnp.int32),
            pltpu.VMEM((bins, LANES), jnp.int32),
            pltpu.SemaphoreType.DMA((5,)),
            pltpu.SemaphoreType.DMA((channels // 2 * local_pulses + 1,)),
        ],
        compiler_params=pltpu.CompilerParams(vmem_limit_bytes=KERNEL_VMEM),
        name="azimuth_focus",
    )(
        received,
        reconstruction.reshape(2, channels * channels, pulses),
        delays,
        split_constant(to_doppler),
        halo_doppler,
        split_constant(final),
        cosine,
        sine,
        reach,
        square,
    )


def local(raw_echoes, chirp_spectrum, reconstruction, *rest):
    local_pulses, channels, _, length = raw_echoes.shape
    devices = lax.axis_size("az") * lax.axis_size("rg")
    if fits(local_pulses * devices, channels, length, devices):
        return blocked_local(raw_echoes, chirp_spectrum, reconstruction, *rest)
    return plain_local(raw_echoes, chirp_spectrum, reconstruction, *rest)


def solution(mesh):
    in_specs = (
        P(("az", "rg"), None, None, None),
        P(),
        P(),
        P(),
        P(("az", "rg")),
        P(("az", "rg")),
        P(("az", "rg")),
    )
    out_specs = P(None, ("az", "rg"), None)
    return jax.shard_map(local, mesh=mesh, in_specs=in_specs, out_specs=out_specs, check_vma=False)
```

```python
import functools
import math

import jax
import jax.numpy as jnp
import ml_dtypes
import numpy as np
from jax import lax
from jax.experimental import pallas as pl
from jax.experimental.pallas import tpu as pltpu
from jax.sharding import PartitionSpec as P

MIG = 16
LANES = 128
HALO_ROWS = 8
KERNEL_VMEM = 62 * 1024 * 1024


highest = lax.Precision.HIGHEST
curvature = 32.0


def passed_along(value, axis, by):
    size = lax.axis_size(axis)
    pairs = [(i, i + by) for i in range(size) if 0 <= i + by < size]
    return lax.ppermute(value, axis, pairs)


def factor_pair(length):
    largest = 1
    for candidate in range(1, length + 1):
        if candidate * candidate > length:
            break
        if length % candidate == 0:
            largest = candidate
    return (largest, length // largest)


def dft_matrix(length, direction):
    indices = jnp.arange(length, dtype=jnp.int32)
    angles = (
        2.0 * math.pi / length * (indices[:, None] * indices[None, :] % length).astype(jnp.float32)
    )
    cosine = jnp.cos(angles)
    sines = direction * jnp.sin(angles)
    return jnp.stack(
        [jnp.stack([cosine, -sines], axis=1), jnp.stack([sines, cosine], axis=1)], axis=0
    )


def twiddle(lead_size, trail_size, length, direction):
    lead_index = jnp.arange(lead_size, dtype=jnp.int32)
    trail_index = jnp.arange(trail_size, dtype=jnp.int32)
    angles = (
        2.0
        * math.pi
        / length
        * (lead_index[:, None] * trail_index[None, :] % length).astype(jnp.float32)
    )
    return (jnp.cos(angles), direction * jnp.sin(angles))


def complex_mul(values, factor_real, factor_imag, part_axis):
    real_part = lax.index_in_dim(values, 0, part_axis, keepdims=True)
    imag_part = lax.index_in_dim(values, 1, part_axis, keepdims=True)
    return jnp.concatenate(
        [
            real_part * factor_real - imag_part * factor_imag,
            real_part * factor_imag + imag_part * factor_real,
        ],
        axis=part_axis,
    )


def range_focus(raw_echoes, chirp_spectrum):
    local_pulses, channels, _, length = raw_echoes.shape
    lead_size, trail_size = factor_pair(length)
    layout = raw_echoes.reshape(local_pulses, channels, 2, lead_size, trail_size)
    sectioned = jnp.einsum(
        "okci,pqcij->pqokj", dft_matrix(lead_size, -1.0), layout, precision=highest
    )
    twiddle_real, twiddle_imag = twiddle(lead_size, trail_size, length, -1.0)
    sectioned = complex_mul(sectioned, twiddle_real, twiddle_imag, 2)
    spectrum = jnp.einsum(
        "olcj,pqckj->pqolk", dft_matrix(trail_size, -1.0), sectioned, precision=highest
    )
    spectrum = spectrum.reshape(local_pulses, channels, 2, length)
    spectrum = complex_mul(spectrum, chirp_spectrum[0], -chirp_spectrum[1], 2)
    layout = spectrum.reshape(local_pulses, channels, 2, lead_size, trail_size)
    sectioned = jnp.einsum(
        "okci,pqcij->pqokj", dft_matrix(lead_size, 1.0), layout, precision=highest
    )
    twiddle_real, twiddle_imag = twiddle(lead_size, trail_size, length, 1.0)
    sectioned = complex_mul(sectioned, twiddle_real, twiddle_imag, 2)
    restored = jnp.einsum(
        "olcj,pqckj->qoplk", dft_matrix(trail_size, 1.0), sectioned, precision=highest
    )
    return restored.reshape(channels, 2, local_pulses, length) / length


def reconstruct(turned, mixing_real, mixing_imag):
    channels, _, local_pulses, blocks, bin_count = turned.shape
    pulse_total = blocks * local_pulses
    sectioned = jnp.einsum("okcm,qcimb->qobik", dft_matrix(blocks, -1.0), turned, precision=highest)
    twiddle_real, twiddle_imag = twiddle(local_pulses, blocks, pulse_total, -1.0)
    sectioned = complex_mul(sectioned, twiddle_real, twiddle_imag, 1)
    spectrum = jnp.einsum(
        "olci,qcbik->qoblk", dft_matrix(local_pulses, -1.0), sectioned, precision=highest
    )
    spectrum = spectrum.reshape(channels, 2, bin_count, pulse_total) / math.sqrt(pulse_total)
    spec_real = spectrum[:, 0]
    spec_imag = spectrum[:, 1]
    unfolded_real = jnp.einsum(
        "bcf,crf->rbf", mixing_real, spec_real, precision=highest
    ) - jnp.einsum("bcf,crf->rbf", mixing_imag, spec_imag, precision=highest)
    unfolded_imag = jnp.einsum(
        "bcf,crf->rbf", mixing_real, spec_imag, precision=highest
    ) + jnp.einsum("bcf,crf->rbf", mixing_imag, spec_real, precision=highest)
    unfolded = jnp.stack([unfolded_real, unfolded_imag], axis=0)
    return unfolded.reshape(2, bin_count, channels * pulse_total)


def azimuth_focus(unfolded, azimuth_rate, band_halfwidth, migration):
    bin_count = azimuth_rate.shape[0]
    length = unfolded.shape[2]
    doppler_index = jnp.arange(length, dtype=jnp.int32)
    centred = doppler_index - length * (doppler_index >= length // 2).astype(jnp.int32)
    band_square = band_halfwidth * band_halfwidth
    squared = jnp.minimum((centred * centred)[None, :], band_square[:, None])
    migration_shift = (migration[:, None] * squared + (band_square // 2)[:, None]) // band_square[
        :, None
    ]
    migrated = jnp.zeros((2, bin_count, length), jnp.float32)
    for offset in range(MIG + 1):
        window = unfolded[:, offset : offset + bin_count, :]
        migrated = jnp.where((migration_shift == offset)[None], window, migrated)
    relative = centred.astype(jnp.float32) / (length // 2)
    matched_phase = math.pi * curvature * azimuth_rate[:, None] * (relative * relative)[None, :]
    focused = complex_mul(migrated, jnp.cos(matched_phase), jnp.sin(matched_phase), 0)
    inside = jnp.abs(centred)[None, :] < band_halfwidth[:, None]
    focused = jnp.where(inside[None], focused, 0.0)
    lead_size, trail_size = factor_pair(length)
    layout = focused.reshape(2, bin_count, lead_size, trail_size)
    sectioned = jnp.einsum("okci,cbij->obkj", dft_matrix(lead_size, 1.0), layout, precision=highest)
    twiddle_real, twiddle_imag = twiddle(lead_size, trail_size, length, 1.0)
    sectioned = complex_mul(sectioned, twiddle_real, twiddle_imag, 0)
    focused_image = jnp.einsum(
        "olcj,cbkj->oblk", dft_matrix(trail_size, 1.0), sectioned, precision=highest
    )
    return focused_image.reshape(2, bin_count, length) / math.sqrt(length)


def plain_local(
    raw_echoes, chirp_spectrum, reconstruction, delays, azimuth_rate, band_halfwidth, migration
):
    compressed = range_focus(raw_echoes, chirp_spectrum)
    channels, _, local_pulses, length = compressed.shape
    azimuth_count = lax.axis_size("az")
    range_count = lax.axis_size("rg")
    bin_count = length // (azimuth_count * range_count)
    layout = compressed.reshape(channels, 2, local_pulses, azimuth_count, range_count, bin_count)
    layout = lax.all_to_all(layout, "rg", split_axis=4, concat_axis=4, tiled=True)
    layout = lax.all_to_all(layout, "az", split_axis=3, concat_axis=3, tiled=True)
    turned = layout.reshape(channels, 2, local_pulses, azimuth_count * range_count, bin_count)
    pulse_total = azimuth_count * range_count * local_pulses
    frequency = jnp.arange(pulse_total, dtype=jnp.int32)
    angles = (
        2.0
        * math.pi
        / pulse_total
        * (frequency[None, :] * delays[:, None] % pulse_total).astype(jnp.float32)
    )
    align_real = jnp.cos(angles)[None]
    align_imag = jnp.sin(angles)[None]
    mixing_real = reconstruction[0] * align_real - reconstruction[1] * align_imag
    mixing_imag = reconstruction[0] * align_imag + reconstruction[1] * align_real
    unfolded = reconstruct(turned, mixing_real, mixing_imag)
    margin_bins = passed_along(unfolded[:, :MIG, :], ("az", "rg"), -1)
    unfolded = jnp.concatenate([unfolded, margin_bins], axis=1)
    return azimuth_focus(unfolded, azimuth_rate, band_halfwidth, migration)


def split_constant(values):
    high = values.astype(ml_dtypes.bfloat16)
    low = (values - high.astype(np.float64)).astype(ml_dtypes.bfloat16)
    return np.stack([high, low])


def roots(rows, columns, length, direction):
    turns = (rows[:, None] * columns[None, :]) % length
    angles = 2.0 * np.pi / length * turns
    return np.cos(angles), direction * np.sin(angles)


def left_matrix(cosine, sine):
    return np.stack([np.stack([cosine, -sine], 1), np.stack([sine, cosine], 1)], 0)


def right_matrix(cosine, sine):
    return np.stack([np.stack([cosine, sine], 1), np.stack([-sine, cosine], 1)], 0)


def split(values):
    high = values.astype(jnp.bfloat16)
    low = (values - high.astype(jnp.float32)).astype(jnp.bfloat16)
    return high, low


def dot(a, b):
    return jnp.dot(a, b, preferred_element_type=jnp.float32)


def dot_right(values, matrix):
    high, low = split(values)
    return dot(high, matrix[0]) + (dot(low, matrix[0]) + dot(high, matrix[1]))


def dot_left(matrix, values):
    high, low = split(values)
    return dot(matrix[0], high) + (dot(matrix[1], high) + dot(matrix[0], low))


def cos_sin_turns(turns):
    quarter = jnp.floor(turns * 4.0 + 0.5)
    theta = (turns - quarter * 0.25) * (2.0 * math.pi)
    square = theta * theta
    cosine = 1.0 + square * (
        -0.5 + square * (1.0 / 24 + square * (-1.0 / 720 + square * (1.0 / 40320)))
    )
    sine = theta * (
        1.0
        + square
        * (-1.0 / 6 + square * (1.0 / 120 + square * (-1.0 / 5040 + square * (1.0 / 362880))))
    )
    index = quarter.astype(jnp.int32)
    odd = (index & 1) == 1
    cos_negative = ((index + 1) & 2) == 2
    sin_negative = (index & 2) == 2
    cos_size = jnp.where(odd, sine, cosine)
    sin_size = jnp.where(odd, cosine, sine)
    return (
        jnp.where(cos_negative, -cos_size, cos_size),
        jnp.where(sin_negative, -sin_size, sin_size),
    )


def spread_rows(values):
    return jnp.concatenate(
        [
            jnp.broadcast_to(values[h : h + 1, :], (LANES, LANES)).T
            for h in range(values.shape[0])
        ],
        axis=0,
    )


def doppler_bins_of(flat, sources, block, channel, pulses, matrix):
    z = jnp.concatenate(
        [
            flat[pl.ds(p * 8 + channel * 2 + part, sources, stride=block), :]
            for part in range(2)
            for p in range(pulses)
        ],
        axis=0,
    )
    return dot_right(z.T, matrix)


def mix_channels(spectra, mix, unfolded, rows, shift):
    channels = spectra.shape[0]
    pulses = spectra.shape[2] // 2
    length = channels * pulses

    def mix_rows(index, carry):
        at = pl.ds(pl.multiple_of(index * 8, 8), 8)
        to = pl.ds(pl.multiple_of(index * 8 + shift, 8), 8)
        spec = [spectra[c, at, :] for c in range(channels)]
        for b in range(channels):
            total_r = total_i = None
            for c in range(channels):
                m = b * channels + c
                m_r = jnp.broadcast_to(mix[0, m : m + 1, :], (8, pulses))
                m_i = jnp.broadcast_to(mix[1, m : m + 1, :], (8, pulses))
                d_r, d_i = spec[c][:, :pulses], spec[c][:, pulses:]
                r = m_r * d_r - m_i * d_i
                i = m_r * d_i + m_i * d_r
                total_r = r if c == 0 else total_r + r
                total_i = i if c == 0 else total_i + i
            unfolded[to, b * pulses : (b + 1) * pulses] = total_r
            unfolded[to, length + b * pulses : length + (b + 1) * pulses] = total_i
        return carry

    lax.fori_loop(0, rows // 8, mix_rows, 0)


def focus_rows(unfolded, cos_ref, sin_ref, reach_ref, square_ref, focused, rows):
    length = reach_ref.shape[1]

    def focus_band(b, carry):
        lane = pl.multiple_of(b * LANES, LANES)
        at_real = pl.ds(lane, LANES)
        at_imag = pl.ds(pl.multiple_of(length + lane, LANES), LANES)
        for start in range(0, rows, 8):
            at = slice(start, start + 8)
            band_square = square_ref[at, :]
            reach = reach_ref[at, at_real]
            real = unfolded[at, at_real]
            imag = unfolded[at, at_imag]
            bound = band_square
            for offset in range(1, MIG + 1):
                moved = reach >= bound
                window = slice(start + offset, start + offset + 8)
                real = jnp.where(moved, unfolded[window, at_real], real)
                imag = jnp.where(moved, unfolded[window, at_imag], imag)
                bound = bound + band_square
            cosine = cos_ref[at, at_real]
            sine = sin_ref[at, at_real]
            focused[at, at_real] = real * cosine - imag * sine
            focused[at, at_imag] = real * sine + imag * cosine
        return carry

    lax.fori_loop(0, length // LANES, focus_band, 0)


def compress_kernel(
    sizes,
    x_hbm,
    chirp_hbm,
    rate_hbm,
    band_hbm,
    migration_hbm,
    first_hbm,
    twiddle_hbm,
    fwd_hbm,
    inv_hbm,
    last_hbm,
    halo_hbm,
    reconstruction_hbm,
    delays_hbm,
    doppler_hbm,
    final_hbm,
    late_ref,
    late_halo_ref,
    cos_hbm,
    sin_hbm,
    reach_hbm,
    square_hbm,
    mix_hbm,
    edge_hbm,
    image_hbm,
    x_ref,
    chirp_ref,
    rate_ref,
    band_ref,
    migration_ref,
    first_ref,
    twiddle_ref,
    fwd_ref,
    inv_ref,
    last_ref,
    halo_ref,
    reconstruction_ref,
    delays_ref,
    doppler_ref,
    final_ref,
    send_ref,
    send_halo_ref,
    early_ref,
    rows_ref,
    cos_ref,
    sin_ref,
    reach_ref,
    square_ref,
    mix_ref,
    spectra,
    unfolded,
    focused,
    image_ref,
    load_sems,
    store_sems,
    local_sems,
    send_sems,
    recv_sems,
):
    pulses, channels, lead, devices, inner, length = sizes
    mine = lax.axis_index("az") * inner + lax.axis_index("rg")
    barrier = pltpu.get_barrier_semaphore()

    def place(index):
        return (lax.div(index, inner), lax.rem(index, inner))

    def greet(k, carry):
        pl.semaphore_signal(
            barrier,
            inc=1,
            device_id=place(lax.rem(mine + k, devices)),
            device_id_type=pl.DeviceIdType.MESH,
        )
        return carry

    loads = []

    def start_load(source, target):
        copy = pltpu.make_async_copy(source, target, load_sems.at[len(loads)])
        copy.start()
        loads.append(copy)
        return copy

    def pulse_load(p):
        at = pl.ds(p * channels, channels)
        return start_load(x_hbm.at[at], x_ref.at[at])

    load_x = [pulse_load(0)]
    load_first = start_load(first_hbm, first_ref)
    load_twiddle = start_load(twiddle_hbm, twiddle_ref)
    load_fwd = start_load(fwd_hbm, fwd_ref)
    load_chirp = start_load(chirp_hbm, chirp_ref)
    load_inv = start_load(inv_hbm, inv_ref)
    load_last = start_load(last_hbm, last_ref)
    load_x += [pulse_load(p) for p in range(1, pulses)]
    load_halo = start_load(halo_hbm, halo_ref)
    load_rate = start_load(rate_hbm, rate_ref)
    load_band = start_load(band_hbm, band_ref)
    load_migration = start_load(migration_hbm, migration_ref)
    load_reconstruction = start_load(reconstruction_hbm, reconstruction_ref)
    load_delays = start_load(delays_hbm, delays_ref)
    load_doppler = start_load(doppler_hbm, doppler_ref)
    load_final = start_load(final_hbm, final_ref)
    lax.fori_loop(1, devices, greet, 0)

    half_rows = pulses * 8

    def parts(chunk, target):
        if chunk == 0:
            at = pl.ds(0, 8)
            return send_ref.at[target, at], early_ref.at[mine, at]
        if chunk == 1:
            at = pl.ds(8, half_rows - 8)
            return send_ref.at[target, at], early_ref.at[mine, at]
        if chunk == 2:
            return send_ref.at[target, pl.ds(half_rows, half_rows)], late_ref.at[mine]
        return send_halo_ref.at[target], late_halo_ref.at[mine]

    def remote(chunk, i):
        far = lax.div(i + 1, 2)
        step = devices // 2 + far - 2 * far * lax.rem(i, 2)
        target = lax.rem(mine + step, devices)
        source, landing = parts(chunk, target)
        return pltpu.make_async_remote_copy(
            src_ref=source,
            dst_ref=landing,
            send_sem=send_sems.at[chunk, step],
            recv_sem=recv_sems.at[chunk, step],
            device_id=place(target),
            device_id_type=pl.DeviceIdType.MESH,
        )

    def send(chunk):
        def body(i, carry):
            remote(chunk, i).start()
            return carry

        lax.fori_loop(0, devices - 1, body, 0)

    lane = lax.broadcasted_iota(jnp.int32, (2 * lead, LANES), 1)
    groups = pulses * channels * MIG // LANES
    per_group = LANES // MIG
    pairs = channels // 2
    packs = [jnp.zeros((2 * lead, LANES), jnp.float32) for _ in range(groups)]
    for p in range(pulses):
        load_x[p].wait()
        if p == 0:
            load_first.wait()
        x = jnp.concatenate([x_ref[p * channels + c] for c in range(channels)], axis=1)
        y = dot_left(first_ref, x)
        if p == 0:
            load_twiddle.wait()
            load_fwd.wait()
            load_chirp.wait()
            load_inv.wait()
            tw_r = jnp.concatenate([twiddle_ref[0]] * channels, axis=0)
            tw_i = jnp.concatenate([twiddle_ref[1]] * channels, axis=0)
            chirp = jnp.concatenate(
                [chirp_ref[pl.ds(part, lead, stride=2), :] for part in range(2)], axis=0
            ).T
            top, bottom = chirp[:lead], chirp[lead:]
            left = lane[:lead] < lead
            chirp_r = jnp.where(left, top, pltpu.roll(bottom, lead, 1))
            chirp_i = jnp.where(left, pltpu.roll(top, lead, 1), bottom)
            chirp_r = jnp.concatenate([chirp_r] * channels, axis=0)
            chirp_i = jnp.concatenate([chirp_i] * channels, axis=0)
        y = jnp.concatenate([y[:, c * LANES : (c + 1) * LANES] for c in range(channels)], axis=0)
        y = y.reshape(channels, 2, lead, LANES)
        y_r = y[:, 0].reshape(channels * lead, LANES)
        y_i = y[:, 1].reshape(channels * lead, LANES)
        y = jnp.concatenate([y_r * tw_r - y_i * tw_i, y_r * tw_i + y_i * tw_r], axis=1)
        s = dot_right(y, fwd_ref)
        s_r, s_i = s[:, :LANES], s[:, LANES:]
        s = jnp.concatenate(
            [s_r * chirp_r + s_i * chirp_i, s_i * chirp_r - s_r * chirp_i], axis=1
        )
        t = dot_right(s, inv_ref)
        t_r, t_i = t[:, :LANES], t[:, LANES:]
        z_r = t_r * tw_r + t_i * tw_i
        z_i = t_i * tw_r - t_r * tw_i
        z = [
            jnp.concatenate(
                [z_r[c * lead : (c + 1) * lead], z_i[c * lead : (c + 1) * lead]], axis=0
            )
            for c in range(channels)
        ]
        stacked = jnp.concatenate(
            [jnp.concatenate([z[2 * k], z[2 * k + 1]], axis=0) for k in range(pairs)], axis=1
        )
        if p == 0:
            load_last.wait()
        w = dot_left(last_ref, stacked)
        line = lax.broadcasted_iota(jnp.int32, (w.shape[0], LANES), 0) % 8
        whole = jnp.where(line < 4, w[:, :LANES], w[:, LANES:]).reshape(2, devices, 8, LANES)
        send_ref[:, p * 8 : p * 8 + 8, :] = whole[0]
        send_ref[:, half_rows + p * 8 : half_rows + p * 8 + 8, :] = whole[1]
        for c in range(channels):
            signal = p * channels + c
            g, where = signal // per_group, signal % per_group
            moved = z[c] if where == 0 else pltpu.roll(z[c], where * MIG, 1)
            packs[g] = jnp.where(lane // MIG == where, moved, packs[g])
        if p == 0:
            pl.semaphore_wait(barrier, devices - 1)
            send(0)
    send(1)
    send(2)
    load_halo.wait()
    w = dot_left(halo_ref, jnp.concatenate(packs, axis=1))
    row = lax.broadcasted_iota(jnp.int32, (devices * HALO_ROWS, LANES), 0) % HALO_ROWS
    total = w[:, :LANES]
    for g in range(1, groups):
        total = jnp.where(row // 2 == g, w[:, g * LANES : (g + 1) * LANES], total)
    send_halo_ref[...] = total.reshape(devices, HALO_ROWS, LANES)[:, : 2 * groups, :]
    send(3)
    own = [
        pltpu.make_async_copy(
            send_ref.at[mine, pl.ds(0, half_rows)], early_ref.at[mine], local_sems.at[0]
        ),
        pltpu.make_async_copy(
            send_ref.at[mine, pl.ds(half_rows, half_rows)], late_ref.at[mine], local_sems.at[1]
        ),
        pltpu.make_async_copy(send_halo_ref.at[mine], late_halo_ref.at[mine], local_sems.at[2]),
    ]
    for copy in own:
        copy.start()

    load_reconstruction.wait()
    load_delays.wait()
    bins_f = pulses * devices
    row = lax.broadcasted_iota(jnp.int32, (channels * channels, bins_f), 0) % channels
    frequency = lax.broadcasted_iota(jnp.int32, (channels * channels, bins_f), 1)
    delay = jnp.zeros_like(row)
    for c in range(channels):
        one = jnp.broadcast_to(delays_ref[0:1, c : c + 1], row.shape)
        delay = jnp.where(row == c, one, delay)
    turns = lax.rem(frequency * delay, bins_f).astype(jnp.float32) * (1.0 / bins_f)
    align_r, align_i = cos_sin_turns(turns)
    rec_r, rec_i = reconstruction_ref[0], reconstruction_ref[1]
    mix_ref[0] = rec_r * align_r - rec_i * align_i
    mix_ref[1] = rec_r * align_i + rec_i * align_r
    load_rate.wait()
    load_band.wait()
    load_migration.wait()
    rows_ref[0] = spread_rows(rate_ref[...])
    rows_ref[1] = spread_rows(band_ref[...].astype(jnp.float32))
    rows_ref[2] = spread_rows(migration_ref[...].astype(jnp.float32))
    bins = rows_ref.shape[1]

    def tables(index, carry):
        at = pl.ds(pl.multiple_of(index * 8, 8), 8)
        rate = rows_ref[0, at, :]
        band = rows_ref[1, at, :].astype(jnp.int32)
        move = rows_ref[2, at, :].astype(jnp.int32)
        band_square = band * band
        square_ref[at, :] = band_square
        for start in range(0, length, LANES):
            doppler = lax.broadcasted_iota(jnp.int32, (8, LANES), 1) + start
            centred = jnp.where(doppler >= length // 2, doppler - length, doppler)
            relative = centred.astype(jnp.float32) * (2.0 / length)
            cosine, sine = cos_sin_turns(rate * (relative * relative * (curvature / 2.0)))
            inside = jnp.abs(centred) < band
            columns = slice(start, start + LANES)
            cos_ref[at, columns] = jnp.where(inside, cosine, 0.0)
            sin_ref[at, columns] = jnp.where(inside, sine, 0.0)
            reach_ref[at, columns] = move * jnp.minimum(centred * centred, band_square) + (
                band_square >> 1
            )
        return carry

    lax.fori_loop(0, bins // 8, tables, 0)
    stores = []

    def store(source, target):
        copy = pltpu.make_async_copy(source, target, store_sems.at[len(stores)])
        copy.start()
        stores.append(copy)

    ready = focused.shape[0]
    later = pl.ds(ready, bins - ready)
    store(cos_ref.at[later], cos_hbm)
    store(sin_ref.at[later], sin_hbm)
    store(reach_ref.at[later], reach_hbm)
    store(square_ref.at[later], square_hbm)
    store(mix_ref, mix_hbm)

    def arrived(chunks):
        def body(i, carry):
            for chunk in chunks:
                remote(chunk, i).wait_recv()
            return carry

        lax.fori_loop(0, devices - 1, body, 0)

    load_doppler.wait()
    own[0].wait()
    arrived((0, 1))
    flat = early_ref.reshape(devices * half_rows, LANES)
    for c in range(channels):
        spectra[c] = doppler_bins_of(flat, devices, half_rows, c, pulses, doppler_ref)
    mix_channels(spectra, mix_ref, unfolded, ready + MIG, 0)
    store(unfolded.at[pl.ds(ready, MIG)], edge_hbm)
    focus_rows(unfolded, cos_ref, sin_ref, reach_ref, square_ref, focused, ready)
    load_final.wait()
    image = dot_right(focused[...], final_ref)
    image_ref[0] = image[:, :length]
    image_ref[1] = image[:, length:]
    store(image_ref, image_hbm)
    for copy in own[1:]:
        copy.wait()
    arrived((2, 3))

    def sent(i, carry):
        for chunk in range(4):
            remote(chunk, i).wait_send()
        return carry

    lax.fori_loop(0, devices - 1, sent, 0)
    for copy in stores:
        copy.wait()


def azimuth_kernel(
    sizes,
    late_hbm,
    late_halo_hbm,
    cos_hbm,
    sin_hbm,
    reach_hbm,
    square_hbm,
    mix_hbm,
    edge_hbm,
    image_hbm,
    doppler_hbm,
    halo_doppler_hbm,
    final_hbm,
    out_hbm,
    late_ref,
    late_halo_ref,
    cos_ref,
    sin_ref,
    reach_ref,
    square_ref,
    mix_ref,
    doppler_ref,
    halo_doppler_ref,
    final_ref,
    spectra,
    unfolded,
    focused,
    image_ref,
    load_sems,
    store_sems,
):
    sources, pulses, channels, bins = sizes
    length = reach_ref.shape[1]
    ready = image_hbm.shape[1]
    rows = bins - ready
    loads = []

    def load(source, target):
        copy = pltpu.make_async_copy(source, target, load_sems.at[len(loads)])
        copy.start()
        loads.append(copy)
        return copy

    load_late = load(late_hbm, late_ref)
    load_doppler = load(doppler_hbm, doppler_ref)
    load_halo = load(late_halo_hbm, late_halo_ref)
    load_halo_doppler = load(halo_doppler_hbm, halo_doppler_ref)
    load_mix = load(mix_hbm, mix_ref)
    load_tables = [
        load(edge_hbm, unfolded.at[pl.ds(0, MIG)]),
        load(reach_hbm, reach_ref),
        load(square_hbm, square_ref),
        load(cos_hbm, cos_ref),
        load(sin_hbm, sin_ref),
    ]
    load_final = load(final_hbm, final_ref)
    passed = load(image_hbm, out_hbm.at[:, pl.ds(0, ready)])

    load_doppler.wait()
    load_late.wait()
    half = LANES
    flat = late_ref.reshape(sources * pulses * 8, LANES)
    for c in range(channels):
        spectra[c, :half, :] = doppler_bins_of(
            flat, sources, pulses * 8, c, pulses, doppler_ref
        )
    groups = pulses * channels * MIG // LANES
    per_group = LANES // (MIG * channels)
    load_halo.wait()
    load_halo_doppler.wait()
    h = jnp.concatenate(
        [late_halo_ref[pl.ds(j, sources, stride=2 * groups), :] for j in range(2 * groups)],
        axis=0,
    ).T
    step = channels * MIG
    halo = dot_right(h[:step], halo_doppler_ref.at[0])
    for k in range(1, per_group):
        halo = halo + dot_right(h[k * step : (k + 1) * step], halo_doppler_ref.at[k])
    for c in range(channels):
        spectra[c, half:, :] = halo[c * MIG : (c + 1) * MIG]
    load_mix.wait()
    mix_channels(spectra, mix_ref, unfolded, half + MIG, MIG)
    for copy in load_tables:
        copy.wait()
    focus_rows(unfolded, cos_ref, sin_ref, reach_ref, square_ref, focused, rows)
    load_final.wait()
    high, low = split(focused[...])
    stores = []
    pieces = 4
    width = 2 * length // pieces
    for k in range(pieces):
        at = slice(k * width, (k + 1) * width)
        part = dot(high, final_ref[0, :, at]) + (
            dot(low, final_ref[0, :, at]) + dot(high, final_ref[1, :, at])
        )
        image_ref[k] = part
        place = (k * width) // length
        copy = pltpu.make_async_copy(
            image_ref.at[k],
            out_hbm.at[place, pl.ds(ready, rows), pl.ds(k * width - place * length, width)],
            store_sems.at[k],
        )
        copy.start()
        stores.append(copy)
    passed.wait()
    for copy in stores:
        copy.wait()


def fits(pulses, channels, length, devices):
    local_pulses = pulses // devices
    signals = local_pulses * channels
    bins = length // devices
    lead = length // LANES
    return (
        pulses == LANES
        and length % (LANES * devices) == 0
        and bins == 2 * LANES
        and channels == 4
        and 2 * lead == LANES
        and devices % 8 == 0
        and signals * MIG % LANES == 0
        and LANES % (MIG * channels) == 0
        and 2 * (signals * MIG // LANES) <= HALO_ROWS
        and channels * pulses <= 512
    )


def hbm():
    return pl.BlockSpec(memory_space=pltpu.HBM)


def vmem():
    return pl.BlockSpec(memory_space=pltpu.VMEM)


def blocked_local(
    raw_echoes, chirp_spectrum, reconstruction, delays, azimuth_rate, band_halfwidth, migration
):
    local_pulses, channels, _, length = raw_echoes.shape
    inner = lax.axis_size("rg")
    devices = lax.axis_size("az") * inner
    bins = length // devices
    lead = length // LANES
    pulses = local_pulses * devices
    signals = local_pulses * channels
    doppler_bins = channels * pulses
    leads = np.arange(lead)
    lanes = np.arange(LANES)

    first = left_matrix(*roots(leads, leads, lead, -1.0))
    first = first.transpose(0, 1, 3, 2).reshape(2 * lead, 2 * lead)
    turned = np.concatenate([lanes[0::2], lanes[1::2]])
    forward = right_matrix(*roots(lanes, turned, LANES, -1.0)).reshape(2 * LANES, 2 * LANES)
    inverse = right_matrix(*roots(turned, lanes, LANES, 1.0)).reshape(2 * LANES, 2 * LANES)
    last = left_matrix(*roots(leads, leads, lead, 1.0)) / length
    by_device = last.reshape(2, devices, 2, 2 * lead).transpose(1, 0, 2, 3)
    pair = np.zeros((2, devices, 2, 2, 2, 2, 2 * lead))
    for s in range(2):
        pair[:, :, :, s, :, s, :] = by_device.transpose(2, 0, 1, 3)[:, :, None]
    pair = pair.reshape(devices * 16, 4 * lead)
    halo = np.zeros((devices, HALO_ROWS, 2 * lead))
    groups = signals * MIG // LANES
    for g in range(groups):
        halo[:-1, 2 * g : 2 * g + 2] = by_device[1:, :, 0]
    halo = halo.reshape(devices * HALO_ROWS, 2 * lead)
    twiddles = np.stack(roots(leads, lanes, length, -1.0)).astype(np.float32)

    sources = np.arange(devices)
    bins_f = np.arange(pulses)
    order = (np.arange(local_pulses)[:, None] + sources[None, :] * local_pulses).reshape(-1)
    scale = 1.0 / math.sqrt(pulses)
    to_doppler = right_matrix(*roots(order, bins_f, pulses, -1.0)) * scale
    to_doppler = to_doppler.reshape(2 * pulses, 2 * pulses)
    per_group = local_pulses // groups
    halo_doppler = []
    for k in range(per_group):
        by_group = []
        for g in range(groups):
            at = sources * local_pulses + g * per_group + k
            by_group.append(
                (right_matrix(*roots(at, bins_f, pulses, -1.0)) * scale).reshape(
                    2 * devices, 2 * pulses
                )
            )
        halo_doppler.append(split_constant(np.concatenate(by_group, axis=0)))
    halo_doppler = np.stack(halo_doppler)
    indices = np.arange(doppler_bins)
    final = right_matrix(*roots(indices, indices, doppler_bins, 1.0)) / math.sqrt(doppler_bins)
    final = final.reshape(2 * doppler_bins, 2 * doppler_bins)

    x = raw_echoes.reshape(signals, 2, lead, LANES).transpose(0, 2, 1, 3)
    x = x.reshape(signals, 2 * lead, LANES)
    chirp = chirp_spectrum.reshape(2, lead, LANES).transpose(1, 0, 2).reshape(2 * lead, LANES)
    by_lane = (bins // LANES, LANES)
    halo_rows = 2 * groups
    half_rows = local_pulses * 8
    ready = LANES - MIG
    rest = bins - ready
    f32, i32, bf16 = jnp.float32, jnp.int32, jnp.bfloat16
    doppler_matrix = split_constant(to_doppler)
    final_matrix = split_constant(final)
    operands = (
        x,
        chirp,
        azimuth_rate.reshape(by_lane),
        band_halfwidth.reshape(by_lane),
        migration.reshape(by_lane),
        split_constant(first),
        twiddles,
        split_constant(forward),
        split_constant(inverse),
        split_constant(pair),
        split_constant(halo),
        reconstruction.reshape(2, channels * channels, pulses),
        delays.reshape(1, channels),
        doppler_matrix,
        final_matrix,
    )
    shapes = (
        ((devices, half_rows, LANES), f32),
        ((devices, halo_rows, LANES), f32),
        ((rest, doppler_bins), f32),
        ((rest, doppler_bins), f32),
        ((rest, doppler_bins), i32),
        ((rest, LANES), i32),
        ((2, channels * channels, pulses), f32),
        ((MIG, 2 * doppler_bins), f32),
        ((2, ready, doppler_bins), f32),
    )
    middle = pl.pallas_call(
        functools.partial(
            compress_kernel, (local_pulses, channels, lead, devices, inner, doppler_bins)
        ),
        out_shape=tuple(jax.ShapeDtypeStruct(*shape) for shape in shapes),
        in_specs=[hbm()] * len(operands),
        out_specs=(hbm(),) * len(shapes),
        scratch_shapes=[pltpu.VMEM(value.shape, value.dtype) for value in operands]
        + [
            pltpu.VMEM((devices, 2 * half_rows, LANES), f32),
            pltpu.VMEM((devices, halo_rows, LANES), f32),
            pltpu.VMEM((devices, half_rows, LANES), f32),
            pltpu.VMEM((3, bins, LANES), f32),
            pltpu.VMEM((bins, doppler_bins), f32),
            pltpu.VMEM((bins, doppler_bins), f32),
            pltpu.VMEM((bins, doppler_bins), i32),
            pltpu.VMEM((bins, LANES), i32),
            pltpu.VMEM((2, channels * channels, pulses), f32),
            pltpu.VMEM((channels, LANES, 2 * pulses), f32),
            pltpu.VMEM((LANES, 2 * doppler_bins), f32),
            pltpu.VMEM((ready, 2 * doppler_bins), f32),
            pltpu.VMEM((2, ready, doppler_bins), f32),
            pltpu.SemaphoreType.DMA((len(operands) + local_pulses - 1,)),
            pltpu.SemaphoreType.DMA((7,)),
            pltpu.SemaphoreType.DMA((3,)),
            pltpu.SemaphoreType.DMA((4, devices)),
            pltpu.SemaphoreType.DMA((4, devices)),
        ],
        compiler_params=pltpu.CompilerParams(
            collective_id=0, has_side_effects=True, vmem_limit_bytes=KERNEL_VMEM
        ),
        name="compress_exchange",
    )(*operands)
    late, late_halo = middle[:2]
    late_halo = late_halo.reshape(devices * halo_rows, LANES)
    inputs = (late, late_halo, *middle[2:], doppler_matrix, halo_doppler, final_matrix)
    kept = inputs[:7] + inputs[9:]
    return pl.pallas_call(
        functools.partial(azimuth_kernel, (devices, local_pulses, channels, bins)),
        out_shape=jax.ShapeDtypeStruct((2, bins, doppler_bins), f32),
        in_specs=[hbm()] * len(inputs),
        out_specs=hbm(),
        scratch_shapes=[pltpu.VMEM(value.shape, value.dtype) for value in kept]
        + [
            pltpu.VMEM((channels, LANES + MIG, 2 * pulses), f32),
            pltpu.VMEM((rest + MIG, 2 * doppler_bins), f32),
            pltpu.VMEM((rest, 2 * doppler_bins), f32),
            pltpu.VMEM((4, rest, doppler_bins // 2), f32),
            pltpu.SemaphoreType.DMA((len(inputs),)),
            pltpu.SemaphoreType.DMA((4,)),
        ],
        compiler_params=pltpu.CompilerParams(vmem_limit_bytes=KERNEL_VMEM),
        name="azimuth_focus",
    )(*inputs)


def local(raw_echoes, chirp_spectrum, reconstruction, *rest):
    local_pulses, channels, _, length = raw_echoes.shape
    devices = lax.axis_size("az") * lax.axis_size("rg")
    if fits(local_pulses * devices, channels, length, devices):
        return blocked_local(raw_echoes, chirp_spectrum, reconstruction, *rest)
    return plain_local(raw_echoes, chirp_spectrum, reconstruction, *rest)


def solution(mesh):
    in_specs = (
        P(("az", "rg"), None, None, None),
        P(),
        P(),
        P(),
        P(("az", "rg")),
        P(("az", "rg")),
        P(("az", "rg")),
    )
    out_specs = P(None, ("az", "rg"), None)
    return jax.shard_map(local, mesh=mesh, in_specs=in_specs, out_specs=out_specs, check_vma=False)
```

```python
import functools
import math

import jax
import jax.numpy as jnp
import ml_dtypes
import numpy as np
from jax import lax
from jax.experimental import pallas as pl
from jax.experimental.pallas import tpu as pltpu
from jax.sharding import PartitionSpec as P

MIG = 16
LANES = 128
HALO_ROWS = 8
KERNEL_VMEM = 62 * 1024 * 1024


highest = lax.Precision.HIGHEST
curvature = 32.0


def passed_along(value, axis, by):
    size = lax.axis_size(axis)
    pairs = [(i, i + by) for i in range(size) if 0 <= i + by < size]
    return lax.ppermute(value, axis, pairs)


def factor_pair(length):
    largest = 1
    for candidate in range(1, length + 1):
        if candidate * candidate > length:
            break
        if length % candidate == 0:
            largest = candidate
    return (largest, length // largest)


def dft_matrix(length, direction):
    indices = jnp.arange(length, dtype=jnp.int32)
    angles = (
        2.0 * math.pi / length * (indices[:, None] * indices[None, :] % length).astype(jnp.float32)
    )
    cosine = jnp.cos(angles)
    sines = direction * jnp.sin(angles)
    return jnp.stack(
        [jnp.stack([cosine, -sines], axis=1), jnp.stack([sines, cosine], axis=1)], axis=0
    )


def twiddle(lead_size, trail_size, length, direction):
    lead_index = jnp.arange(lead_size, dtype=jnp.int32)
    trail_index = jnp.arange(trail_size, dtype=jnp.int32)
    angles = (
        2.0
        * math.pi
        / length
        * (lead_index[:, None] * trail_index[None, :] % length).astype(jnp.float32)
    )
    return (jnp.cos(angles), direction * jnp.sin(angles))


def complex_mul(values, factor_real, factor_imag, part_axis):
    real_part = lax.index_in_dim(values, 0, part_axis, keepdims=True)
    imag_part = lax.index_in_dim(values, 1, part_axis, keepdims=True)
    return jnp.concatenate(
        [
            real_part * factor_real - imag_part * factor_imag,
            real_part * factor_imag + imag_part * factor_real,
        ],
        axis=part_axis,
    )


def range_focus(raw_echoes, chirp_spectrum):
    local_pulses, channels, _, length = raw_echoes.shape
    lead_size, trail_size = factor_pair(length)
    layout = raw_echoes.reshape(local_pulses, channels, 2, lead_size, trail_size)
    sectioned = jnp.einsum(
        "okci,pqcij->pqokj", dft_matrix(lead_size, -1.0), layout, precision=highest
    )
    twiddle_real, twiddle_imag = twiddle(lead_size, trail_size, length, -1.0)
    sectioned = complex_mul(sectioned, twiddle_real, twiddle_imag, 2)
    spectrum = jnp.einsum(
        "olcj,pqckj->pqolk", dft_matrix(trail_size, -1.0), sectioned, precision=highest
    )
    spectrum = spectrum.reshape(local_pulses, channels, 2, length)
    spectrum = complex_mul(spectrum, chirp_spectrum[0], -chirp_spectrum[1], 2)
    layout = spectrum.reshape(local_pulses, channels, 2, lead_size, trail_size)
    sectioned = jnp.einsum(
        "okci,pqcij->pqokj", dft_matrix(lead_size, 1.0), layout, precision=highest
    )
    twiddle_real, twiddle_imag = twiddle(lead_size, trail_size, length, 1.0)
    sectioned = complex_mul(sectioned, twiddle_real, twiddle_imag, 2)
    restored = jnp.einsum(
        "olcj,pqckj->qoplk", dft_matrix(trail_size, 1.0), sectioned, precision=highest
    )
    return restored.reshape(channels, 2, local_pulses, length) / length


def reconstruct(turned, mixing_real, mixing_imag):
    channels, _, local_pulses, blocks, bin_count = turned.shape
    pulse_total = blocks * local_pulses
    sectioned = jnp.einsum("okcm,qcimb->qobik", dft_matrix(blocks, -1.0), turned, precision=highest)
    twiddle_real, twiddle_imag = twiddle(local_pulses, blocks, pulse_total, -1.0)
    sectioned = complex_mul(sectioned, twiddle_real, twiddle_imag, 1)
    spectrum = jnp.einsum(
        "olci,qcbik->qoblk", dft_matrix(local_pulses, -1.0), sectioned, precision=highest
    )
    spectrum = spectrum.reshape(channels, 2, bin_count, pulse_total) / math.sqrt(pulse_total)
    spec_real = spectrum[:, 0]
    spec_imag = spectrum[:, 1]
    unfolded_real = jnp.einsum(
        "bcf,crf->rbf", mixing_real, spec_real, precision=highest
    ) - jnp.einsum("bcf,crf->rbf", mixing_imag, spec_imag, precision=highest)
    unfolded_imag = jnp.einsum(
        "bcf,crf->rbf", mixing_real, spec_imag, precision=highest
    ) + jnp.einsum("bcf,crf->rbf", mixing_imag, spec_real, precision=highest)
    unfolded = jnp.stack([unfolded_real, unfolded_imag], axis=0)
    return unfolded.reshape(2, bin_count, channels * pulse_total)


def azimuth_focus(unfolded, azimuth_rate, band_halfwidth, migration):
    bin_count = azimuth_rate.shape[0]
    length = unfolded.shape[2]
    doppler_index = jnp.arange(length, dtype=jnp.int32)
    centred = doppler_index - length * (doppler_index >= length // 2).astype(jnp.int32)
    band_square = band_halfwidth * band_halfwidth
    squared = jnp.minimum((centred * centred)[None, :], band_square[:, None])
    migration_shift = (migration[:, None] * squared + (band_square // 2)[:, None]) // band_square[
        :, None
    ]
    migrated = jnp.zeros((2, bin_count, length), jnp.float32)
    for offset in range(MIG + 1):
        window = unfolded[:, offset : offset + bin_count, :]
        migrated = jnp.where((migration_shift == offset)[None], window, migrated)
    relative = centred.astype(jnp.float32) / (length // 2)
    matched_phase = math.pi * curvature * azimuth_rate[:, None] * (relative * relative)[None, :]
    focused = complex_mul(migrated, jnp.cos(matched_phase), jnp.sin(matched_phase), 0)
    inside = jnp.abs(centred)[None, :] < band_halfwidth[:, None]
    focused = jnp.where(inside[None], focused, 0.0)
    lead_size, trail_size = factor_pair(length)
    layout = focused.reshape(2, bin_count, lead_size, trail_size)
    sectioned = jnp.einsum("okci,cbij->obkj", dft_matrix(lead_size, 1.0), layout, precision=highest)
    twiddle_real, twiddle_imag = twiddle(lead_size, trail_size, length, 1.0)
    sectioned = complex_mul(sectioned, twiddle_real, twiddle_imag, 0)
    focused_image = jnp.einsum(
        "olcj,cbkj->oblk", dft_matrix(trail_size, 1.0), sectioned, precision=highest
    )
    return focused_image.reshape(2, bin_count, length) / math.sqrt(length)


def plain_local(
    raw_echoes, chirp_spectrum, reconstruction, delays, azimuth_rate, band_halfwidth, migration
):
    compressed = range_focus(raw_echoes, chirp_spectrum)
    channels, _, local_pulses, length = compressed.shape
    azimuth_count = lax.axis_size("az")
    range_count = lax.axis_size("rg")
    bin_count = length // (azimuth_count * range_count)
    layout = compressed.reshape(channels, 2, local_pulses, azimuth_count, range_count, bin_count)
    layout = lax.all_to_all(layout, "rg", split_axis=4, concat_axis=4, tiled=True)
    layout = lax.all_to_all(layout, "az", split_axis=3, concat_axis=3, tiled=True)
    turned = layout.reshape(channels, 2, local_pulses, azimuth_count * range_count, bin_count)
    pulse_total = azimuth_count * range_count * local_pulses
    frequency = jnp.arange(pulse_total, dtype=jnp.int32)
    angles = (
        2.0
        * math.pi
        / pulse_total
        * (frequency[None, :] * delays[:, None] % pulse_total).astype(jnp.float32)
    )
    align_real = jnp.cos(angles)[None]
    align_imag = jnp.sin(angles)[None]
    mixing_real = reconstruction[0] * align_real - reconstruction[1] * align_imag
    mixing_imag = reconstruction[0] * align_imag + reconstruction[1] * align_real
    unfolded = reconstruct(turned, mixing_real, mixing_imag)
    margin_bins = passed_along(unfolded[:, :MIG, :], ("az", "rg"), -1)
    unfolded = jnp.concatenate([unfolded, margin_bins], axis=1)
    return azimuth_focus(unfolded, azimuth_rate, band_halfwidth, migration)


def split_constant(values):
    high = values.astype(ml_dtypes.bfloat16)
    low = (values - high.astype(np.float64)).astype(ml_dtypes.bfloat16)
    return np.stack([high, low])


def roots(rows, columns, length, direction):
    turns = (rows[:, None] * columns[None, :]) % length
    angles = 2.0 * np.pi / length * turns
    return np.cos(angles), direction * np.sin(angles)


def left_matrix(cosine, sine):
    return np.stack([np.stack([cosine, -sine], 1), np.stack([sine, cosine], 1)], 0)


def right_matrix(cosine, sine):
    return np.stack([np.stack([cosine, sine], 1), np.stack([-sine, cosine], 1)], 0)


def split(values):
    high = values.astype(jnp.bfloat16)
    low = (values - high.astype(jnp.float32)).astype(jnp.bfloat16)
    return high, low


def dot(a, b):
    return jnp.dot(a, b, preferred_element_type=jnp.float32)


def dot_right(values, matrix):
    high, low = split(values)
    return dot(high, matrix[0]) + (dot(low, matrix[0]) + dot(high, matrix[1]))


def dot_left(matrix, values):
    high, low = split(values)
    return dot(matrix[0], high) + (dot(matrix[1], high) + dot(matrix[0], low))


def cos_sin_turns(turns):
    quarter = jnp.floor(turns * 4.0 + 0.5)
    theta = (turns - quarter * 0.25) * (2.0 * math.pi)
    square = theta * theta
    cosine = 1.0 + square * (
        -0.5 + square * (1.0 / 24 + square * (-1.0 / 720 + square * (1.0 / 40320)))
    )
    sine = theta * (
        1.0
        + square
        * (-1.0 / 6 + square * (1.0 / 120 + square * (-1.0 / 5040 + square * (1.0 / 362880))))
    )
    index = quarter.astype(jnp.int32)
    odd = (index & 1) == 1
    cos_negative = ((index + 1) & 2) == 2
    sin_negative = (index & 2) == 2
    cos_size = jnp.where(odd, sine, cosine)
    sin_size = jnp.where(odd, cosine, sine)
    return (
        jnp.where(cos_negative, -cos_size, cos_size),
        jnp.where(sin_negative, -sin_size, sin_size),
    )


def spread_rows(values):
    return jnp.concatenate(
        [
            jnp.broadcast_to(values[h : h + 1, :], (LANES, LANES)).T
            for h in range(values.shape[0])
        ],
        axis=0,
    )


def doppler_bins_of(flat, sources, block, channel, pulses, matrix):
    z = jnp.concatenate(
        [
            flat[pl.ds(p * 8 + channel * 2 + part, sources, stride=block), :]
            for part in range(2)
            for p in range(pulses)
        ],
        axis=0,
    )
    return dot_right(z.T, matrix)


def mix_channels(spectra, mix, unfolded, rows, shift):
    channels = spectra.shape[0]
    pulses = spectra.shape[2] // 2
    length = channels * pulses

    def mix_rows(index, carry):
        at = pl.ds(pl.multiple_of(index * 8, 8), 8)
        to = pl.ds(pl.multiple_of(index * 8 + shift, 8), 8)
        spec = [spectra[c, at, :] for c in range(channels)]
        for b in range(channels):
            total_r = total_i = None
            for c in range(channels):
                m = b * channels + c
                m_r = jnp.broadcast_to(mix[0, m : m + 1, :], (8, pulses))
                m_i = jnp.broadcast_to(mix[1, m : m + 1, :], (8, pulses))
                d_r, d_i = spec[c][:, :pulses], spec[c][:, pulses:]
                r = m_r * d_r - m_i * d_i
                i = m_r * d_i + m_i * d_r
                total_r = r if c == 0 else total_r + r
                total_i = i if c == 0 else total_i + i
            unfolded[to, b * pulses : (b + 1) * pulses] = total_r
            unfolded[to, length + b * pulses : length + (b + 1) * pulses] = total_i
        return carry

    lax.fori_loop(0, rows // 8, mix_rows, 0)


def focus_rows(unfolded, cos_ref, sin_ref, reach_ref, square_ref, focused, rows):
    length = reach_ref.shape[1]

    def focus_band(b, carry):
        lane = pl.multiple_of(b * LANES, LANES)
        at_real = pl.ds(lane, LANES)
        at_imag = pl.ds(pl.multiple_of(length + lane, LANES), LANES)
        for start in range(0, rows, 8):
            at = slice(start, start + 8)
            band_square = square_ref[at, :]
            reach = reach_ref[at, at_real]
            real = unfolded[at, at_real]
            imag = unfolded[at, at_imag]
            bound = band_square
            for offset in range(1, MIG + 1):
                moved = reach >= bound
                window = slice(start + offset, start + offset + 8)
                real = jnp.where(moved, unfolded[window, at_real], real)
                imag = jnp.where(moved, unfolded[window, at_imag], imag)
                bound = bound + band_square
            cosine = cos_ref[at, at_real]
            sine = sin_ref[at, at_real]
            focused[at, at_real] = real * cosine - imag * sine
            focused[at, at_imag] = real * sine + imag * cosine
        return carry

    lax.fori_loop(0, length // LANES, focus_band, 0)


def compress_kernel(
    sizes,
    x_hbm,
    chirp_hbm,
    rate_hbm,
    band_hbm,
    migration_hbm,
    first_hbm,
    twiddle_hbm,
    fwd_hbm,
    inv_hbm,
    last_hbm,
    halo_hbm,
    reconstruction_hbm,
    delays_hbm,
    doppler_hbm,
    final_hbm,
    late_ref,
    late_halo_ref,
    cos_hbm,
    sin_hbm,
    reach_hbm,
    square_hbm,
    mix_hbm,
    edge_hbm,
    image_hbm,
    x_ref,
    chirp_ref,
    rate_ref,
    band_ref,
    migration_ref,
    first_ref,
    twiddle_ref,
    fwd_ref,
    inv_ref,
    last_ref,
    halo_ref,
    reconstruction_ref,
    delays_ref,
    doppler_ref,
    final_ref,
    send_ref,
    send_halo_ref,
    early_ref,
    rows_ref,
    cos_ref,
    sin_ref,
    reach_ref,
    square_ref,
    mix_ref,
    spectra,
    unfolded,
    focused,
    image_ref,
    load_sems,
    store_sems,
    local_sems,
    send_sems,
    recv_sems,
):
    pulses, channels, lead, devices, inner, length = sizes
    mine = lax.axis_index("az") * inner + lax.axis_index("rg")
    barrier = pltpu.get_barrier_semaphore()

    def place(index):
        return (lax.div(index, inner), lax.rem(index, inner))

    def greet(k, carry):
        pl.semaphore_signal(
            barrier,
            inc=1,
            device_id=place(lax.rem(mine + k, devices)),
            device_id_type=pl.DeviceIdType.MESH,
        )
        return carry

    loads = []

    def start_load(source, target):
        copy = pltpu.make_async_copy(source, target, load_sems.at[len(loads)])
        copy.start()
        loads.append(copy)
        return copy

    def pulse_load(p):
        at = pl.ds(p * channels, channels)
        return start_load(x_hbm.at[at], x_ref.at[at])

    load_x = [pulse_load(0)]
    load_first = start_load(first_hbm, first_ref)
    load_twiddle = start_load(twiddle_hbm, twiddle_ref)
    load_fwd = start_load(fwd_hbm, fwd_ref)
    load_chirp = start_load(chirp_hbm, chirp_ref)
    load_inv = start_load(inv_hbm, inv_ref)
    load_last = start_load(last_hbm, last_ref)
    load_x += [pulse_load(p) for p in range(1, pulses)]
    load_halo = start_load(halo_hbm, halo_ref)
    load_rate = start_load(rate_hbm, rate_ref)
    load_band = start_load(band_hbm, band_ref)
    load_migration = start_load(migration_hbm, migration_ref)
    load_reconstruction = start_load(reconstruction_hbm, reconstruction_ref)
    load_delays = start_load(delays_hbm, delays_ref)
    load_doppler = start_load(doppler_hbm, doppler_ref)
    load_final = start_load(final_hbm, final_ref)
    lax.fori_loop(1, devices, greet, 0)

    half_rows = pulses * 8

    def parts(chunk, target):
        if chunk == 0:
            at = pl.ds(0, 8)
            return send_ref.at[target, at], early_ref.at[mine, at]
        if chunk == 1:
            at = pl.ds(8, half_rows - 8)
            return send_ref.at[target, at], early_ref.at[mine, at]
        if chunk == 2:
            return send_ref.at[target, pl.ds(half_rows, half_rows)], late_ref.at[mine]
        return send_halo_ref.at[target], late_halo_ref.at[mine]

    def remote(chunk, i):
        far = lax.div(i + 1, 2)
        step = devices // 2 + far - 2 * far * lax.rem(i, 2)
        target = lax.rem(mine + step, devices)
        source, landing = parts(chunk, target)
        return pltpu.make_async_remote_copy(
            src_ref=source,
            dst_ref=landing,
            send_sem=send_sems.at[chunk, step],
            recv_sem=recv_sems.at[chunk, step],
            device_id=place(target),
            device_id_type=pl.DeviceIdType.MESH,
        )

    def send(chunk):
        def body(i, carry):
            remote(chunk, i).start()
            return carry

        lax.fori_loop(0, devices - 1, body, 0)

    lane = lax.broadcasted_iota(jnp.int32, (2 * lead, LANES), 1)
    groups = pulses * channels * MIG // LANES
    per_group = LANES // MIG
    pairs = channels // 2
    packs = [jnp.zeros((2 * lead, LANES), jnp.float32) for _ in range(groups)]
    for p in range(pulses):
        load_x[p].wait()
        if p == 0:
            load_first.wait()
        x = jnp.concatenate([x_ref[p * channels + c] for c in range(channels)], axis=1)
        y = dot_left(first_ref, x)
        if p == 0:
            load_twiddle.wait()
            load_fwd.wait()
            load_chirp.wait()
            load_inv.wait()
            tw_r = jnp.concatenate([twiddle_ref[0]] * channels, axis=0)
            tw_i = jnp.concatenate([twiddle_ref[1]] * channels, axis=0)
            chirp = jnp.concatenate(
                [chirp_ref[pl.ds(part, lead, stride=2), :] for part in range(2)], axis=0
            ).T
            top, bottom = chirp[:lead], chirp[lead:]
            left = lane[:lead] < lead
            chirp_r = jnp.where(left, top, pltpu.roll(bottom, lead, 1))
            chirp_i = jnp.where(left, pltpu.roll(top, lead, 1), bottom)
            chirp_r = jnp.concatenate([chirp_r] * channels, axis=0)
            chirp_i = jnp.concatenate([chirp_i] * channels, axis=0)
        y = jnp.concatenate([y[:, c * LANES : (c + 1) * LANES] for c in range(channels)], axis=0)
        y = y.reshape(channels, 2, lead, LANES)
        y_r = y[:, 0].reshape(channels * lead, LANES)
        y_i = y[:, 1].reshape(channels * lead, LANES)
        y = jnp.concatenate([y_r * tw_r - y_i * tw_i, y_r * tw_i + y_i * tw_r], axis=1)
        s = dot_right(y, fwd_ref)
        s_r, s_i = s[:, :LANES], s[:, LANES:]
        s = jnp.concatenate(
            [s_r * chirp_r + s_i * chirp_i, s_i * chirp_r - s_r * chirp_i], axis=1
        )
        t = dot_right(s, inv_ref)
        t_r, t_i = t[:, :LANES], t[:, LANES:]
        z_r = t_r * tw_r + t_i * tw_i
        z_i = t_i * tw_r - t_r * tw_i
        z = [
            jnp.concatenate(
                [z_r[c * lead : (c + 1) * lead], z_i[c * lead : (c + 1) * lead]], axis=0
            )
            for c in range(channels)
        ]
        stacked = jnp.concatenate(
            [jnp.concatenate([z[2 * k], z[2 * k + 1]], axis=0) for k in range(pairs)], axis=1
        )
        if p == 0:
            load_last.wait()
        w = dot_left(last_ref, stacked)
        line = lax.broadcasted_iota(jnp.int32, (w.shape[0], LANES), 0) % 8
        whole = jnp.where(line < 4, w[:, :LANES], w[:, LANES:]).reshape(2, devices, 8, LANES)
        send_ref[:, p * 8 : p * 8 + 8, :] = whole[0]
        send_ref[:, half_rows + p * 8 : half_rows + p * 8 + 8, :] = whole[1]
        for c in range(channels):
            signal = p * channels + c
            g, where = signal // per_group, signal % per_group
            moved = z[c] if where == 0 else pltpu.roll(z[c], where * MIG, 1)
            packs[g] = jnp.where(lane // MIG == where, moved, packs[g])
        if p == 0:
            pl.semaphore_wait(barrier, devices - 1)
            send(0)
    send(1)
    load_halo.wait()
    w = dot_left(halo_ref, jnp.concatenate(packs, axis=1))
    row = lax.broadcasted_iota(jnp.int32, (devices * HALO_ROWS, LANES), 0) % HALO_ROWS
    total = w[:, :LANES]
    for g in range(1, groups):
        total = jnp.where(row // 2 == g, w[:, g * LANES : (g + 1) * LANES], total)
    send_halo_ref[...] = total.reshape(devices, HALO_ROWS, LANES)[:, : 2 * groups, :]
    own = [
        pltpu.make_async_copy(
            send_ref.at[mine, pl.ds(0, half_rows)], early_ref.at[mine], local_sems.at[0]
        ),
        pltpu.make_async_copy(
            send_ref.at[mine, pl.ds(half_rows, half_rows)], late_ref.at[mine], local_sems.at[1]
        ),
        pltpu.make_async_copy(send_halo_ref.at[mine], late_halo_ref.at[mine], local_sems.at[2]),
    ]
    for copy in own:
        copy.start()

    load_reconstruction.wait()
    load_delays.wait()
    bins_f = pulses * devices
    row = lax.broadcasted_iota(jnp.int32, (channels * channels, bins_f), 0) % channels
    frequency = lax.broadcasted_iota(jnp.int32, (channels * channels, bins_f), 1)
    delay = jnp.zeros_like(row)
    for c in range(channels):
        one = jnp.broadcast_to(delays_ref[0:1, c : c + 1], row.shape)
        delay = jnp.where(row == c, one, delay)
    turns = lax.rem(frequency * delay, bins_f).astype(jnp.float32) * (1.0 / bins_f)
    align_r, align_i = cos_sin_turns(turns)
    rec_r, rec_i = reconstruction_ref[0], reconstruction_ref[1]
    mix_ref[0] = rec_r * align_r - rec_i * align_i
    mix_ref[1] = rec_r * align_i + rec_i * align_r
    load_rate.wait()
    load_band.wait()
    load_migration.wait()
    rows_ref[0] = spread_rows(rate_ref[...])
    rows_ref[1] = spread_rows(band_ref[...].astype(jnp.float32))
    rows_ref[2] = spread_rows(migration_ref[...].astype(jnp.float32))
    bins = rows_ref.shape[1]

    def tables(index, carry):
        at = pl.ds(pl.multiple_of(index * 8, 8), 8)
        rate = rows_ref[0, at, :]
        band = rows_ref[1, at, :].astype(jnp.int32)
        move = rows_ref[2, at, :].astype(jnp.int32)
        band_square = band * band
        square_ref[at, :] = band_square
        for start in range(0, length, LANES):
            doppler = lax.broadcasted_iota(jnp.int32, (8, LANES), 1) + start
            centred = jnp.where(doppler >= length // 2, doppler - length, doppler)
            relative = centred.astype(jnp.float32) * (2.0 / length)
            cosine, sine = cos_sin_turns(rate * (relative * relative * (curvature / 2.0)))
            inside = jnp.abs(centred) < band
            columns = slice(start, start + LANES)
            cos_ref[at, columns] = jnp.where(inside, cosine, 0.0)
            sin_ref[at, columns] = jnp.where(inside, sine, 0.0)
            reach_ref[at, columns] = move * jnp.minimum(centred * centred, band_square) + (
                band_square >> 1
            )
        return carry

    lax.fori_loop(0, bins // 8, tables, 0)
    stores = []

    def store(source, target):
        copy = pltpu.make_async_copy(source, target, store_sems.at[len(stores)])
        copy.start()
        stores.append(copy)

    ready = focused.shape[0]
    later = pl.ds(ready, bins - ready)
    store(cos_ref.at[later], cos_hbm)
    store(sin_ref.at[later], sin_hbm)
    store(reach_ref.at[later], reach_hbm)
    store(square_ref.at[later], square_hbm)
    store(mix_ref, mix_hbm)

    def arrived(chunks):
        def body(i, carry):
            for chunk in chunks:
                remote(chunk, i).wait_recv()
            return carry

        lax.fori_loop(0, devices - 1, body, 0)

    def follow(i, carry):
        remote(1, i).wait_send()
        remote(2, i).start()
        remote(3, i).start()
        return carry

    lax.fori_loop(0, devices - 1, follow, 0)
    load_doppler.wait()
    own[0].wait()
    arrived((0, 1))
    flat = early_ref.reshape(devices * half_rows, LANES)
    for c in range(channels):
        spectra[c] = doppler_bins_of(flat, devices, half_rows, c, pulses, doppler_ref)
    mix_channels(spectra, mix_ref, unfolded, ready + MIG, 0)
    store(unfolded.at[pl.ds(ready, MIG)], edge_hbm)
    focus_rows(unfolded, cos_ref, sin_ref, reach_ref, square_ref, focused, ready)
    load_final.wait()
    image = dot_right(focused[...], final_ref)
    image_ref[0] = image[:, :length]
    image_ref[1] = image[:, length:]
    store(image_ref, image_hbm)
    for copy in own[1:]:
        copy.wait()
    arrived((2, 3))

    def sent(i, carry):
        for chunk in (0, 2, 3):
            remote(chunk, i).wait_send()
        return carry

    lax.fori_loop(0, devices - 1, sent, 0)
    for copy in stores:
        copy.wait()


def azimuth_kernel(
    sizes,
    late_hbm,
    late_halo_hbm,
    cos_hbm,
    sin_hbm,
    reach_hbm,
    square_hbm,
    mix_hbm,
    edge_hbm,
    image_hbm,
    doppler_hbm,
    halo_doppler_hbm,
    final_hbm,
    out_hbm,
    late_ref,
    late_halo_ref,
    cos_ref,
    sin_ref,
    reach_ref,
    square_ref,
    mix_ref,
    doppler_ref,
    halo_doppler_ref,
    final_ref,
    spectra,
    unfolded,
    focused,
    image_ref,
    early_image_ref,
    load_sems,
    store_sems,
):
    sources, pulses, channels, bins = sizes
    length = reach_ref.shape[1]
    ready = image_hbm.shape[1]
    rows = bins - ready
    loads = []

    def load(source, target):
        copy = pltpu.make_async_copy(source, target, load_sems.at[len(loads)])
        copy.start()
        loads.append(copy)
        return copy

    load_late = load(late_hbm, late_ref)
    load_doppler = load(doppler_hbm, doppler_ref)
    load_halo = load(late_halo_hbm, late_halo_ref)
    load_halo_doppler = load(halo_doppler_hbm, halo_doppler_ref)
    load_mix = load(mix_hbm, mix_ref)
    load_tables = [
        load(edge_hbm, unfolded.at[pl.ds(0, MIG)]),
        load(reach_hbm, reach_ref),
        load(square_hbm, square_ref),
        load(cos_hbm, cos_ref),
        load(sin_hbm, sin_ref),
    ]
    load_final = load(final_hbm, final_ref)
    load_image = load(image_hbm, early_image_ref)

    load_doppler.wait()
    load_late.wait()
    load_image.wait()
    passed = pltpu.make_async_copy(
        early_image_ref, out_hbm.at[:, pl.ds(0, ready)], store_sems.at[4]
    )
    passed.start()
    half = LANES
    flat = late_ref.reshape(sources * pulses * 8, LANES)
    for c in range(channels):
        spectra[c, :half, :] = doppler_bins_of(
            flat, sources, pulses * 8, c, pulses, doppler_ref
        )
    groups = pulses * channels * MIG // LANES
    per_group = LANES // (MIG * channels)
    load_halo.wait()
    load_halo_doppler.wait()
    h = jnp.concatenate(
        [late_halo_ref[pl.ds(j, sources, stride=2 * groups), :] for j in range(2 * groups)],
        axis=0,
    ).T
    step = channels * MIG
    halo = dot_right(h[:step], halo_doppler_ref.at[0])
    for k in range(1, per_group):
        halo = halo + dot_right(h[k * step : (k + 1) * step], halo_doppler_ref.at[k])
    for c in range(channels):
        spectra[c, half:, :] = halo[c * MIG : (c + 1) * MIG]
    load_mix.wait()
    mix_channels(spectra, mix_ref, unfolded, half + MIG, MIG)
    for copy in load_tables:
        copy.wait()
    focus_rows(unfolded, cos_ref, sin_ref, reach_ref, square_ref, focused, rows)
    load_final.wait()
    high, low = split(focused[...])
    stores = []
    pieces = 4
    width = 2 * length // pieces
    for k in range(pieces):
        at = slice(k * width, (k + 1) * width)
        part = dot(high, final_ref[0, :, at]) + (
            dot(low, final_ref[0, :, at]) + dot(high, final_ref[1, :, at])
        )
        image_ref[k] = part
        place = (k * width) // length
        copy = pltpu.make_async_copy(
            image_ref.at[k],
            out_hbm.at[place, pl.ds(ready, rows), pl.ds(k * width - place * length, width)],
            store_sems.at[k],
        )
        copy.start()
        stores.append(copy)
    passed.wait()
    for copy in stores:
        copy.wait()


def fits(pulses, channels, length, devices):
    local_pulses = pulses // devices
    signals = local_pulses * channels
    bins = length // devices
    lead = length // LANES
    return (
        pulses == LANES
        and length % (LANES * devices) == 0
        and bins == 2 * LANES
        and channels == 4
        and 2 * lead == LANES
        and devices % 8 == 0
        and signals * MIG % LANES == 0
        and LANES % (MIG * channels) == 0
        and 2 * (signals * MIG // LANES) <= HALO_ROWS
        and channels * pulses <= 512
    )


def hbm():
    return pl.BlockSpec(memory_space=pltpu.HBM)


def vmem():
    return pl.BlockSpec(memory_space=pltpu.VMEM)


def blocked_local(
    raw_echoes, chirp_spectrum, reconstruction, delays, azimuth_rate, band_halfwidth, migration
):
    local_pulses, channels, _, length = raw_echoes.shape
    inner = lax.axis_size("rg")
    devices = lax.axis_size("az") * inner
    bins = length // devices
    lead = length // LANES
    pulses = local_pulses * devices
    signals = local_pulses * channels
    doppler_bins = channels * pulses
    leads = np.arange(lead)
    lanes = np.arange(LANES)

    first = left_matrix(*roots(leads, leads, lead, -1.0))
    first = first.transpose(0, 1, 3, 2).reshape(2 * lead, 2 * lead)
    turned = np.concatenate([lanes[0::2], lanes[1::2]])
    forward = right_matrix(*roots(lanes, turned, LANES, -1.0)).reshape(2 * LANES, 2 * LANES)
    inverse = right_matrix(*roots(turned, lanes, LANES, 1.0)).reshape(2 * LANES, 2 * LANES)
    last = left_matrix(*roots(leads, leads, lead, 1.0)) / length
    by_device = last.reshape(2, devices, 2, 2 * lead).transpose(1, 0, 2, 3)
    pair = np.zeros((2, devices, 2, 2, 2, 2, 2 * lead))
    for s in range(2):
        pair[:, :, :, s, :, s, :] = by_device.transpose(2, 0, 1, 3)[:, :, None]
    pair = pair.reshape(devices * 16, 4 * lead)
    halo = np.zeros((devices, HALO_ROWS, 2 * lead))
    groups = signals * MIG // LANES
    for g in range(groups):
        halo[:-1, 2 * g : 2 * g + 2] = by_device[1:, :, 0]
    halo = halo.reshape(devices * HALO_ROWS, 2 * lead)
    twiddles = np.stack(roots(leads, lanes, length, -1.0)).astype(np.float32)

    sources = np.arange(devices)
    bins_f = np.arange(pulses)
    order = (np.arange(local_pulses)[:, None] + sources[None, :] * local_pulses).reshape(-1)
    scale = 1.0 / math.sqrt(pulses)
    to_doppler = right_matrix(*roots(order, bins_f, pulses, -1.0)) * scale
    to_doppler = to_doppler.reshape(2 * pulses, 2 * pulses)
    per_group = local_pulses // groups
    halo_doppler = []
    for k in range(per_group):
        by_group = []
        for g in range(groups):
            at = sources * local_pulses + g * per_group + k
            by_group.append(
                (right_matrix(*roots(at, bins_f, pulses, -1.0)) * scale).reshape(
                    2 * devices, 2 * pulses
                )
            )
        halo_doppler.append(split_constant(np.concatenate(by_group, axis=0)))
    halo_doppler = np.stack(halo_doppler)
    indices = np.arange(doppler_bins)
    final = right_matrix(*roots(indices, indices, doppler_bins, 1.0)) / math.sqrt(doppler_bins)
    final = final.reshape(2 * doppler_bins, 2 * doppler_bins)

    x = raw_echoes.reshape(signals, 2, lead, LANES).transpose(0, 2, 1, 3)
    x = x.reshape(signals, 2 * lead, LANES)
    chirp = chirp_spectrum.reshape(2, lead, LANES).transpose(1, 0, 2).reshape(2 * lead, LANES)
    by_lane = (bins // LANES, LANES)
    halo_rows = 2 * groups
    half_rows = local_pulses * 8
    ready = LANES - MIG
    rest = bins - ready
    f32, i32, bf16 = jnp.float32, jnp.int32, jnp.bfloat16
    doppler_matrix = split_constant(to_doppler)
    final_matrix = split_constant(final)
    operands = (
        x,
        chirp,
        azimuth_rate.reshape(by_lane),
        band_halfwidth.reshape(by_lane),
        migration.reshape(by_lane),
        split_constant(first),
        twiddles,
        split_constant(forward),
        split_constant(inverse),
        split_constant(pair),
        split_constant(halo),
        reconstruction.reshape(2, channels * channels, pulses),
        delays.reshape(1, channels),
        doppler_matrix,
        final_matrix,
    )
    shapes = (
        ((devices, half_rows, LANES), f32),
        ((devices, halo_rows, LANES), f32),
        ((rest, doppler_bins), f32),
        ((rest, doppler_bins), f32),
        ((rest, doppler_bins), i32),
        ((rest, LANES), i32),
        ((2, channels * channels, pulses), f32),
        ((MIG, 2 * doppler_bins), f32),
        ((2, ready, doppler_bins), f32),
    )
    middle = pl.pallas_call(
        functools.partial(
            compress_kernel, (local_pulses, channels, lead, devices, inner, doppler_bins)
        ),
        out_shape=tuple(jax.ShapeDtypeStruct(*shape) for shape in shapes),
        in_specs=[hbm()] * len(operands),
        out_specs=(hbm(),) * len(shapes),
        scratch_shapes=[pltpu.VMEM(value.shape, value.dtype) for value in operands]
        + [
            pltpu.VMEM((devices, 2 * half_rows, LANES), f32),
            pltpu.VMEM((devices, halo_rows, LANES), f32),
            pltpu.VMEM((devices, half_rows, LANES), f32),
            pltpu.VMEM((3, bins, LANES), f32),
            pltpu.VMEM((bins, doppler_bins), f32),
            pltpu.VMEM((bins, doppler_bins), f32),
            pltpu.VMEM((bins, doppler_bins), i32),
            pltpu.VMEM((bins, LANES), i32),
            pltpu.VMEM((2, channels * channels, pulses), f32),
            pltpu.VMEM((channels, LANES, 2 * pulses), f32),
            pltpu.VMEM((LANES, 2 * doppler_bins), f32),
            pltpu.VMEM((ready, 2 * doppler_bins), f32),
            pltpu.VMEM((2, ready, doppler_bins), f32),
            pltpu.SemaphoreType.DMA((len(operands) + local_pulses - 1,)),
            pltpu.SemaphoreType.DMA((7,)),
            pltpu.SemaphoreType.DMA((3,)),
            pltpu.SemaphoreType.DMA((4, devices)),
            pltpu.SemaphoreType.DMA((4, devices)),
        ],
        compiler_params=pltpu.CompilerParams(
            collective_id=0, has_side_effects=True, vmem_limit_bytes=KERNEL_VMEM
        ),
        name="compress_exchange",
    )(*operands)
    late, late_halo = middle[:2]
    late_halo = late_halo.reshape(devices * halo_rows, LANES)
    inputs = (late, late_halo, *middle[2:], doppler_matrix, halo_doppler, final_matrix)
    kept = inputs[:7] + inputs[9:]
    return pl.pallas_call(
        functools.partial(azimuth_kernel, (devices, local_pulses, channels, bins)),
        out_shape=jax.ShapeDtypeStruct((2, bins, doppler_bins), f32),
        in_specs=[hbm()] * len(inputs),
        out_specs=hbm(),
        scratch_shapes=[pltpu.VMEM(value.shape, value.dtype) for value in kept]
        + [
            pltpu.VMEM((channels, LANES + MIG, 2 * pulses), f32),
            pltpu.VMEM((rest + MIG, 2 * doppler_bins), f32),
            pltpu.VMEM((rest, 2 * doppler_bins), f32),
            pltpu.VMEM((4, rest, doppler_bins // 2), f32),
            pltpu.VMEM((2, ready, doppler_bins), f32),
            pltpu.SemaphoreType.DMA((len(inputs),)),
            pltpu.SemaphoreType.DMA((5,)),
        ],
        compiler_params=pltpu.CompilerParams(vmem_limit_bytes=KERNEL_VMEM),
        name="azimuth_focus",
    )(*inputs)


def local(raw_echoes, chirp_spectrum, reconstruction, *rest):
    local_pulses, channels, _, length = raw_echoes.shape
    devices = lax.axis_size("az") * lax.axis_size("rg")
    if fits(local_pulses * devices, channels, length, devices):
        return blocked_local(raw_echoes, chirp_spectrum, reconstruction, *rest)
    return plain_local(raw_echoes, chirp_spectrum, reconstruction, *rest)


def solution(mesh):
    in_specs = (
        P(("az", "rg"), None, None, None),
        P(),
        P(),
        P(),
        P(("az", "rg")),
        P(("az", "rg")),
        P(("az", "rg")),
    )
    out_specs = P(None, ("az", "rg"), None)
    return jax.shard_map(local, mesh=mesh, in_specs=in_specs, out_specs=out_specs, check_vma=False)
```

```python
import functools
import math

import jax
import jax.numpy as jnp
import ml_dtypes
import numpy as np
from jax import lax
from jax.experimental import pallas as pl
from jax.experimental.pallas import tpu as pltpu
from jax.sharding import PartitionSpec as P

MIG = 16
LANES = 128
HALO_ROWS = 8
KERNEL_VMEM = 62 * 1024 * 1024


highest = lax.Precision.HIGHEST
curvature = 32.0


def passed_along(value, axis, by):
    size = lax.axis_size(axis)
    pairs = [(i, i + by) for i in range(size) if 0 <= i + by < size]
    return lax.ppermute(value, axis, pairs)


def factor_pair(length):
    largest = 1
    for candidate in range(1, length + 1):
        if candidate * candidate > length:
            break
        if length % candidate == 0:
            largest = candidate
    return (largest, length // largest)


def dft_matrix(length, direction):
    indices = jnp.arange(length, dtype=jnp.int32)
    angles = (
        2.0 * math.pi / length * (indices[:, None] * indices[None, :] % length).astype(jnp.float32)
    )
    cosine = jnp.cos(angles)
    sines = direction * jnp.sin(angles)
    return jnp.stack(
        [jnp.stack([cosine, -sines], axis=1), jnp.stack([sines, cosine], axis=1)], axis=0
    )


def twiddle(lead_size, trail_size, length, direction):
    lead_index = jnp.arange(lead_size, dtype=jnp.int32)
    trail_index = jnp.arange(trail_size, dtype=jnp.int32)
    angles = (
        2.0
        * math.pi
        / length
        * (lead_index[:, None] * trail_index[None, :] % length).astype(jnp.float32)
    )
    return (jnp.cos(angles), direction * jnp.sin(angles))


def complex_mul(values, factor_real, factor_imag, part_axis):
    real_part = lax.index_in_dim(values, 0, part_axis, keepdims=True)
    imag_part = lax.index_in_dim(values, 1, part_axis, keepdims=True)
    return jnp.concatenate(
        [
            real_part * factor_real - imag_part * factor_imag,
            real_part * factor_imag + imag_part * factor_real,
        ],
        axis=part_axis,
    )


def range_focus(raw_echoes, chirp_spectrum):
    local_pulses, channels, _, length = raw_echoes.shape
    lead_size, trail_size = factor_pair(length)
    layout = raw_echoes.reshape(local_pulses, channels, 2, lead_size, trail_size)
    sectioned = jnp.einsum(
        "okci,pqcij->pqokj", dft_matrix(lead_size, -1.0), layout, precision=highest
    )
    twiddle_real, twiddle_imag = twiddle(lead_size, trail_size, length, -1.0)
    sectioned = complex_mul(sectioned, twiddle_real, twiddle_imag, 2)
    spectrum = jnp.einsum(
        "olcj,pqckj->pqolk", dft_matrix(trail_size, -1.0), sectioned, precision=highest
    )
    spectrum = spectrum.reshape(local_pulses, channels, 2, length)
    spectrum = complex_mul(spectrum, chirp_spectrum[0], -chirp_spectrum[1], 2)
    layout = spectrum.reshape(local_pulses, channels, 2, lead_size, trail_size)
    sectioned = jnp.einsum(
        "okci,pqcij->pqokj", dft_matrix(lead_size, 1.0), layout, precision=highest
    )
    twiddle_real, twiddle_imag = twiddle(lead_size, trail_size, length, 1.0)
    sectioned = complex_mul(sectioned, twiddle_real, twiddle_imag, 2)
    restored = jnp.einsum(
        "olcj,pqckj->qoplk", dft_matrix(trail_size, 1.0), sectioned, precision=highest
    )
    return restored.reshape(channels, 2, local_pulses, length) / length


def reconstruct(turned, mixing_real, mixing_imag):
    channels, _, local_pulses, blocks, bin_count = turned.shape
    pulse_total = blocks * local_pulses
    sectioned = jnp.einsum("okcm,qcimb->qobik", dft_matrix(blocks, -1.0), turned, precision=highest)
    twiddle_real, twiddle_imag = twiddle(local_pulses, blocks, pulse_total, -1.0)
    sectioned = complex_mul(sectioned, twiddle_real, twiddle_imag, 1)
    spectrum = jnp.einsum(
        "olci,qcbik->qoblk", dft_matrix(local_pulses, -1.0), sectioned, precision=highest
    )
    spectrum = spectrum.reshape(channels, 2, bin_count, pulse_total) / math.sqrt(pulse_total)
    spec_real = spectrum[:, 0]
    spec_imag = spectrum[:, 1]
    unfolded_real = jnp.einsum(
        "bcf,crf->rbf", mixing_real, spec_real, precision=highest
    ) - jnp.einsum("bcf,crf->rbf", mixing_imag, spec_imag, precision=highest)
    unfolded_imag = jnp.einsum(
        "bcf,crf->rbf", mixing_real, spec_imag, precision=highest
    ) + jnp.einsum("bcf,crf->rbf", mixing_imag, spec_real, precision=highest)
    unfolded = jnp.stack([unfolded_real, unfolded_imag], axis=0)
    return unfolded.reshape(2, bin_count, channels * pulse_total)


def azimuth_focus(unfolded, azimuth_rate, band_halfwidth, migration):
    bin_count = azimuth_rate.shape[0]
    length = unfolded.shape[2]
    doppler_index = jnp.arange(length, dtype=jnp.int32)
    centred = doppler_index - length * (doppler_index >= length // 2).astype(jnp.int32)
    band_square = band_halfwidth * band_halfwidth
    squared = jnp.minimum((centred * centred)[None, :], band_square[:, None])
    migration_shift = (migration[:, None] * squared + (band_square // 2)[:, None]) // band_square[
        :, None
    ]
    migrated = jnp.zeros((2, bin_count, length), jnp.float32)
    for offset in range(MIG + 1):
        window = unfolded[:, offset : offset + bin_count, :]
        migrated = jnp.where((migration_shift == offset)[None], window, migrated)
    relative = centred.astype(jnp.float32) / (length // 2)
    matched_phase = math.pi * curvature * azimuth_rate[:, None] * (relative * relative)[None, :]
    focused = complex_mul(migrated, jnp.cos(matched_phase), jnp.sin(matched_phase), 0)
    inside = jnp.abs(centred)[None, :] < band_halfwidth[:, None]
    focused = jnp.where(inside[None], focused, 0.0)
    lead_size, trail_size = factor_pair(length)
    layout = focused.reshape(2, bin_count, lead_size, trail_size)
    sectioned = jnp.einsum("okci,cbij->obkj", dft_matrix(lead_size, 1.0), layout, precision=highest)
    twiddle_real, twiddle_imag = twiddle(lead_size, trail_size, length, 1.0)
    sectioned = complex_mul(sectioned, twiddle_real, twiddle_imag, 0)
    focused_image = jnp.einsum(
        "olcj,cbkj->oblk", dft_matrix(trail_size, 1.0), sectioned, precision=highest
    )
    return focused_image.reshape(2, bin_count, length) / math.sqrt(length)


def plain_local(
    raw_echoes, chirp_spectrum, reconstruction, delays, azimuth_rate, band_halfwidth, migration
):
    compressed = range_focus(raw_echoes, chirp_spectrum)
    channels, _, local_pulses, length = compressed.shape
    azimuth_count = lax.axis_size("az")
    range_count = lax.axis_size("rg")
    bin_count = length // (azimuth_count * range_count)
    layout = compressed.reshape(channels, 2, local_pulses, azimuth_count, range_count, bin_count)
    layout = lax.all_to_all(layout, "rg", split_axis=4, concat_axis=4, tiled=True)
    layout = lax.all_to_all(layout, "az", split_axis=3, concat_axis=3, tiled=True)
    turned = layout.reshape(channels, 2, local_pulses, azimuth_count * range_count, bin_count)
    pulse_total = azimuth_count * range_count * local_pulses
    frequency = jnp.arange(pulse_total, dtype=jnp.int32)
    angles = (
        2.0
        * math.pi
        / pulse_total
        * (frequency[None, :] * delays[:, None] % pulse_total).astype(jnp.float32)
    )
    align_real = jnp.cos(angles)[None]
    align_imag = jnp.sin(angles)[None]
    mixing_real = reconstruction[0] * align_real - reconstruction[1] * align_imag
    mixing_imag = reconstruction[0] * align_imag + reconstruction[1] * align_real
    unfolded = reconstruct(turned, mixing_real, mixing_imag)
    margin_bins = passed_along(unfolded[:, :MIG, :], ("az", "rg"), -1)
    unfolded = jnp.concatenate([unfolded, margin_bins], axis=1)
    return azimuth_focus(unfolded, azimuth_rate, band_halfwidth, migration)


def split_constant(values):
    high = values.astype(ml_dtypes.bfloat16)
    low = (values - high.astype(np.float64)).astype(ml_dtypes.bfloat16)
    return np.stack([high, low])


def roots(rows, columns, length, direction):
    turns = (rows[:, None] * columns[None, :]) % length
    angles = 2.0 * np.pi / length * turns
    return np.cos(angles), direction * np.sin(angles)


def left_matrix(cosine, sine):
    return np.stack([np.stack([cosine, -sine], 1), np.stack([sine, cosine], 1)], 0)


def right_matrix(cosine, sine):
    return np.stack([np.stack([cosine, sine], 1), np.stack([-sine, cosine], 1)], 0)


def split(values):
    high = values.astype(jnp.bfloat16)
    low = (values - high.astype(jnp.float32)).astype(jnp.bfloat16)
    return high, low


def dot(a, b):
    return jnp.dot(a, b, preferred_element_type=jnp.float32)


def dot_right(values, matrix):
    high, low = split(values)
    return dot(high, matrix[0]) + (dot(low, matrix[0]) + dot(high, matrix[1]))


def dot_left(matrix, values):
    high, low = split(values)
    return dot(matrix[0], high) + (dot(matrix[1], high) + dot(matrix[0], low))


def cos_sin_turns(turns):
    quarter = jnp.floor(turns * 4.0 + 0.5)
    theta = (turns - quarter * 0.25) * (2.0 * math.pi)
    square = theta * theta
    cosine = 1.0 + square * (
        -0.5 + square * (1.0 / 24 + square * (-1.0 / 720 + square * (1.0 / 40320)))
    )
    sine = theta * (
        1.0
        + square
        * (-1.0 / 6 + square * (1.0 / 120 + square * (-1.0 / 5040 + square * (1.0 / 362880))))
    )
    index = quarter.astype(jnp.int32)
    odd = (index & 1) == 1
    cos_negative = ((index + 1) & 2) == 2
    sin_negative = (index & 2) == 2
    cos_size = jnp.where(odd, sine, cosine)
    sin_size = jnp.where(odd, cosine, sine)
    return (
        jnp.where(cos_negative, -cos_size, cos_size),
        jnp.where(sin_negative, -sin_size, sin_size),
    )


def spread_rows(values):
    return jnp.concatenate(
        [
            jnp.broadcast_to(values[h : h + 1, :], (LANES, LANES)).T
            for h in range(values.shape[0])
        ],
        axis=0,
    )


def dot_exact(values, matrix):
    high = values.astype(jnp.bfloat16)
    rest = values - high.astype(jnp.float32)
    middle = rest.astype(jnp.bfloat16)
    low = (rest - middle.astype(jnp.float32)).astype(jnp.bfloat16)
    return dot(high, matrix) + dot(middle, matrix) + dot(low, matrix)


def doppler_of(lane):
    return (lane % (LANES // 4)) * 4 + lane // (LANES // 4)


def mix_channels(spectra, mix, unfolded, rows, shift):
    channels = spectra.shape[0]
    pulses = spectra.shape[2] // 2
    length = channels * pulses

    def mix_rows(index, carry):
        at = pl.ds(pl.multiple_of(index * 8, 8), 8)
        to = pl.ds(pl.multiple_of(index * 8 + shift, 8), 8)
        spec = [spectra[c, at, :] for c in range(channels)]
        for b in range(channels):
            total_r = total_i = None
            for c in range(channels):
                m = b * channels + c
                m_r = jnp.broadcast_to(mix[0, m : m + 1, :], (8, pulses))
                m_i = jnp.broadcast_to(mix[1, m : m + 1, :], (8, pulses))
                d_r, d_i = spec[c][:, :pulses], spec[c][:, pulses:]
                r = m_r * d_r - m_i * d_i
                i = m_r * d_i + m_i * d_r
                total_r = r if c == 0 else total_r + r
                total_i = i if c == 0 else total_i + i
            unfolded[to, b * pulses : (b + 1) * pulses] = total_r
            unfolded[to, length + b * pulses : length + (b + 1) * pulses] = total_i
        return carry

    lax.fori_loop(0, rows // 8, mix_rows, 0)


def migrate_rows(unfolded, cos_ref, sin_ref, reach_ref, square_ref, focused, rows):
    length = reach_ref.shape[1]

    def focus_band(b, carry):
        lane = pl.multiple_of(b * LANES, LANES)
        at_real = pl.ds(lane, LANES)
        at_imag = pl.ds(pl.multiple_of(length + lane, LANES), LANES)
        for start in range(0, rows, 8):
            at = slice(start, start + 8)
            band_square = square_ref[at, :]
            reach = reach_ref[at, at_real]
            real = unfolded[at, at_real]
            imag = unfolded[at, at_imag]
            bound = band_square
            for offset in range(1, MIG + 1):
                moved = reach >= bound
                window = slice(start + offset, start + offset + 8)
                real = jnp.where(moved, unfolded[window, at_real], real)
                imag = jnp.where(moved, unfolded[window, at_imag], imag)
                bound = bound + band_square
            cosine = cos_ref[at, at_real]
            sine = sin_ref[at, at_real]
            focused[at, at_real] = real * cosine - imag * sine
            focused[at, at_imag] = real * sine + imag * cosine
        return carry

    lax.fori_loop(0, length // LANES, focus_band, 0)


def inverse_rows(focused, final_ref, twiddle_ref, at):
    group = LANES // 4
    rows = at.stop - at.start
    line = lax.broadcasted_iota(jnp.int32, (rows, LANES), 1) // group
    parts = []
    for part in range(2):
        base = part * 4 * LANES
        turned = []
        for b in range(4):
            value = focused[at, base + b * LANES : base + (b + 1) * LANES]
            turned.append(value if b == 0 else pltpu.roll(value, b * group, 1))
        grouped = []
        for j in range(4):
            value = turned[(0 - j) % 4]
            for g in range(1, 4):
                value = jnp.where(line == g, turned[(g - j) % 4], value)
            grouped.append(value if j == 0 else pltpu.roll(value, LANES - j * group, 1))
        parts.append(grouped)
    stacked = jnp.concatenate(
        [jnp.concatenate([parts[0][j], parts[1][j]], axis=1) for j in range(4)], axis=0
    )
    image = dot_right(stacked, final_ref)
    real, imag = [], []
    for j in range(4):
        r = image[j * rows : (j + 1) * rows, :LANES]
        i = image[j * rows : (j + 1) * rows, LANES:]
        if j > 0:
            t_r, t_i = twiddle_ref[0, j : j + 1, :], twiddle_ref[1, j : j + 1, :]
            r, i = r * t_r - i * t_i, r * t_i + i * t_r
        real.append(r)
        imag.append(i)
    a_r, a_i = real[0] + real[2], imag[0] + imag[2]
    b_r, b_i = real[0] - real[2], imag[0] - imag[2]
    c_r, c_i = real[1] + real[3], imag[1] + imag[3]
    d_r, d_i = imag[3] - imag[1], real[1] - real[3]
    return (
        jnp.concatenate([a_r + c_r, b_r + d_r, a_r - c_r, b_r - d_r], axis=1),
        jnp.concatenate([a_i + c_i, b_i + d_i, a_i - c_i, b_i - d_i], axis=1),
    )


def compress_kernel(
    sizes,
    x_hbm,
    chirp_hbm,
    rate_hbm,
    band_hbm,
    migration_hbm,
    first_hbm,
    twiddle_hbm,
    fwd_hbm,
    inv_hbm,
    last_hbm,
    halo_hbm,
    reconstruction_hbm,
    delays_hbm,
    order_hbm,
    recv_ref,
    cos_hbm,
    sin_hbm,
    reach_hbm,
    square_hbm,
    mix_hbm,
    x_ref,
    chirp_ref,
    rate_ref,
    band_ref,
    migration_ref,
    first_ref,
    twiddle_ref,
    fwd_ref,
    inv_ref,
    last_ref,
    halo_ref,
    reconstruction_ref,
    delays_ref,
    order_ref,
    send_ref,
    rows_ref,
    cos_ref,
    sin_ref,
    reach_ref,
    square_ref,
    mix_ref,
    load_sems,
    store_sems,
    local_sem,
    send_sems,
    recv_sems,
):
    pulses, channels, lead, devices, inner, length = sizes
    mine = lax.axis_index("az") * inner + lax.axis_index("rg")
    barrier = pltpu.get_barrier_semaphore()

    def place(index):
        return (lax.div(index, inner), lax.rem(index, inner))

    def greet(k, carry):
        pl.semaphore_signal(
            barrier,
            inc=1,
            device_id=place(lax.rem(mine + k, devices)),
            device_id_type=pl.DeviceIdType.MESH,
        )
        return carry

    loads = []

    def start_load(source, target):
        copy = pltpu.make_async_copy(source, target, load_sems.at[len(loads)])
        copy.start()
        loads.append(copy)
        return copy

    def pulse_load(p):
        at = pl.ds(p * channels, channels)
        return start_load(x_hbm.at[at], x_ref.at[at])

    load_x = [pulse_load(0)]
    load_first = start_load(first_hbm, first_ref)
    load_twiddle = start_load(twiddle_hbm, twiddle_ref)
    load_fwd = start_load(fwd_hbm, fwd_ref)
    load_chirp = start_load(chirp_hbm, chirp_ref)
    load_inv = start_load(inv_hbm, inv_ref)
    load_last = start_load(last_hbm, last_ref)
    load_x += [pulse_load(p) for p in range(1, pulses)]
    load_halo = start_load(halo_hbm, halo_ref)
    load_rate = start_load(rate_hbm, rate_ref)
    load_band = start_load(band_hbm, band_ref)
    load_migration = start_load(migration_hbm, migration_ref)
    load_reconstruction = start_load(reconstruction_hbm, reconstruction_ref)
    load_delays = start_load(delays_hbm, delays_ref)
    load_order = start_load(order_hbm, order_ref)
    lax.fori_loop(1, devices, greet, 0)

    rows = pulses * channels * 4 + HALO_ROWS
    cut = channels * 4

    def remote(chunk, i):
        far = lax.div(i + 1, 2)
        step = devices // 2 + far - 2 * far * lax.rem(i, 2)
        target = lax.rem(mine + step, devices)
        at = pl.ds(0, cut) if chunk == 0 else pl.ds(cut, rows - cut)
        return pltpu.make_async_remote_copy(
            src_ref=send_ref.at[target, at],
            dst_ref=recv_ref.at[mine, at],
            send_sem=send_sems.at[chunk, step],
            recv_sem=recv_sems.at[chunk, step],
            device_id=place(target),
            device_id_type=pl.DeviceIdType.MESH,
        )

    def send(chunk):
        def body(i, carry):
            remote(chunk, i).start()
            return carry

        lax.fori_loop(0, devices - 1, body, 0)

    lane = lax.broadcasted_iota(jnp.int32, (2 * lead, LANES), 1)
    groups = pulses * channels * MIG // LANES
    per_group = LANES // MIG
    pairs = channels // 2
    packs = [jnp.zeros((2 * lead, LANES), jnp.float32) for _ in range(groups)]
    for p in range(pulses):
        load_x[p].wait()
        if p == 0:
            load_first.wait()
        x = jnp.concatenate([x_ref[p * channels + c] for c in range(channels)], axis=1)
        y = dot_left(first_ref, x)
        if p == 0:
            load_twiddle.wait()
            load_fwd.wait()
            load_chirp.wait()
            load_inv.wait()
            tw_r = jnp.concatenate([twiddle_ref[0]] * channels, axis=0)
            tw_i = jnp.concatenate([twiddle_ref[1]] * channels, axis=0)
            chirp = jnp.concatenate(
                [chirp_ref[pl.ds(part, lead, stride=2), :] for part in range(2)], axis=0
            ).T
            top, bottom = chirp[:lead], chirp[lead:]
            left = lane[:lead] < lead
            chirp_r = jnp.where(left, top, pltpu.roll(bottom, lead, 1))
            chirp_i = jnp.where(left, pltpu.roll(top, lead, 1), bottom)
            chirp_r = jnp.concatenate([chirp_r] * channels, axis=0)
            chirp_i = jnp.concatenate([chirp_i] * channels, axis=0)
        y = jnp.concatenate([y[:, c * LANES : (c + 1) * LANES] for c in range(channels)], axis=0)
        y = y.reshape(channels, 2, lead, LANES)
        y_r = y[:, 0].reshape(channels * lead, LANES)
        y_i = y[:, 1].reshape(channels * lead, LANES)
        y = jnp.concatenate([y_r * tw_r - y_i * tw_i, y_r * tw_i + y_i * tw_r], axis=1)
        s = dot_right(y, fwd_ref)
        s_r, s_i = s[:, :LANES], s[:, LANES:]
        s = jnp.concatenate(
            [s_r * chirp_r + s_i * chirp_i, s_i * chirp_r - s_r * chirp_i], axis=1
        )
        t = dot_right(s, inv_ref)
        t_r, t_i = t[:, :LANES], t[:, LANES:]
        z_r = t_r * tw_r + t_i * tw_i
        z_i = t_i * tw_r - t_r * tw_i
        z = [
            jnp.concatenate(
                [z_r[c * lead : (c + 1) * lead], z_i[c * lead : (c + 1) * lead]], axis=0
            )
            for c in range(channels)
        ]
        stacked = jnp.concatenate(
            [jnp.concatenate([z[2 * k], z[2 * k + 1]], axis=0) for k in range(pairs)], axis=1
        )
        if p == 0:
            load_last.wait()
        w = dot_left(last_ref, stacked)
        for k in range(pairs):
            row = (p * pairs + k) * 8
            send_ref[:, row : row + 8, :] = w[:, k * LANES : (k + 1) * LANES].reshape(
                devices, 8, LANES
            )
        for c in range(channels):
            signal = p * channels + c
            g, where = signal // per_group, signal % per_group
            moved = z[c] if where == 0 else pltpu.roll(z[c], where * MIG, 1)
            packs[g] = jnp.where(lane // MIG == where, moved, packs[g])
        if p == 0:
            pl.semaphore_wait(barrier, devices - 1)
            send(0)
    load_halo.wait()
    w = dot_left(halo_ref, jnp.concatenate(packs, axis=1))
    row = lax.broadcasted_iota(jnp.int32, (devices * HALO_ROWS, LANES), 0) % HALO_ROWS
    total = w[:, :LANES]
    for g in range(1, groups):
        total = jnp.where(row // 2 == g, w[:, g * LANES : (g + 1) * LANES], total)
    send_ref[:, pulses * channels * 4 :, :] = total.reshape(devices, HALO_ROWS, LANES)
    send(1)
    own = pltpu.make_async_copy(send_ref.at[mine], recv_ref.at[mine], local_sem)
    own.start()

    load_reconstruction.wait()
    load_delays.wait()
    load_order.wait()
    bins_f = pulses * devices
    shape = (channels * channels, bins_f)
    row = lax.broadcasted_iota(jnp.int32, shape, 0) % channels
    frequency = doppler_of(lax.broadcasted_iota(jnp.int32, shape, 1))
    delay = jnp.zeros_like(row)
    for c in range(channels):
        one = jnp.broadcast_to(delays_ref[0:1, c : c + 1], row.shape)
        delay = jnp.where(row == c, one, delay)
    turns = lax.rem(frequency * delay, bins_f).astype(jnp.float32) * (1.0 / bins_f)
    align_r, align_i = cos_sin_turns(turns)
    rec_r = dot_exact(reconstruction_ref[0], order_ref[...])
    rec_i = dot_exact(reconstruction_ref[1], order_ref[...])
    mix_ref[0] = rec_r * align_r - rec_i * align_i
    mix_ref[1] = rec_r * align_i + rec_i * align_r

    load_rate.wait()
    load_band.wait()
    load_migration.wait()
    rows_ref[0] = spread_rows(rate_ref[...])
    rows_ref[1] = spread_rows(band_ref[...].astype(jnp.float32))
    rows_ref[2] = spread_rows(migration_ref[...].astype(jnp.float32))
    bins = rows_ref.shape[1]

    def tables(index, carry):
        at = pl.ds(pl.multiple_of(index * 8, 8), 8)
        rate = rows_ref[0, at, :]
        band = rows_ref[1, at, :].astype(jnp.int32)
        move = rows_ref[2, at, :].astype(jnp.int32)
        band_square = band * band
        square_ref[at, :] = band_square
        for start in range(0, length, LANES):
            doppler = doppler_of(lax.broadcasted_iota(jnp.int32, (8, LANES), 1)) + start
            centred = jnp.where(doppler >= length // 2, doppler - length, doppler)
            relative = centred.astype(jnp.float32) * (2.0 / length)
            cosine, sine = cos_sin_turns(rate * (relative * relative * (curvature / 2.0)))
            inside = jnp.abs(centred) < band
            columns = slice(start, start + LANES)
            cos_ref[at, columns] = jnp.where(inside, cosine, 0.0)
            sin_ref[at, columns] = jnp.where(inside, sine, 0.0)
            reach_ref[at, columns] = move * jnp.minimum(centred * centred, band_square) + (
                band_square >> 1
            )
        return carry

    lax.fori_loop(0, bins // 8, tables, 0)
    stores = []
    for source, target in (
        (cos_ref, cos_hbm),
        (sin_ref, sin_hbm),
        (reach_ref, reach_hbm),
        (square_ref, square_hbm),
        (mix_ref, mix_hbm),
    ):
        copy = pltpu.make_async_copy(source, target, store_sems.at[len(stores)])
        copy.start()
        stores.append(copy)
    for copy in stores:
        copy.wait()
    own.wait()

    def finish(i, carry):
        for chunk in range(2):
            copy = remote(chunk, i)
            copy.wait_send()
            copy.wait_recv()
        return carry

    lax.fori_loop(0, devices - 1, finish, 0)


def azimuth_kernel(
    sizes,
    recv_hbm,
    doppler_hbm,
    halo_doppler_hbm,
    mix_hbm,
    reach_hbm,
    square_hbm,
    cos_hbm,
    sin_hbm,
    final_hbm,
    twiddle_hbm,
    out_hbm,
    recv_ref,
    doppler_ref,
    halo_doppler_ref,
    mix_ref,
    reach_ref,
    square_ref,
    cos_ref,
    sin_ref,
    final_ref,
    twiddle_ref,
    spectra,
    unfolded,
    focused,
    image_ref,
    load_sems,
    recv_sems,
    store_sems,
):
    sources, local_pulses, channels, bins = sizes
    block = local_pulses * channels * 4 + HALO_ROWS
    arrivals = []

    def arrive(row):
        at = pl.ds(row, 8)
        copy = pltpu.make_async_copy(
            recv_hbm.at[:, at], recv_ref.at[:, at], recv_sems.at[len(arrivals)]
        )
        copy.start()
        arrivals.append(copy)

    loads = []

    def load(source, target):
        copy = pltpu.make_async_copy(source, target, load_sems.at[len(loads)])
        copy.start()
        loads.append(copy)
        return copy

    load_doppler = load(doppler_hbm, doppler_ref)
    for pair in range(channels // 2):
        for p in range(local_pulses):
            arrive((p * (channels // 2) + pair) * 8)
    arrive(local_pulses * channels * 4)
    load_halo_doppler = load(halo_doppler_hbm, halo_doppler_ref)
    load_mix = load(mix_hbm, mix_ref)
    load_tables = [
        load(reach_hbm, reach_ref),
        load(square_hbm, square_ref),
        load(cos_hbm, cos_ref),
        load(sin_hbm, sin_ref),
    ]
    load_final = [load(final_hbm, final_ref), load(twiddle_hbm, twiddle_ref)]

    flat = recv_ref.reshape(sources * block, LANES)

    def rows_of(start):
        return flat[pl.ds(start, sources, stride=block), :]

    load_doppler.wait()
    for c in range(channels):
        if c % 2 == 0:
            for p in range(local_pulses):
                arrivals[c // 2 * local_pulses + p].wait()
        for half in range(bins // LANES):
            z = jnp.concatenate(
                [
                    rows_of(p * channels * 4 + c * 4 + part * 2 + half)
                    for part in range(2)
                    for p in range(local_pulses)
                ],
                axis=0,
            )
            spectra[c, half * LANES : (half + 1) * LANES, :] = dot_right(z.T, doppler_ref)
    groups = local_pulses * channels * MIG // LANES
    per_group = LANES // (MIG * channels)
    arrivals[-1].wait()
    load_halo_doppler.wait()
    h = jnp.concatenate(
        [rows_of(local_pulses * channels * 4 + j) for j in range(2 * groups)], axis=0
    ).T
    step = channels * MIG
    halo = dot_right(h[:step], halo_doppler_ref.at[0])
    for k in range(1, per_group):
        halo = halo + dot_right(h[k * step : (k + 1) * step], halo_doppler_ref.at[k])
    for c in range(channels):
        spectra[c, bins:, :] = halo[c * MIG : (c + 1) * MIG]
    load_mix.wait()
    mix_channels(spectra, mix_ref, unfolded, bins + MIG, 0)
    for copy in load_tables:
        copy.wait()
    migrate_rows(unfolded, cos_ref, sin_ref, reach_ref, square_ref, focused, bins)
    for copy in load_final:
        copy.wait()
    stores = []
    for k in range(bins // LANES):
        at = slice(k * LANES, (k + 1) * LANES)
        real, imag = inverse_rows(focused, final_ref, twiddle_ref, at)
        image_ref[0, at, :] = real
        image_ref[1, at, :] = imag
        rows = pl.ds(k * LANES, LANES)
        copy = pltpu.make_async_copy(
            image_ref.at[:, rows], out_hbm.at[:, rows], store_sems.at[k]
        )
        copy.start()
        stores.append(copy)
    for copy in stores:
        copy.wait()


def fits(pulses, channels, length, devices):
    local_pulses = pulses // devices
    signals = local_pulses * channels
    bins = length // devices
    lead = length // LANES
    return (
        pulses == LANES
        and length % (LANES * devices) == 0
        and bins == 2 * LANES
        and channels == 4
        and 2 * lead == LANES
        and devices % 8 == 0
        and signals * MIG % LANES == 0
        and LANES % (MIG * channels) == 0
        and 2 * (signals * MIG // LANES) <= HALO_ROWS
        and channels * pulses <= 512
    )


def hbm():
    return pl.BlockSpec(memory_space=pltpu.HBM)


def vmem():
    return pl.BlockSpec(memory_space=pltpu.VMEM)


def blocked_local(
    raw_echoes, chirp_spectrum, reconstruction, delays, azimuth_rate, band_halfwidth, migration
):
    local_pulses, channels, _, length = raw_echoes.shape
    inner = lax.axis_size("rg")
    devices = lax.axis_size("az") * inner
    bins = length // devices
    lead = length // LANES
    pulses = local_pulses * devices
    signals = local_pulses * channels
    doppler_bins = channels * pulses
    leads = np.arange(lead)
    lanes = np.arange(LANES)

    first = left_matrix(*roots(leads, leads, lead, -1.0))
    first = first.transpose(0, 1, 3, 2).reshape(2 * lead, 2 * lead)
    turned = np.concatenate([lanes[0::2], lanes[1::2]])
    forward = right_matrix(*roots(lanes, turned, LANES, -1.0)).reshape(2 * LANES, 2 * LANES)
    inverse = right_matrix(*roots(turned, lanes, LANES, 1.0)).reshape(2 * LANES, 2 * LANES)
    last = left_matrix(*roots(leads, leads, lead, 1.0)) / length
    pair = np.zeros((devices, 2, 2, 2, 2, 2 * lead))
    by_device = last.reshape(2, devices, 2, 2 * lead).transpose(1, 0, 2, 3)
    for s in range(2):
        pair[:, s, :, :, s, :] = by_device
    pair = pair.reshape(devices * 8, 4 * lead)
    halo = np.zeros((devices, HALO_ROWS, 2 * lead))
    groups = signals * MIG // LANES
    for g in range(groups):
        halo[:-1, 2 * g : 2 * g + 2] = by_device[1:, :, 0]
    halo = halo.reshape(devices * HALO_ROWS, 2 * lead)
    twiddles = np.stack(roots(leads, lanes, length, -1.0)).astype(np.float32)

    sources = np.arange(devices)
    bins_f = doppler_of(np.arange(pulses))
    order_f = (np.arange(pulses)[:, None] == bins_f[None, :]).astype(ml_dtypes.bfloat16)
    order = (np.arange(local_pulses)[:, None] + sources[None, :] * local_pulses).reshape(-1)
    scale = 1.0 / math.sqrt(pulses)
    to_doppler = right_matrix(*roots(order, bins_f, pulses, -1.0)) * scale
    to_doppler = to_doppler.reshape(2 * pulses, 2 * pulses)
    per_group = local_pulses // groups
    halo_doppler = []
    for k in range(per_group):
        by_group = []
        for g in range(groups):
            at = sources * local_pulses + g * per_group + k
            by_group.append(
                (right_matrix(*roots(at, bins_f, pulses, -1.0)) * scale).reshape(
                    2 * devices, 2 * pulses
                )
            )
        halo_doppler.append(split_constant(np.concatenate(by_group, axis=0)))
    halo_doppler = np.stack(halo_doppler)
    final = right_matrix(*roots(lanes, lanes, LANES, 1.0)) / math.sqrt(doppler_bins)
    final = split_constant(final.reshape(2 * LANES, 2 * LANES))
    regroup = np.stack(roots(np.arange(8) % 4, lanes, doppler_bins, 1.0)).astype(np.float32)

    x = raw_echoes.reshape(signals, 2, lead, LANES).transpose(0, 2, 1, 3)
    x = x.reshape(signals, 2 * lead, LANES)
    chirp = chirp_spectrum.reshape(2, lead, LANES).transpose(1, 0, 2).reshape(2 * lead, LANES)
    block = signals * 4 + HALO_ROWS
    tables = (bins, doppler_bins)
    by_lane = (bins // LANES, LANES)
    operands = (
        x,
        chirp,
        azimuth_rate.reshape(by_lane),
        band_halfwidth.reshape(by_lane),
        migration.reshape(by_lane),
        split_constant(first),
        twiddles,
        split_constant(forward),
        split_constant(inverse),
        split_constant(pair),
        split_constant(halo),
        reconstruction.reshape(2, channels * channels, pulses),
        delays.reshape(1, channels),
        order_f,
    )
    received, cosine, sine, reach, square, mix = pl.pallas_call(
        functools.partial(
            compress_kernel, (local_pulses, channels, lead, devices, inner, doppler_bins)
        ),
        out_shape=(
            jax.ShapeDtypeStruct((devices, block, LANES), jnp.float32),
            jax.ShapeDtypeStruct(tables, jnp.float32),
            jax.ShapeDtypeStruct(tables, jnp.float32),
            jax.ShapeDtypeStruct(tables, jnp.int32),
            jax.ShapeDtypeStruct((bins, LANES), jnp.int32),
            jax.ShapeDtypeStruct((2, channels * channels, pulses), jnp.float32),
        ),
        in_specs=[hbm()] * len(operands),
        out_specs=(hbm(),) * 6,
        scratch_shapes=[pltpu.VMEM(value.shape, value.dtype) for value in operands]
        + [
            pltpu.VMEM((devices, block, LANES), jnp.float32),
            pltpu.VMEM((3, bins, LANES), jnp.float32),
            pltpu.VMEM(tables, jnp.float32),
            pltpu.VMEM(tables, jnp.float32),
            pltpu.VMEM(tables, jnp.int32),
            pltpu.VMEM((bins, LANES), jnp.int32),
            pltpu.VMEM((2, channels * channels, pulses), jnp.float32),
            pltpu.SemaphoreType.DMA((len(operands) + local_pulses - 1,)),
            pltpu.SemaphoreType.DMA((5,)),
            pltpu.SemaphoreType.DMA,
            pltpu.SemaphoreType.DMA((2, devices)),
            pltpu.SemaphoreType.DMA((2, devices)),
        ],
        compiler_params=pltpu.CompilerParams(
            collective_id=0, has_side_effects=True, vmem_limit_bytes=KERNEL_VMEM
        ),
        name="compress_exchange",
    )(*operands)
    inputs = (
        received,
        split_constant(to_doppler),
        halo_doppler,
        mix,
        reach,
        square,
        cosine,
        sine,
        final,
        regroup,
    )
    return pl.pallas_call(
        functools.partial(azimuth_kernel, (devices, local_pulses, channels, bins)),
        out_shape=jax.ShapeDtypeStruct((2, bins, doppler_bins), jnp.float32),
        in_specs=[hbm()] * len(inputs),
        out_specs=hbm(),
        scratch_shapes=[pltpu.VMEM(value.shape, value.dtype) for value in inputs]
        + [
            pltpu.VMEM((channels, bins + MIG, 2 * pulses), jnp.float32),
            pltpu.VMEM((bins + MIG, 2 * doppler_bins), jnp.float32),
            pltpu.VMEM((bins, 2 * doppler_bins), jnp.float32),
            pltpu.VMEM((2, bins, doppler_bins), jnp.float32),
            pltpu.SemaphoreType.DMA((len(inputs) - 1,)),
            pltpu.SemaphoreType.DMA((channels // 2 * local_pulses + 1,)),
            pltpu.SemaphoreType.DMA((bins // LANES,)),
        ],
        compiler_params=pltpu.CompilerParams(vmem_limit_bytes=KERNEL_VMEM),
        name="azimuth_focus",
    )(*inputs)


def local(raw_echoes, chirp_spectrum, reconstruction, *rest):
    local_pulses, channels, _, length = raw_echoes.shape
    devices = lax.axis_size("az") * lax.axis_size("rg")
    if fits(local_pulses * devices, channels, length, devices):
        return blocked_local(raw_echoes, chirp_spectrum, reconstruction, *rest)
    return plain_local(raw_echoes, chirp_spectrum, reconstruction, *rest)


def solution(mesh):
    in_specs = (
        P(("az", "rg"), None, None, None),
        P(),
        P(),
        P(),
        P(("az", "rg")),
        P(("az", "rg")),
        P(("az", "rg")),
    )
    out_specs = P(None, ("az", "rg"), None)
    return jax.shard_map(local, mesh=mesh, in_specs=in_specs, out_specs=out_specs, check_vma=False)
```

```python
import functools
import math

import jax
import jax.numpy as jnp
import ml_dtypes
import numpy as np
from jax import lax
from jax.experimental import pallas as pl
from jax.experimental.pallas import tpu as pltpu
from jax.sharding import PartitionSpec as P

MIG = 16
LANES = 128
HALO_ROWS = 8
KERNEL_VMEM = 62 * 1024 * 1024


highest = lax.Precision.HIGHEST
curvature = 32.0


def passed_along(value, axis, by):
    size = lax.axis_size(axis)
    pairs = [(i, i + by) for i in range(size) if 0 <= i + by < size]
    return lax.ppermute(value, axis, pairs)


def factor_pair(length):
    largest = 1
    for candidate in range(1, length + 1):
        if candidate * candidate > length:
            break
        if length % candidate == 0:
            largest = candidate
    return (largest, length // largest)


def dft_matrix(length, direction):
    indices = jnp.arange(length, dtype=jnp.int32)
    angles = (
        2.0 * math.pi / length * (indices[:, None] * indices[None, :] % length).astype(jnp.float32)
    )
    cosine = jnp.cos(angles)
    sines = direction * jnp.sin(angles)
    return jnp.stack(
        [jnp.stack([cosine, -sines], axis=1), jnp.stack([sines, cosine], axis=1)], axis=0
    )


def twiddle(lead_size, trail_size, length, direction):
    lead_index = jnp.arange(lead_size, dtype=jnp.int32)
    trail_index = jnp.arange(trail_size, dtype=jnp.int32)
    angles = (
        2.0
        * math.pi
        / length
        * (lead_index[:, None] * trail_index[None, :] % length).astype(jnp.float32)
    )
    return (jnp.cos(angles), direction * jnp.sin(angles))


def complex_mul(values, factor_real, factor_imag, part_axis):
    real_part = lax.index_in_dim(values, 0, part_axis, keepdims=True)
    imag_part = lax.index_in_dim(values, 1, part_axis, keepdims=True)
    return jnp.concatenate(
        [
            real_part * factor_real - imag_part * factor_imag,
            real_part * factor_imag + imag_part * factor_real,
        ],
        axis=part_axis,
    )


def range_focus(raw_echoes, chirp_spectrum):
    local_pulses, channels, _, length = raw_echoes.shape
    lead_size, trail_size = factor_pair(length)
    layout = raw_echoes.reshape(local_pulses, channels, 2, lead_size, trail_size)
    sectioned = jnp.einsum(
        "okci,pqcij->pqokj", dft_matrix(lead_size, -1.0), layout, precision=highest
    )
    twiddle_real, twiddle_imag = twiddle(lead_size, trail_size, length, -1.0)
    sectioned = complex_mul(sectioned, twiddle_real, twiddle_imag, 2)
    spectrum = jnp.einsum(
        "olcj,pqckj->pqolk", dft_matrix(trail_size, -1.0), sectioned, precision=highest
    )
    spectrum = spectrum.reshape(local_pulses, channels, 2, length)
    spectrum = complex_mul(spectrum, chirp_spectrum[0], -chirp_spectrum[1], 2)
    layout = spectrum.reshape(local_pulses, channels, 2, lead_size, trail_size)
    sectioned = jnp.einsum(
        "okci,pqcij->pqokj", dft_matrix(lead_size, 1.0), layout, precision=highest
    )
    twiddle_real, twiddle_imag = twiddle(lead_size, trail_size, length, 1.0)
    sectioned = complex_mul(sectioned, twiddle_real, twiddle_imag, 2)
    restored = jnp.einsum(
        "olcj,pqckj->qoplk", dft_matrix(trail_size, 1.0), sectioned, precision=highest
    )
    return restored.reshape(channels, 2, local_pulses, length) / length


def reconstruct(turned, mixing_real, mixing_imag):
    channels, _, local_pulses, blocks, bin_count = turned.shape
    pulse_total = blocks * local_pulses
    sectioned = jnp.einsum("okcm,qcimb->qobik", dft_matrix(blocks, -1.0), turned, precision=highest)
    twiddle_real, twiddle_imag = twiddle(local_pulses, blocks, pulse_total, -1.0)
    sectioned = complex_mul(sectioned, twiddle_real, twiddle_imag, 1)
    spectrum = jnp.einsum(
        "olci,qcbik->qoblk", dft_matrix(local_pulses, -1.0), sectioned, precision=highest
    )
    spectrum = spectrum.reshape(channels, 2, bin_count, pulse_total) / math.sqrt(pulse_total)
    spec_real = spectrum[:, 0]
    spec_imag = spectrum[:, 1]
    unfolded_real = jnp.einsum(
        "bcf,crf->rbf", mixing_real, spec_real, precision=highest
    ) - jnp.einsum("bcf,crf->rbf", mixing_imag, spec_imag, precision=highest)
    unfolded_imag = jnp.einsum(
        "bcf,crf->rbf", mixing_real, spec_imag, precision=highest
    ) + jnp.einsum("bcf,crf->rbf", mixing_imag, spec_real, precision=highest)
    unfolded = jnp.stack([unfolded_real, unfolded_imag], axis=0)
    return unfolded.reshape(2, bin_count, channels * pulse_total)


def azimuth_focus(unfolded, azimuth_rate, band_halfwidth, migration):
    bin_count = azimuth_rate.shape[0]
    length = unfolded.shape[2]
    doppler_index = jnp.arange(length, dtype=jnp.int32)
    centred = doppler_index - length * (doppler_index >= length // 2).astype(jnp.int32)
    band_square = band_halfwidth * band_halfwidth
    squared = jnp.minimum((centred * centred)[None, :], band_square[:, None])
    migration_shift = (migration[:, None] * squared + (band_square // 2)[:, None]) // band_square[
        :, None
    ]
    migrated = jnp.zeros((2, bin_count, length), jnp.float32)
    for offset in range(MIG + 1):
        window = unfolded[:, offset : offset + bin_count, :]
        migrated = jnp.where((migration_shift == offset)[None], window, migrated)
    relative = centred.astype(jnp.float32) / (length // 2)
    matched_phase = math.pi * curvature * azimuth_rate[:, None] * (relative * relative)[None, :]
    focused = complex_mul(migrated, jnp.cos(matched_phase), jnp.sin(matched_phase), 0)
    inside = jnp.abs(centred)[None, :] < band_halfwidth[:, None]
    focused = jnp.where(inside[None], focused, 0.0)
    lead_size, trail_size = factor_pair(length)
    layout = focused.reshape(2, bin_count, lead_size, trail_size)
    sectioned = jnp.einsum("okci,cbij->obkj", dft_matrix(lead_size, 1.0), layout, precision=highest)
    twiddle_real, twiddle_imag = twiddle(lead_size, trail_size, length, 1.0)
    sectioned = complex_mul(sectioned, twiddle_real, twiddle_imag, 0)
    focused_image = jnp.einsum(
        "olcj,cbkj->oblk", dft_matrix(trail_size, 1.0), sectioned, precision=highest
    )
    return focused_image.reshape(2, bin_count, length) / math.sqrt(length)


def plain_local(
    raw_echoes, chirp_spectrum, reconstruction, delays, azimuth_rate, band_halfwidth, migration
):
    compressed = range_focus(raw_echoes, chirp_spectrum)
    channels, _, local_pulses, length = compressed.shape
    azimuth_count = lax.axis_size("az")
    range_count = lax.axis_size("rg")
    bin_count = length // (azimuth_count * range_count)
    layout = compressed.reshape(channels, 2, local_pulses, azimuth_count, range_count, bin_count)
    layout = lax.all_to_all(layout, "rg", split_axis=4, concat_axis=4, tiled=True)
    layout = lax.all_to_all(layout, "az", split_axis=3, concat_axis=3, tiled=True)
    turned = layout.reshape(channels, 2, local_pulses, azimuth_count * range_count, bin_count)
    pulse_total = azimuth_count * range_count * local_pulses
    frequency = jnp.arange(pulse_total, dtype=jnp.int32)
    angles = (
        2.0
        * math.pi
        / pulse_total
        * (frequency[None, :] * delays[:, None] % pulse_total).astype(jnp.float32)
    )
    align_real = jnp.cos(angles)[None]
    align_imag = jnp.sin(angles)[None]
    mixing_real = reconstruction[0] * align_real - reconstruction[1] * align_imag
    mixing_imag = reconstruction[0] * align_imag + reconstruction[1] * align_real
    unfolded = reconstruct(turned, mixing_real, mixing_imag)
    margin_bins = passed_along(unfolded[:, :MIG, :], ("az", "rg"), -1)
    unfolded = jnp.concatenate([unfolded, margin_bins], axis=1)
    return azimuth_focus(unfolded, azimuth_rate, band_halfwidth, migration)


def split_constant(values):
    high = values.astype(ml_dtypes.bfloat16)
    low = (values - high.astype(np.float64)).astype(ml_dtypes.bfloat16)
    return np.stack([high, low])


def roots(rows, columns, length, direction):
    turns = (rows[:, None] * columns[None, :]) % length
    angles = 2.0 * np.pi / length * turns
    return np.cos(angles), direction * np.sin(angles)


def left_matrix(cosine, sine):
    return np.stack([np.stack([cosine, -sine], 1), np.stack([sine, cosine], 1)], 0)


def right_matrix(cosine, sine):
    return np.stack([np.stack([cosine, sine], 1), np.stack([-sine, cosine], 1)], 0)


def split(values):
    high = values.astype(jnp.bfloat16)
    low = (values - high.astype(jnp.float32)).astype(jnp.bfloat16)
    return high, low


def dot(a, b):
    return jnp.dot(a, b, preferred_element_type=jnp.float32)


def dot_right(values, matrix):
    high, low = split(values)
    return dot(high, matrix[0]) + (dot(low, matrix[0]) + dot(high, matrix[1]))


def dot_left(matrix, values):
    high, low = split(values)
    return dot(matrix[0], high) + (dot(matrix[1], high) + dot(matrix[0], low))


def cos_sin_turns(turns):
    quarter = jnp.floor(turns * 4.0 + 0.5)
    theta = (turns - quarter * 0.25) * (2.0 * math.pi)
    square = theta * theta
    cosine = 1.0 + square * (
        -0.5 + square * (1.0 / 24 + square * (-1.0 / 720 + square * (1.0 / 40320)))
    )
    sine = theta * (
        1.0
        + square
        * (-1.0 / 6 + square * (1.0 / 120 + square * (-1.0 / 5040 + square * (1.0 / 362880))))
    )
    index = quarter.astype(jnp.int32)
    odd = (index & 1) == 1
    cos_negative = ((index + 1) & 2) == 2
    sin_negative = (index & 2) == 2
    cos_size = jnp.where(odd, sine, cosine)
    sin_size = jnp.where(odd, cosine, sine)
    return (
        jnp.where(cos_negative, -cos_size, cos_size),
        jnp.where(sin_negative, -sin_size, sin_size),
    )


def spread_rows(values):
    return jnp.concatenate(
        [
            jnp.broadcast_to(values[h : h + 1, :], (LANES, LANES)).T
            for h in range(values.shape[0])
        ],
        axis=0,
    )


def dot_exact(values, matrix):
    high = values.astype(jnp.bfloat16)
    rest = values - high.astype(jnp.float32)
    middle = rest.astype(jnp.bfloat16)
    low = (rest - middle.astype(jnp.float32)).astype(jnp.bfloat16)
    return dot(high, matrix) + dot(middle, matrix) + dot(low, matrix)


def doppler_of(lane):
    return (lane % (LANES // 4)) * 4 + lane // (LANES // 4)


def mix_channels(spectra, mix, unfolded, rows, shift):
    channels = spectra.shape[0]
    pulses = spectra.shape[2] // 2
    length = channels * pulses

    def mix_rows(index, carry):
        at = pl.ds(pl.multiple_of(index * 8, 8), 8)
        to = pl.ds(pl.multiple_of(index * 8 + shift, 8), 8)
        spec = [spectra[c, at, :] for c in range(channels)]
        for b in range(channels):
            total_r = total_i = None
            for c in range(channels):
                m = b * channels + c
                m_r = jnp.broadcast_to(mix[0, m : m + 1, :], (8, pulses))
                m_i = jnp.broadcast_to(mix[1, m : m + 1, :], (8, pulses))
                d_r, d_i = spec[c][:, :pulses], spec[c][:, pulses:]
                r = m_r * d_r - m_i * d_i
                i = m_r * d_i + m_i * d_r
                total_r = r if c == 0 else total_r + r
                total_i = i if c == 0 else total_i + i
            unfolded[to, b * pulses : (b + 1) * pulses] = total_r
            unfolded[to, length + b * pulses : length + (b + 1) * pulses] = total_i
        return carry

    lax.fori_loop(0, rows // 8, mix_rows, 0)


def migrate_rows(unfolded, cos_ref, sin_ref, reach_ref, square_ref, focused, rows):
    length = reach_ref.shape[1]

    def focus_band(b, carry):
        lane = pl.multiple_of(b * LANES, LANES)
        at_real = pl.ds(lane, LANES)
        at_imag = pl.ds(pl.multiple_of(length + lane, LANES), LANES)
        for start in range(0, rows, 8):
            at = slice(start, start + 8)
            band_square = square_ref[at, :]
            reach = reach_ref[at, at_real]
            real = unfolded[at, at_real]
            imag = unfolded[at, at_imag]
            bound = band_square
            for offset in range(1, MIG + 1):
                moved = reach >= bound
                window = slice(start + offset, start + offset + 8)
                real = jnp.where(moved, unfolded[window, at_real], real)
                imag = jnp.where(moved, unfolded[window, at_imag], imag)
                bound = bound + band_square
            cosine = cos_ref[at, at_real]
            sine = sin_ref[at, at_real]
            focused[at, at_real] = real * cosine - imag * sine
            focused[at, at_imag] = real * sine + imag * cosine
        return carry

    lax.fori_loop(0, length // LANES, focus_band, 0)


def inverse_rows(focused, final_ref, twiddle_ref, at):
    group = LANES // 4
    rows = at.stop - at.start
    line = lax.broadcasted_iota(jnp.int32, (rows, LANES), 1) // group
    parts = []
    for part in range(2):
        base = part * 4 * LANES
        turned = []
        for b in range(4):
            value = focused[at, base + b * LANES : base + (b + 1) * LANES]
            turned.append(value if b == 0 else pltpu.roll(value, b * group, 1))
        grouped = []
        for j in range(4):
            value = turned[(0 - j) % 4]
            for g in range(1, 4):
                value = jnp.where(line == g, turned[(g - j) % 4], value)
            grouped.append(value if j == 0 else pltpu.roll(value, LANES - j * group, 1))
        parts.append(grouped)
    stacked = jnp.concatenate(
        [jnp.concatenate([parts[0][j], parts[1][j]], axis=1) for j in range(4)], axis=0
    )
    image = dot_right(stacked, final_ref)
    real, imag = [], []
    for j in range(4):
        r = image[j * rows : (j + 1) * rows, :LANES]
        i = image[j * rows : (j + 1) * rows, LANES:]
        if j > 0:
            t_r, t_i = twiddle_ref[0, j : j + 1, :], twiddle_ref[1, j : j + 1, :]
            r, i = r * t_r - i * t_i, r * t_i + i * t_r
        real.append(r)
        imag.append(i)
    a_r, a_i = real[0] + real[2], imag[0] + imag[2]
    b_r, b_i = real[0] - real[2], imag[0] - imag[2]
    c_r, c_i = real[1] + real[3], imag[1] + imag[3]
    d_r, d_i = imag[3] - imag[1], real[1] - real[3]
    return (
        jnp.concatenate([a_r + c_r, b_r + d_r, a_r - c_r, b_r - d_r], axis=1),
        jnp.concatenate([a_i + c_i, b_i + d_i, a_i - c_i, b_i - d_i], axis=1),
    )


def compress_kernel(
    sizes,
    x_hbm,
    chirp_hbm,
    rate_hbm,
    band_hbm,
    migration_hbm,
    first_hbm,
    twiddle_hbm,
    fwd_hbm,
    inv_hbm,
    last_hbm,
    halo_hbm,
    reconstruction_hbm,
    delays_hbm,
    order_hbm,
    recv_ref,
    cos_hbm,
    sin_hbm,
    reach_hbm,
    square_hbm,
    mix_hbm,
    x_ref,
    chirp_ref,
    rate_ref,
    band_ref,
    migration_ref,
    first_ref,
    twiddle_ref,
    fwd_ref,
    inv_ref,
    last_ref,
    halo_ref,
    reconstruction_ref,
    delays_ref,
    order_ref,
    send_ref,
    rows_ref,
    cos_ref,
    sin_ref,
    reach_ref,
    square_ref,
    mix_ref,
    load_sems,
    store_sems,
    local_sem,
    send_sems,
    recv_sems,
):
    pulses, channels, lead, devices, inner, length = sizes
    mine = lax.axis_index("az") * inner + lax.axis_index("rg")
    barrier = pltpu.get_barrier_semaphore()

    def place(index):
        return (lax.div(index, inner), lax.rem(index, inner))

    def greet(k, carry):
        pl.semaphore_signal(
            barrier,
            inc=1,
            device_id=place(lax.rem(mine + k, devices)),
            device_id_type=pl.DeviceIdType.MESH,
        )
        return carry

    loads = []

    def start_load(source, target):
        copy = pltpu.make_async_copy(source, target, load_sems.at[len(loads)])
        copy.start()
        loads.append(copy)
        return copy

    def pulse_load(p):
        at = pl.ds(p * channels, channels)
        return start_load(x_hbm.at[at], x_ref.at[at])

    load_x = [pulse_load(0)]
    load_first = start_load(first_hbm, first_ref)
    load_twiddle = start_load(twiddle_hbm, twiddle_ref)
    load_fwd = start_load(fwd_hbm, fwd_ref)
    load_chirp = start_load(chirp_hbm, chirp_ref)
    load_inv = start_load(inv_hbm, inv_ref)
    load_last = start_load(last_hbm, last_ref)
    load_x += [pulse_load(p) for p in range(1, pulses)]
    load_halo = start_load(halo_hbm, halo_ref)
    load_rate = start_load(rate_hbm, rate_ref)
    load_band = start_load(band_hbm, band_ref)
    load_migration = start_load(migration_hbm, migration_ref)
    load_reconstruction = start_load(reconstruction_hbm, reconstruction_ref)
    load_delays = start_load(delays_hbm, delays_ref)
    load_order = start_load(order_hbm, order_ref)
    lax.fori_loop(1, devices, greet, 0)

    rows = pulses * channels * 4 + HALO_ROWS
    cut = channels * 4
    middle = devices // 2

    def flipped(value, mask):
        result = value
        bit = 1
        while bit <= mask:
            if mask & bit:
                result = result + bit * (1 - 2 * lax.rem(lax.div(value, bit), 2))
            bit *= 2
        return result

    outer = devices // inner
    outer_at = [flipped(lax.axis_index("az"), mask) for mask in range(outer)]
    inner_at = [flipped(lax.axis_index("rg"), mask) for mask in range(inner)]

    def remote(chunk, step):
        place_outer, place_inner = outer_at[step // inner], inner_at[step % inner]
        target = place_outer * inner + place_inner
        if step < middle:
            at = pl.ds(0, rows)
        else:
            at = pl.ds(0, cut) if chunk == 0 else pl.ds(cut, rows - cut)
        return pltpu.make_async_remote_copy(
            src_ref=send_ref.at[target, at],
            dst_ref=recv_ref.at[mine, at],
            send_sem=send_sems.at[chunk, step],
            recv_sem=recv_sems.at[chunk, step],
            device_id=(place_outer, place_inner),
            device_id_type=pl.DeviceIdType.MESH,
        )

    across = range(devices - 1, middle - 1, -1)
    sequence = [(0, step) for step in across]
    for step in across:
        sequence.append((1, step))
        if step > middle:
            sequence.append((1, step - middle))

    def send(chunk):
        for at, step in sequence:
            if at == chunk:
                remote(at, step).start()

    lane = lax.broadcasted_iota(jnp.int32, (2 * lead, LANES), 1)
    groups = pulses * channels * MIG // LANES
    per_group = LANES // MIG
    pairs = channels // 2
    packs = [jnp.zeros((2 * lead, LANES), jnp.float32) for _ in range(groups)]
    for p in range(pulses):
        load_x[p].wait()
        if p == 0:
            load_first.wait()
        x = jnp.concatenate([x_ref[p * channels + c] for c in range(channels)], axis=1)
        y = dot_left(first_ref, x)
        if p == 0:
            load_twiddle.wait()
            load_fwd.wait()
            load_chirp.wait()
            load_inv.wait()
            tw_r = jnp.concatenate([twiddle_ref[0]] * channels, axis=0)
            tw_i = jnp.concatenate([twiddle_ref[1]] * channels, axis=0)
            chirp = jnp.concatenate(
                [chirp_ref[pl.ds(part, lead, stride=2), :] for part in range(2)], axis=0
            ).T
            top, bottom = chirp[:lead], chirp[lead:]
            left = lane[:lead] < lead
            chirp_r = jnp.where(left, top, pltpu.roll(bottom, lead, 1))
            chirp_i = jnp.where(left, pltpu.roll(top, lead, 1), bottom)
            chirp_r = jnp.concatenate([chirp_r] * channels, axis=0)
            chirp_i = jnp.concatenate([chirp_i] * channels, axis=0)
        y = jnp.concatenate([y[:, c * LANES : (c + 1) * LANES] for c in range(channels)], axis=0)
        y = y.reshape(channels, 2, lead, LANES)
        y_r = y[:, 0].reshape(channels * lead, LANES)
        y_i = y[:, 1].reshape(channels * lead, LANES)
        y = jnp.concatenate([y_r * tw_r - y_i * tw_i, y_r * tw_i + y_i * tw_r], axis=1)
        s = dot_right(y, fwd_ref)
        s_r, s_i = s[:, :LANES], s[:, LANES:]
        s = jnp.concatenate(
            [s_r * chirp_r + s_i * chirp_i, s_i * chirp_r - s_r * chirp_i], axis=1
        )
        t = dot_right(s, inv_ref)
        t_r, t_i = t[:, :LANES], t[:, LANES:]
        z_r = t_r * tw_r + t_i * tw_i
        z_i = t_i * tw_r - t_r * tw_i
        z = [
            jnp.concatenate(
                [z_r[c * lead : (c + 1) * lead], z_i[c * lead : (c + 1) * lead]], axis=0
            )
            for c in range(channels)
        ]
        stacked = jnp.concatenate(
            [jnp.concatenate([z[2 * k], z[2 * k + 1]], axis=0) for k in range(pairs)], axis=1
        )
        if p == 0:
            load_last.wait()
        w = dot_left(last_ref, stacked)
        for k in range(pairs):
            row = (p * pairs + k) * 8
            send_ref[:, row : row + 8, :] = w[:, k * LANES : (k + 1) * LANES].reshape(
                devices, 8, LANES
            )
        for c in range(channels):
            signal = p * channels + c
            g, where = signal // per_group, signal % per_group
            moved = z[c] if where == 0 else pltpu.roll(z[c], where * MIG, 1)
            packs[g] = jnp.where(lane // MIG == where, moved, packs[g])
        if p == 0:
            pl.semaphore_wait(barrier, devices - 1)
            send(0)
    load_halo.wait()
    w = dot_left(halo_ref, jnp.concatenate(packs, axis=1))
    row = lax.broadcasted_iota(jnp.int32, (devices * HALO_ROWS, LANES), 0) % HALO_ROWS
    total = w[:, :LANES]
    for g in range(1, groups):
        total = jnp.where(row // 2 == g, w[:, g * LANES : (g + 1) * LANES], total)
    send_ref[:, pulses * channels * 4 :, :] = total.reshape(devices, HALO_ROWS, LANES)
    send(1)
    own = pltpu.make_async_copy(send_ref.at[mine], recv_ref.at[mine], local_sem)
    own.start()

    load_reconstruction.wait()
    load_delays.wait()
    load_order.wait()
    bins_f = pulses * devices
    shape = (channels * channels, bins_f)
    row = lax.broadcasted_iota(jnp.int32, shape, 0) % channels
    frequency = doppler_of(lax.broadcasted_iota(jnp.int32, shape, 1))
    delay = jnp.zeros_like(row)
    for c in range(channels):
        one = jnp.broadcast_to(delays_ref[0:1, c : c + 1], row.shape)
        delay = jnp.where(row == c, one, delay)
    turns = lax.rem(frequency * delay, bins_f).astype(jnp.float32) * (1.0 / bins_f)
    align_r, align_i = cos_sin_turns(turns)
    rec_r = dot_exact(reconstruction_ref[0], order_ref[...])
    rec_i = dot_exact(reconstruction_ref[1], order_ref[...])
    mix_ref[0] = rec_r * align_r - rec_i * align_i
    mix_ref[1] = rec_r * align_i + rec_i * align_r

    load_rate.wait()
    load_band.wait()
    load_migration.wait()
    rows_ref[0] = spread_rows(rate_ref[...])
    rows_ref[1] = spread_rows(band_ref[...].astype(jnp.float32))
    rows_ref[2] = spread_rows(migration_ref[...].astype(jnp.float32))
    bins = rows_ref.shape[1]

    def tables(index, carry):
        at = pl.ds(pl.multiple_of(index * 8, 8), 8)
        rate = rows_ref[0, at, :]
        band = rows_ref[1, at, :].astype(jnp.int32)
        move = rows_ref[2, at, :].astype(jnp.int32)
        band_square = band * band
        square_ref[at, :] = band_square
        for start in range(0, length, LANES):
            doppler = doppler_of(lax.broadcasted_iota(jnp.int32, (8, LANES), 1)) + start
            centred = jnp.where(doppler >= length // 2, doppler - length, doppler)
            relative = centred.astype(jnp.float32) * (2.0 / length)
            cosine, sine = cos_sin_turns(rate * (relative * relative * (curvature / 2.0)))
            inside = jnp.abs(centred) < band
            columns = slice(start, start + LANES)
            cos_ref[at, columns] = jnp.where(inside, cosine, 0.0)
            sin_ref[at, columns] = jnp.where(inside, sine, 0.0)
            reach_ref[at, columns] = move * jnp.minimum(centred * centred, band_square) + (
                band_square >> 1
            )
        return carry

    lax.fori_loop(0, bins // 8, tables, 0)
    stores = []
    for source, target in (
        (cos_ref, cos_hbm),
        (sin_ref, sin_hbm),
        (reach_ref, reach_hbm),
        (square_ref, square_hbm),
        (mix_ref, mix_hbm),
    ):
        copy = pltpu.make_async_copy(source, target, store_sems.at[len(stores)])
        copy.start()
        stores.append(copy)
    for copy in stores:
        copy.wait()
    own.wait()

    for chunk, step in sequence:
        copy = remote(chunk, step)
        copy.wait_send()
        copy.wait_recv()


def azimuth_kernel(
    sizes,
    recv_hbm,
    doppler_hbm,
    halo_doppler_hbm,
    mix_hbm,
    reach_hbm,
    square_hbm,
    cos_hbm,
    sin_hbm,
    final_hbm,
    twiddle_hbm,
    out_hbm,
    recv_ref,
    doppler_ref,
    halo_doppler_ref,
    mix_ref,
    reach_ref,
    square_ref,
    cos_ref,
    sin_ref,
    final_ref,
    twiddle_ref,
    spectra,
    unfolded,
    focused,
    image_ref,
    load_sems,
    recv_sems,
    store_sems,
):
    sources, local_pulses, channels, bins = sizes
    block = local_pulses * channels * 4 + HALO_ROWS
    arrivals = []

    def arrive(row):
        at = pl.ds(row, 8)
        copy = pltpu.make_async_copy(
            recv_hbm.at[:, at], recv_ref.at[:, at], recv_sems.at[len(arrivals)]
        )
        copy.start()
        arrivals.append(copy)

    loads = []

    def load(source, target):
        copy = pltpu.make_async_copy(source, target, load_sems.at[len(loads)])
        copy.start()
        loads.append(copy)
        return copy

    load_doppler = load(doppler_hbm, doppler_ref)
    for pair in range(channels // 2):
        for p in range(local_pulses):
            arrive((p * (channels // 2) + pair) * 8)
    arrive(local_pulses * channels * 4)
    load_halo_doppler = load(halo_doppler_hbm, halo_doppler_ref)
    load_mix = load(mix_hbm, mix_ref)
    load_tables = [
        load(reach_hbm, reach_ref),
        load(square_hbm, square_ref),
        load(cos_hbm, cos_ref),
        load(sin_hbm, sin_ref),
    ]
    load_final = [load(final_hbm, final_ref), load(twiddle_hbm, twiddle_ref)]

    flat = recv_ref.reshape(sources * block, LANES)

    def rows_of(start):
        return flat[pl.ds(start, sources, stride=block), :]

    load_doppler.wait()
    for c in range(channels):
        if c % 2 == 0:
            for p in range(local_pulses):
                arrivals[c // 2 * local_pulses + p].wait()
        for half in range(bins // LANES):
            z = jnp.concatenate(
                [
                    rows_of(p * channels * 4 + c * 4 + part * 2 + half)
                    for part in range(2)
                    for p in range(local_pulses)
                ],
                axis=0,
            )
            spectra[c, half * LANES : (half + 1) * LANES, :] = dot_right(z.T, doppler_ref)
    groups = local_pulses * channels * MIG // LANES
    per_group = LANES // (MIG * channels)
    arrivals[-1].wait()
    load_halo_doppler.wait()
    h = jnp.concatenate(
        [rows_of(local_pulses * channels * 4 + j) for j in range(2 * groups)], axis=0
    ).T
    step = channels * MIG
    halo = dot_right(h[:step], halo_doppler_ref.at[0])
    for k in range(1, per_group):
        halo = halo + dot_right(h[k * step : (k + 1) * step], halo_doppler_ref.at[k])
    for c in range(channels):
        spectra[c, bins:, :] = halo[c * MIG : (c + 1) * MIG]
    load_mix.wait()
    mix_channels(spectra, mix_ref, unfolded, bins + MIG, 0)
    for copy in load_tables:
        copy.wait()
    migrate_rows(unfolded, cos_ref, sin_ref, reach_ref, square_ref, focused, bins)
    for copy in load_final:
        copy.wait()
    stores = []
    for k in range(bins // LANES):
        at = slice(k * LANES, (k + 1) * LANES)
        real, imag = inverse_rows(focused, final_ref, twiddle_ref, at)
        image_ref[0, at, :] = real
        image_ref[1, at, :] = imag
        rows = pl.ds(k * LANES, LANES)
        copy = pltpu.make_async_copy(
            image_ref.at[:, rows], out_hbm.at[:, rows], store_sems.at[k]
        )
        copy.start()
        stores.append(copy)
    for copy in stores:
        copy.wait()


def fits(pulses, channels, length, devices):
    local_pulses = pulses // devices
    signals = local_pulses * channels
    bins = length // devices
    lead = length // LANES
    return (
        pulses == LANES
        and length % (LANES * devices) == 0
        and bins == 2 * LANES
        and channels == 4
        and 2 * lead == LANES
        and devices % 8 == 0
        and devices & (devices - 1) == 0
        and signals * MIG % LANES == 0
        and LANES % (MIG * channels) == 0
        and 2 * (signals * MIG // LANES) <= HALO_ROWS
        and channels * pulses <= 512
    )


def hbm():
    return pl.BlockSpec(memory_space=pltpu.HBM)


def vmem():
    return pl.BlockSpec(memory_space=pltpu.VMEM)


def blocked_local(
    raw_echoes, chirp_spectrum, reconstruction, delays, azimuth_rate, band_halfwidth, migration
):
    local_pulses, channels, _, length = raw_echoes.shape
    inner = lax.axis_size("rg")
    devices = lax.axis_size("az") * inner
    bins = length // devices
    lead = length // LANES
    pulses = local_pulses * devices
    signals = local_pulses * channels
    doppler_bins = channels * pulses
    leads = np.arange(lead)
    lanes = np.arange(LANES)

    first = left_matrix(*roots(leads, leads, lead, -1.0))
    first = first.transpose(0, 1, 3, 2).reshape(2 * lead, 2 * lead)
    turned = np.concatenate([lanes[0::2], lanes[1::2]])
    forward = right_matrix(*roots(lanes, turned, LANES, -1.0)).reshape(2 * LANES, 2 * LANES)
    inverse = right_matrix(*roots(turned, lanes, LANES, 1.0)).reshape(2 * LANES, 2 * LANES)
    last = left_matrix(*roots(leads, leads, lead, 1.0)) / length
    pair = np.zeros((devices, 2, 2, 2, 2, 2 * lead))
    by_device = last.reshape(2, devices, 2, 2 * lead).transpose(1, 0, 2, 3)
    for s in range(2):
        pair[:, s, :, :, s, :] = by_device
    pair = pair.reshape(devices * 8, 4 * lead)
    halo = np.zeros((devices, HALO_ROWS, 2 * lead))
    groups = signals * MIG // LANES
    for g in range(groups):
        halo[:-1, 2 * g : 2 * g + 2] = by_device[1:, :, 0]
    halo = halo.reshape(devices * HALO_ROWS, 2 * lead)
    twiddles = np.stack(roots(leads, lanes, length, -1.0)).astype(np.float32)

    sources = np.arange(devices)
    bins_f = doppler_of(np.arange(pulses))
    order_f = (np.arange(pulses)[:, None] == bins_f[None, :]).astype(ml_dtypes.bfloat16)
    order = (np.arange(local_pulses)[:, None] + sources[None, :] * local_pulses).reshape(-1)
    scale = 1.0 / math.sqrt(pulses)
    to_doppler = right_matrix(*roots(order, bins_f, pulses, -1.0)) * scale
    to_doppler = to_doppler.reshape(2 * pulses, 2 * pulses)
    per_group = local_pulses // groups
    halo_doppler = []
    for k in range(per_group):
        by_group = []
        for g in range(groups):
            at = sources * local_pulses + g * per_group + k
            by_group.append(
                (right_matrix(*roots(at, bins_f, pulses, -1.0)) * scale).reshape(
                    2 * devices, 2 * pulses
                )
            )
        halo_doppler.append(split_constant(np.concatenate(by_group, axis=0)))
    halo_doppler = np.stack(halo_doppler)
    final = right_matrix(*roots(lanes, lanes, LANES, 1.0)) / math.sqrt(doppler_bins)
    final = split_constant(final.reshape(2 * LANES, 2 * LANES))
    regroup = np.stack(roots(np.arange(8) % 4, lanes, doppler_bins, 1.0)).astype(np.float32)

    x = raw_echoes.reshape(signals, 2, lead, LANES).transpose(0, 2, 1, 3)
    x = x.reshape(signals, 2 * lead, LANES)
    chirp = chirp_spectrum.reshape(2, lead, LANES).transpose(1, 0, 2).reshape(2 * lead, LANES)
    block = signals * 4 + HALO_ROWS
    tables = (bins, doppler_bins)
    by_lane = (bins // LANES, LANES)
    operands = (
        x,
        chirp,
        azimuth_rate.reshape(by_lane),
        band_halfwidth.reshape(by_lane),
        migration.reshape(by_lane),
        split_constant(first),
        twiddles,
        split_constant(forward),
        split_constant(inverse),
        split_constant(pair),
        split_constant(halo),
        reconstruction.reshape(2, channels * channels, pulses),
        delays.reshape(1, channels),
        order_f,
    )
    received, cosine, sine, reach, square, mix = pl.pallas_call(
        functools.partial(
            compress_kernel, (local_pulses, channels, lead, devices, inner, doppler_bins)
        ),
        out_shape=(
            jax.ShapeDtypeStruct((devices, block, LANES), jnp.float32),
            jax.ShapeDtypeStruct(tables, jnp.float32),
            jax.ShapeDtypeStruct(tables, jnp.float32),
            jax.ShapeDtypeStruct(tables, jnp.int32),
            jax.ShapeDtypeStruct((bins, LANES), jnp.int32),
            jax.ShapeDtypeStruct((2, channels * channels, pulses), jnp.float32),
        ),
        in_specs=[hbm()] * len(operands),
        out_specs=(hbm(),) * 6,
        scratch_shapes=[pltpu.VMEM(value.shape, value.dtype) for value in operands]
        + [
            pltpu.VMEM((devices, block, LANES), jnp.float32),
            pltpu.VMEM((3, bins, LANES), jnp.float32),
            pltpu.VMEM(tables, jnp.float32),
            pltpu.VMEM(tables, jnp.float32),
            pltpu.VMEM(tables, jnp.int32),
            pltpu.VMEM((bins, LANES), jnp.int32),
            pltpu.VMEM((2, channels * channels, pulses), jnp.float32),
            pltpu.SemaphoreType.DMA((len(operands) + local_pulses - 1,)),
            pltpu.SemaphoreType.DMA((5,)),
            pltpu.SemaphoreType.DMA,
            pltpu.SemaphoreType.DMA((2, devices)),
            pltpu.SemaphoreType.DMA((2, devices)),
        ],
        compiler_params=pltpu.CompilerParams(
            collective_id=0, has_side_effects=True, vmem_limit_bytes=KERNEL_VMEM
        ),
        name="compress_exchange",
    )(*operands)
    inputs = (
        received,
        split_constant(to_doppler),
        halo_doppler,
        mix,
        reach,
        square,
        cosine,
        sine,
        final,
        regroup,
    )
    return pl.pallas_call(
        functools.partial(azimuth_kernel, (devices, local_pulses, channels, bins)),
        out_shape=jax.ShapeDtypeStruct((2, bins, doppler_bins), jnp.float32),
        in_specs=[hbm()] * len(inputs),
        out_specs=hbm(),
        scratch_shapes=[pltpu.VMEM(value.shape, value.dtype) for value in inputs]
        + [
            pltpu.VMEM((channels, bins + MIG, 2 * pulses), jnp.float32),
            pltpu.VMEM((bins + MIG, 2 * doppler_bins), jnp.float32),
            pltpu.VMEM((bins, 2 * doppler_bins), jnp.float32),
            pltpu.VMEM((2, bins, doppler_bins), jnp.float32),
            pltpu.SemaphoreType.DMA((len(inputs) - 1,)),
            pltpu.SemaphoreType.DMA((channels // 2 * local_pulses + 1,)),
            pltpu.SemaphoreType.DMA((bins // LANES,)),
        ],
        compiler_params=pltpu.CompilerParams(vmem_limit_bytes=KERNEL_VMEM),
        name="azimuth_focus",
    )(*inputs)


def local(raw_echoes, chirp_spectrum, reconstruction, *rest):
    local_pulses, channels, _, length = raw_echoes.shape
    devices = lax.axis_size("az") * lax.axis_size("rg")
    if fits(local_pulses * devices, channels, length, devices):
        return blocked_local(raw_echoes, chirp_spectrum, reconstruction, *rest)
    return plain_local(raw_echoes, chirp_spectrum, reconstruction, *rest)


def solution(mesh):
    in_specs = (
        P(("az", "rg"), None, None, None),
        P(),
        P(),
        P(),
        P(("az", "rg")),
        P(("az", "rg")),
        P(("az", "rg")),
    )
    out_specs = P(None, ("az", "rg"), None)
    return jax.shard_map(local, mesh=mesh, in_specs=in_specs, out_specs=out_specs, check_vma=False)
```

```python
import functools
import math

import jax
import jax.numpy as jnp
import ml_dtypes
import numpy as np
from jax import lax
from jax.experimental import pallas as pl
from jax.experimental.pallas import tpu as pltpu
from jax.sharding import PartitionSpec as P

MIG = 16
LANES = 128
HALO_ROWS = 8
KERNEL_VMEM = 62 * 1024 * 1024


highest = lax.Precision.HIGHEST
curvature = 32.0


def passed_along(value, axis, by):
    size = lax.axis_size(axis)
    pairs = [(i, i + by) for i in range(size) if 0 <= i + by < size]
    return lax.ppermute(value, axis, pairs)


def factor_pair(length):
    largest = 1
    for candidate in range(1, length + 1):
        if candidate * candidate > length:
            break
        if length % candidate == 0:
            largest = candidate
    return (largest, length // largest)


def dft_matrix(length, direction):
    indices = jnp.arange(length, dtype=jnp.int32)
    angles = (
        2.0 * math.pi / length * (indices[:, None] * indices[None, :] % length).astype(jnp.float32)
    )
    cosine = jnp.cos(angles)
    sines = direction * jnp.sin(angles)
    return jnp.stack(
        [jnp.stack([cosine, -sines], axis=1), jnp.stack([sines, cosine], axis=1)], axis=0
    )


def twiddle(lead_size, trail_size, length, direction):
    lead_index = jnp.arange(lead_size, dtype=jnp.int32)
    trail_index = jnp.arange(trail_size, dtype=jnp.int32)
    angles = (
        2.0
        * math.pi
        / length
        * (lead_index[:, None] * trail_index[None, :] % length).astype(jnp.float32)
    )
    return (jnp.cos(angles), direction * jnp.sin(angles))


def complex_mul(values, factor_real, factor_imag, part_axis):
    real_part = lax.index_in_dim(values, 0, part_axis, keepdims=True)
    imag_part = lax.index_in_dim(values, 1, part_axis, keepdims=True)
    return jnp.concatenate(
        [
            real_part * factor_real - imag_part * factor_imag,
            real_part * factor_imag + imag_part * factor_real,
        ],
        axis=part_axis,
    )


def range_focus(raw_echoes, chirp_spectrum):
    local_pulses, channels, _, length = raw_echoes.shape
    lead_size, trail_size = factor_pair(length)
    layout = raw_echoes.reshape(local_pulses, channels, 2, lead_size, trail_size)
    sectioned = jnp.einsum(
        "okci,pqcij->pqokj", dft_matrix(lead_size, -1.0), layout, precision=highest
    )
    twiddle_real, twiddle_imag = twiddle(lead_size, trail_size, length, -1.0)
    sectioned = complex_mul(sectioned, twiddle_real, twiddle_imag, 2)
    spectrum = jnp.einsum(
        "olcj,pqckj->pqolk", dft_matrix(trail_size, -1.0), sectioned, precision=highest
    )
    spectrum = spectrum.reshape(local_pulses, channels, 2, length)
    spectrum = complex_mul(spectrum, chirp_spectrum[0], -chirp_spectrum[1], 2)
    layout = spectrum.reshape(local_pulses, channels, 2, lead_size, trail_size)
    sectioned = jnp.einsum(
        "okci,pqcij->pqokj", dft_matrix(lead_size, 1.0), layout, precision=highest
    )
    twiddle_real, twiddle_imag = twiddle(lead_size, trail_size, length, 1.0)
    sectioned = complex_mul(sectioned, twiddle_real, twiddle_imag, 2)
    restored = jnp.einsum(
        "olcj,pqckj->qoplk", dft_matrix(trail_size, 1.0), sectioned, precision=highest
    )
    return restored.reshape(channels, 2, local_pulses, length) / length


def reconstruct(turned, mixing_real, mixing_imag):
    channels, _, local_pulses, blocks, bin_count = turned.shape
    pulse_total = blocks * local_pulses
    sectioned = jnp.einsum("okcm,qcimb->qobik", dft_matrix(blocks, -1.0), turned, precision=highest)
    twiddle_real, twiddle_imag = twiddle(local_pulses, blocks, pulse_total, -1.0)
    sectioned = complex_mul(sectioned, twiddle_real, twiddle_imag, 1)
    spectrum = jnp.einsum(
        "olci,qcbik->qoblk", dft_matrix(local_pulses, -1.0), sectioned, precision=highest
    )
    spectrum = spectrum.reshape(channels, 2, bin_count, pulse_total) / math.sqrt(pulse_total)
    spec_real = spectrum[:, 0]
    spec_imag = spectrum[:, 1]
    unfolded_real = jnp.einsum(
        "bcf,crf->rbf", mixing_real, spec_real, precision=highest
    ) - jnp.einsum("bcf,crf->rbf", mixing_imag, spec_imag, precision=highest)
    unfolded_imag = jnp.einsum(
        "bcf,crf->rbf", mixing_real, spec_imag, precision=highest
    ) + jnp.einsum("bcf,crf->rbf", mixing_imag, spec_real, precision=highest)
    unfolded = jnp.stack([unfolded_real, unfolded_imag], axis=0)
    return unfolded.reshape(2, bin_count, channels * pulse_total)


def azimuth_focus(unfolded, azimuth_rate, band_halfwidth, migration):
    bin_count = azimuth_rate.shape[0]
    length = unfolded.shape[2]
    doppler_index = jnp.arange(length, dtype=jnp.int32)
    centred = doppler_index - length * (doppler_index >= length // 2).astype(jnp.int32)
    band_square = band_halfwidth * band_halfwidth
    squared = jnp.minimum((centred * centred)[None, :], band_square[:, None])
    migration_shift = (migration[:, None] * squared + (band_square // 2)[:, None]) // band_square[
        :, None
    ]
    migrated = jnp.zeros((2, bin_count, length), jnp.float32)
    for offset in range(MIG + 1):
        window = unfolded[:, offset : offset + bin_count, :]
        migrated = jnp.where((migration_shift == offset)[None], window, migrated)
    relative = centred.astype(jnp.float32) / (length // 2)
    matched_phase = math.pi * curvature * azimuth_rate[:, None] * (relative * relative)[None, :]
    focused = complex_mul(migrated, jnp.cos(matched_phase), jnp.sin(matched_phase), 0)
    inside = jnp.abs(centred)[None, :] < band_halfwidth[:, None]
    focused = jnp.where(inside[None], focused, 0.0)
    lead_size, trail_size = factor_pair(length)
    layout = focused.reshape(2, bin_count, lead_size, trail_size)
    sectioned = jnp.einsum("okci,cbij->obkj", dft_matrix(lead_size, 1.0), layout, precision=highest)
    twiddle_real, twiddle_imag = twiddle(lead_size, trail_size, length, 1.0)
    sectioned = complex_mul(sectioned, twiddle_real, twiddle_imag, 0)
    focused_image = jnp.einsum(
        "olcj,cbkj->oblk", dft_matrix(trail_size, 1.0), sectioned, precision=highest
    )
    return focused_image.reshape(2, bin_count, length) / math.sqrt(length)


def plain_local(
    raw_echoes, chirp_spectrum, reconstruction, delays, azimuth_rate, band_halfwidth, migration
):
    compressed = range_focus(raw_echoes, chirp_spectrum)
    channels, _, local_pulses, length = compressed.shape
    azimuth_count = lax.axis_size("az")
    range_count = lax.axis_size("rg")
    bin_count = length // (azimuth_count * range_count)
    layout = compressed.reshape(channels, 2, local_pulses, azimuth_count, range_count, bin_count)
    layout = lax.all_to_all(layout, "rg", split_axis=4, concat_axis=4, tiled=True)
    layout = lax.all_to_all(layout, "az", split_axis=3, concat_axis=3, tiled=True)
    turned = layout.reshape(channels, 2, local_pulses, azimuth_count * range_count, bin_count)
    pulse_total = azimuth_count * range_count * local_pulses
    frequency = jnp.arange(pulse_total, dtype=jnp.int32)
    angles = (
        2.0
        * math.pi
        / pulse_total
        * (frequency[None, :] * delays[:, None] % pulse_total).astype(jnp.float32)
    )
    align_real = jnp.cos(angles)[None]
    align_imag = jnp.sin(angles)[None]
    mixing_real = reconstruction[0] * align_real - reconstruction[1] * align_imag
    mixing_imag = reconstruction[0] * align_imag + reconstruction[1] * align_real
    unfolded = reconstruct(turned, mixing_real, mixing_imag)
    margin_bins = passed_along(unfolded[:, :MIG, :], ("az", "rg"), -1)
    unfolded = jnp.concatenate([unfolded, margin_bins], axis=1)
    return azimuth_focus(unfolded, azimuth_rate, band_halfwidth, migration)


def split_constant(values):
    high = values.astype(ml_dtypes.bfloat16)
    low = (values - high.astype(np.float64)).astype(ml_dtypes.bfloat16)
    return np.stack([high, low])


def roots(rows, columns, length, direction):
    turns = (rows[:, None] * columns[None, :]) % length
    angles = 2.0 * np.pi / length * turns
    return np.cos(angles), direction * np.sin(angles)


def left_matrix(cosine, sine):
    return np.stack([np.stack([cosine, -sine], 1), np.stack([sine, cosine], 1)], 0)


def right_matrix(cosine, sine):
    return np.stack([np.stack([cosine, sine], 1), np.stack([-sine, cosine], 1)], 0)


def split(values):
    high = values.astype(jnp.bfloat16)
    low = (values - high.astype(jnp.float32)).astype(jnp.bfloat16)
    return high, low


def dot(a, b):
    return jnp.dot(a, b, preferred_element_type=jnp.float32)


def dot_right(values, matrix):
    high, low = split(values)
    return dot(high, matrix[0]) + (dot(low, matrix[0]) + dot(high, matrix[1]))


def dot_left(matrix, values):
    high, low = split(values)
    return dot(matrix[0], high) + (dot(matrix[1], high) + dot(matrix[0], low))


def cos_sin_turns(turns):
    quarter = jnp.floor(turns * 4.0 + 0.5)
    theta = (turns - quarter * 0.25) * (2.0 * math.pi)
    square = theta * theta
    cosine = 1.0 + square * (
        -0.5 + square * (1.0 / 24 + square * (-1.0 / 720 + square * (1.0 / 40320)))
    )
    sine = theta * (
        1.0
        + square
        * (-1.0 / 6 + square * (1.0 / 120 + square * (-1.0 / 5040 + square * (1.0 / 362880))))
    )
    index = quarter.astype(jnp.int32)
    odd = (index & 1) == 1
    cos_negative = ((index + 1) & 2) == 2
    sin_negative = (index & 2) == 2
    cos_size = jnp.where(odd, sine, cosine)
    sin_size = jnp.where(odd, cosine, sine)
    return (
        jnp.where(cos_negative, -cos_size, cos_size),
        jnp.where(sin_negative, -sin_size, sin_size),
    )


def spread_rows(values):
    return jnp.concatenate(
        [
            jnp.broadcast_to(values[h : h + 1, :], (LANES, LANES)).T
            for h in range(values.shape[0])
        ],
        axis=0,
    )


def dot_exact(values, matrix):
    high = values.astype(jnp.bfloat16)
    rest = values - high.astype(jnp.float32)
    middle = rest.astype(jnp.bfloat16)
    low = (rest - middle.astype(jnp.float32)).astype(jnp.bfloat16)
    return dot(high, matrix) + dot(middle, matrix) + dot(low, matrix)


def doppler_of(lane):
    return (lane % (LANES // 4)) * 4 + lane // (LANES // 4)


def mix_channels(spectra, mix, unfolded, rows, shift):
    channels = spectra.shape[0]
    pulses = spectra.shape[2] // 2
    length = channels * pulses

    def mix_rows(index, carry):
        at = pl.ds(pl.multiple_of(index * 16, 16), 16)
        to = pl.ds(pl.multiple_of(index * 16 + shift, 8), 16)
        spec = [spectra[c, at, :] for c in range(channels)]
        for b in range(channels):
            total_r = total_i = None
            for c in range(channels):
                m = b * channels + c
                m_r, m_i = mix[0, m : m + 1, :], mix[1, m : m + 1, :]
                d_r, d_i = spec[c][:, :pulses], spec[c][:, pulses:]
                r = m_r * d_r - m_i * d_i
                i = m_r * d_i + m_i * d_r
                total_r = r if c == 0 else total_r + r
                total_i = i if c == 0 else total_i + i
            unfolded[to, b * pulses : (b + 1) * pulses] = total_r
            unfolded[to, length + b * pulses : length + (b + 1) * pulses] = total_i
        return carry

    lax.fori_loop(0, rows // 16, mix_rows, 0)


def migrate_rows(unfolded, cos_ref, sin_ref, shift_ref, focused, rows):
    length = shift_ref.shape[1]

    def focus_band(b, carry):
        lane = pl.multiple_of(b * LANES, LANES)
        columns = (pl.ds(lane, LANES), pl.ds(pl.multiple_of(length + lane, LANES), LANES))

        def windows(start):
            return [
                [unfolded[start + k : start + k + 8, column] for k in range(8)]
                for column in columns
            ]

        ahead = windows(0)
        for start in range(0, rows, 8):
            at = slice(start, start + 8)
            now, ahead = ahead, windows(start + 8)
            shift = shift_ref[at, columns[0]]
            bits = [(shift & (1 << level)) != 0 for level in range(5)]
            values = []
            for part, column in enumerate(columns):
                level_values = now[part] + ahead[part]
                for level in range(4):
                    level_values = [
                        jnp.where(bits[level], level_values[k + 1], level_values[k])
                        for k in range(0, len(level_values), 2)
                    ]
                last = unfolded[start + MIG : start + MIG + 8, column]
                values.append(jnp.where(bits[4], last, level_values[0]))
            real, imag = values
            cosine = cos_ref[at, columns[0]]
            sine = sin_ref[at, columns[0]]
            focused[at, columns[0]] = real * cosine - imag * sine
            focused[at, columns[1]] = real * sine + imag * cosine
        return carry

    lax.fori_loop(0, length // LANES, focus_band, 0)


def inverse_rows(focused, final_ref, twiddle_ref, at):
    group = LANES // 4
    rows = at.stop - at.start
    line = lax.broadcasted_iota(jnp.int32, (rows, LANES), 1) // group
    parts = []
    for part in range(2):
        base = part * 4 * LANES
        turned = []
        for b in range(4):
            value = focused[at, base + b * LANES : base + (b + 1) * LANES]
            turned.append(value if b == 0 else pltpu.roll(value, b * group, 1))
        grouped = []
        for j in range(4):
            value = turned[(0 - j) % 4]
            for g in range(1, 4):
                value = jnp.where(line == g, turned[(g - j) % 4], value)
            grouped.append(value if j == 0 else pltpu.roll(value, LANES - j * group, 1))
        parts.append(grouped)
    stacked = jnp.concatenate(
        [jnp.concatenate([parts[0][j], parts[1][j]], axis=1) for j in range(4)], axis=0
    )
    image = dot_right(stacked, final_ref)
    real, imag = [], []
    for j in range(4):
        r = image[j * rows : (j + 1) * rows, :LANES]
        i = image[j * rows : (j + 1) * rows, LANES:]
        if j > 0:
            t_r, t_i = twiddle_ref[0, j : j + 1, :], twiddle_ref[1, j : j + 1, :]
            r, i = r * t_r - i * t_i, r * t_i + i * t_r
        real.append(r)
        imag.append(i)
    a_r, a_i = real[0] + real[2], imag[0] + imag[2]
    b_r, b_i = real[0] - real[2], imag[0] - imag[2]
    c_r, c_i = real[1] + real[3], imag[1] + imag[3]
    d_r, d_i = imag[3] - imag[1], real[1] - real[3]
    return (
        jnp.concatenate([a_r + c_r, b_r + d_r, a_r - c_r, b_r - d_r], axis=1),
        jnp.concatenate([a_i + c_i, b_i + d_i, a_i - c_i, b_i - d_i], axis=1),
    )


def compress_kernel(
    sizes,
    x_hbm,
    chirp_hbm,
    rate_hbm,
    band_hbm,
    migration_hbm,
    first_hbm,
    twiddle_hbm,
    fwd_hbm,
    inv_hbm,
    last_hbm,
    halo_hbm,
    reconstruction_hbm,
    delays_hbm,
    order_hbm,
    recv_ref,
    halo_recv_ref,
    cos_hbm,
    sin_hbm,
    shift_hbm,
    mix_hbm,
    x_ref,
    chirp_ref,
    rate_ref,
    band_ref,
    migration_ref,
    first_ref,
    twiddle_ref,
    fwd_ref,
    inv_ref,
    last_ref,
    halo_ref,
    reconstruction_ref,
    delays_ref,
    order_ref,
    send_ref,
    send_halo_ref,
    rows_ref,
    cos_ref,
    sin_ref,
    shift_ref,
    mix_ref,
    load_sems,
    store_sems,
    local_sems,
    send_sems,
    recv_sems,
):
    pulses, channels, lead, devices, inner, length = sizes
    mine = lax.axis_index("az") * inner + lax.axis_index("rg")
    barrier = pltpu.get_barrier_semaphore()

    def place(index):
        return (lax.div(index, inner), lax.rem(index, inner))

    def greet(k, carry):
        pl.semaphore_signal(
            barrier,
            inc=1,
            device_id=place(lax.rem(mine + k, devices)),
            device_id_type=pl.DeviceIdType.MESH,
        )
        return carry

    loads = []

    def start_load(source, target):
        copy = pltpu.make_async_copy(source, target, load_sems.at[len(loads)])
        copy.start()
        loads.append(copy)
        return copy

    def pulse_load(p):
        at = pl.ds(p * channels, channels)
        return start_load(x_hbm.at[at], x_ref.at[at])

    load_x = [pulse_load(0)]
    load_first = start_load(first_hbm, first_ref)
    load_twiddle = start_load(twiddle_hbm, twiddle_ref)
    load_fwd = start_load(fwd_hbm, fwd_ref)
    load_chirp = start_load(chirp_hbm, chirp_ref)
    load_inv = start_load(inv_hbm, inv_ref)
    load_last = start_load(last_hbm, last_ref)
    load_x += [pulse_load(p) for p in range(1, pulses)]
    load_halo = start_load(halo_hbm, halo_ref)
    load_rate = start_load(rate_hbm, rate_ref)
    load_band = start_load(band_hbm, band_ref)
    load_migration = start_load(migration_hbm, migration_ref)
    load_reconstruction = start_load(reconstruction_hbm, reconstruction_ref)
    load_delays = start_load(delays_hbm, delays_ref)
    load_order = start_load(order_hbm, order_ref)
    lax.fori_loop(1, devices, greet, 0)

    rows = pulses * channels * 4
    cut = channels * 4

    def parts(chunk, target):
        if chunk == 2:
            return send_halo_ref.at[target], halo_recv_ref.at[mine]
        at = pl.ds(0, cut) if chunk == 0 else pl.ds(cut, rows - cut)
        return send_ref.at[target, at], recv_ref.at[mine, at]

    def remote(chunk, i):
        far = lax.div(i + 1, 2)
        step = devices // 2 + far - 2 * far * lax.rem(i, 2)
        target = lax.rem(mine + step, devices)
        source, landing = parts(chunk, target)
        return pltpu.make_async_remote_copy(
            src_ref=source,
            dst_ref=landing,
            send_sem=send_sems.at[chunk, step],
            recv_sem=recv_sems.at[chunk, step],
            device_id=place(target),
            device_id_type=pl.DeviceIdType.MESH,
        )

    def send(chunk):
        def body(i, carry):
            remote(chunk, i).start()
            return carry

        lax.fori_loop(0, devices - 1, body, 0)

    lane = lax.broadcasted_iota(jnp.int32, (2 * lead, LANES), 1)
    groups = pulses * channels * MIG // LANES
    per_group = LANES // MIG
    pairs = channels // 2
    packs = [jnp.zeros((2 * lead, LANES), jnp.float32) for _ in range(groups)]
    for p in range(pulses):
        load_x[p].wait()
        if p == 0:
            load_first.wait()
        x = jnp.concatenate([x_ref[p * channels + c] for c in range(channels)], axis=1)
        y = dot_left(first_ref, x)
        if p == 0:
            load_twiddle.wait()
            load_fwd.wait()
            load_chirp.wait()
            load_inv.wait()
            tw_r = jnp.concatenate([twiddle_ref[0]] * channels, axis=0)
            tw_i = jnp.concatenate([twiddle_ref[1]] * channels, axis=0)
            chirp = jnp.concatenate(
                [chirp_ref[pl.ds(part, lead, stride=2), :] for part in range(2)], axis=0
            ).T
            top, bottom = chirp[:lead], chirp[lead:]
            left = lane[:lead] < lead
            chirp_r = jnp.where(left, top, pltpu.roll(bottom, lead, 1))
            chirp_i = jnp.where(left, pltpu.roll(top, lead, 1), bottom)
            chirp_r = jnp.concatenate([chirp_r] * channels, axis=0)
            chirp_i = jnp.concatenate([chirp_i] * channels, axis=0)
        y = jnp.concatenate([y[:, c * LANES : (c + 1) * LANES] for c in range(channels)], axis=0)
        y = y.reshape(channels, 2, lead, LANES)
        y_r = y[:, 0].reshape(channels * lead, LANES)
        y_i = y[:, 1].reshape(channels * lead, LANES)
        y = jnp.concatenate([y_r * tw_r - y_i * tw_i, y_r * tw_i + y_i * tw_r], axis=1)
        s = dot_right(y, fwd_ref)
        s_r, s_i = s[:, :LANES], s[:, LANES:]
        s = jnp.concatenate(
            [s_r * chirp_r + s_i * chirp_i, s_i * chirp_r - s_r * chirp_i], axis=1
        )
        t = dot_right(s, inv_ref)
        t_r, t_i = t[:, :LANES], t[:, LANES:]
        z_r = t_r * tw_r + t_i * tw_i
        z_i = t_i * tw_r - t_r * tw_i
        z = [
            jnp.concatenate(
                [z_r[c * lead : (c + 1) * lead], z_i[c * lead : (c + 1) * lead]], axis=0
            )
            for c in range(channels)
        ]
        stacked = jnp.concatenate(
            [jnp.concatenate([z[2 * k], z[2 * k + 1]], axis=0) for k in range(pairs)], axis=1
        )
        if p == 0:
            load_last.wait()
        w = dot_left(last_ref, stacked)
        for k in range(pairs):
            row = (p * pairs + k) * 8
            send_ref[:, row : row + 8, :] = w[:, k * LANES : (k + 1) * LANES].reshape(
                devices, 8, LANES
            )
        for c in range(channels):
            signal = p * channels + c
            g, where = signal // per_group, signal % per_group
            moved = z[c] if where == 0 else pltpu.roll(z[c], where * MIG, 1)
            packs[g] = jnp.where(lane // MIG == where, moved, packs[g])
        if p == 0:
            pl.semaphore_wait(barrier, devices - 1)
            send(0)
    send(1)
    load_halo.wait()
    w = dot_left(halo_ref, jnp.concatenate(packs, axis=1))
    row = lax.broadcasted_iota(jnp.int32, (devices * HALO_ROWS, LANES), 0) % HALO_ROWS
    total = w[:, :LANES]
    for g in range(1, groups):
        total = jnp.where(row // 2 == g, w[:, g * LANES : (g + 1) * LANES], total)
    send_halo_ref[...] = total.reshape(devices, HALO_ROWS, LANES)[:, : 2 * groups, :]
    send(2)
    own = [
        pltpu.make_async_copy(send_ref.at[mine], recv_ref.at[mine], local_sems.at[0]),
        pltpu.make_async_copy(send_halo_ref.at[mine], halo_recv_ref.at[mine], local_sems.at[1]),
    ]
    for copy in own:
        copy.start()

    load_reconstruction.wait()
    load_delays.wait()
    load_order.wait()
    bins_f = pulses * devices
    shape = (channels * channels, bins_f)
    row = lax.broadcasted_iota(jnp.int32, shape, 0) % channels
    frequency = doppler_of(lax.broadcasted_iota(jnp.int32, shape, 1))
    delay = jnp.zeros_like(row)
    for c in range(channels):
        one = jnp.broadcast_to(delays_ref[0:1, c : c + 1], row.shape)
        delay = jnp.where(row == c, one, delay)
    turns = lax.rem(frequency * delay, bins_f).astype(jnp.float32) * (1.0 / bins_f)
    align_r, align_i = cos_sin_turns(turns)
    rec_r = dot_exact(reconstruction_ref[0], order_ref[...])
    rec_i = dot_exact(reconstruction_ref[1], order_ref[...])
    mix_ref[0] = rec_r * align_r - rec_i * align_i
    mix_ref[1] = rec_r * align_i + rec_i * align_r

    load_rate.wait()
    load_band.wait()
    load_migration.wait()
    rows_ref[0] = spread_rows(rate_ref[...])
    rows_ref[1] = spread_rows(band_ref[...].astype(jnp.float32))
    rows_ref[2] = spread_rows(migration_ref[...].astype(jnp.float32))
    bins = rows_ref.shape[1]

    def tables(index, carry):
        at = pl.ds(pl.multiple_of(index * 8, 8), 8)
        rate = rows_ref[0, at, :]
        band = rows_ref[1, at, :].astype(jnp.int32)
        move = rows_ref[2, at, :].astype(jnp.int32)
        band_square = band * band
        for start in range(0, length, LANES):
            doppler = doppler_of(lax.broadcasted_iota(jnp.int32, (8, LANES), 1)) + start
            centred = jnp.where(doppler >= length // 2, doppler - length, doppler)
            relative = centred.astype(jnp.float32) * (2.0 / length)
            cosine, sine = cos_sin_turns(rate * (relative * relative * (curvature / 2.0)))
            inside = jnp.abs(centred) < band
            columns = slice(start, start + LANES)
            cos_ref[at, columns] = jnp.where(inside, cosine, 0.0)
            sin_ref[at, columns] = jnp.where(inside, sine, 0.0)
            reach = move * jnp.minimum(centred * centred, band_square) + (band_square >> 1)
            shift = jnp.zeros((8, LANES), jnp.int32)
            bound = band_square
            for offset in range(1, MIG + 1):
                shift = jnp.where(reach >= bound, offset, shift)
                bound = bound + band_square
            shift_ref[at, columns] = shift
        return carry

    lax.fori_loop(0, bins // 8, tables, 0)
    stores = []
    for source, target in (
        (cos_ref, cos_hbm),
        (sin_ref, sin_hbm),
        (shift_ref, shift_hbm),
        (mix_ref, mix_hbm),
    ):
        copy = pltpu.make_async_copy(source, target, store_sems.at[len(stores)])
        copy.start()
        stores.append(copy)
    for copy in stores:
        copy.wait()
    for copy in own:
        copy.wait()

    def finish(i, carry):
        for chunk in range(3):
            copy = remote(chunk, i)
            copy.wait_send()
            copy.wait_recv()
        return carry

    lax.fori_loop(0, devices - 1, finish, 0)


def azimuth_kernel(
    sizes,
    recv_hbm,
    halo_hbm,
    doppler_hbm,
    halo_doppler_hbm,
    mix_hbm,
    shift_hbm,
    cos_hbm,
    sin_hbm,
    final_hbm,
    twiddle_hbm,
    out_hbm,
    recv_ref,
    halo_ref,
    doppler_ref,
    halo_doppler_ref,
    mix_ref,
    shift_ref,
    cos_ref,
    sin_ref,
    final_ref,
    twiddle_ref,
    spectra,
    unfolded,
    focused,
    image_ref,
    load_sems,
    recv_sems,
    store_sems,
):
    sources, local_pulses, channels, bins = sizes
    block = local_pulses * channels * 4
    arrivals = []

    def arrive(row):
        at = pl.ds(row, 8)
        copy = pltpu.make_async_copy(
            recv_hbm.at[:, at], recv_ref.at[:, at], recv_sems.at[len(arrivals)]
        )
        copy.start()
        arrivals.append(copy)

    loads = []

    def load(source, target):
        copy = pltpu.make_async_copy(source, target, load_sems.at[len(loads)])
        copy.start()
        loads.append(copy)
        return copy

    load_doppler = load(doppler_hbm, doppler_ref)
    for pair in range(channels // 2):
        for p in range(local_pulses):
            arrive((p * (channels // 2) + pair) * 8)
    load_halo = load(halo_hbm, halo_ref)
    load_halo_doppler = load(halo_doppler_hbm, halo_doppler_ref)
    load_mix = load(mix_hbm, mix_ref)
    load_tables = [
        load(shift_hbm, shift_ref),
        load(cos_hbm, cos_ref),
        load(sin_hbm, sin_ref),
    ]
    load_final = [load(final_hbm, final_ref), load(twiddle_hbm, twiddle_ref)]

    flat = recv_ref.reshape(sources * block, LANES)

    def rows_of(start):
        return flat[pl.ds(start, sources, stride=block), :]

    load_doppler.wait()
    for c in range(channels):
        if c % 2 == 0:
            for p in range(local_pulses):
                arrivals[c // 2 * local_pulses + p].wait()
        for half in range(bins // LANES):
            z = jnp.concatenate(
                [
                    rows_of(p * channels * 4 + c * 4 + part * 2 + half)
                    for part in range(2)
                    for p in range(local_pulses)
                ],
                axis=0,
            )
            spectra[c, half * LANES : (half + 1) * LANES, :] = dot_right(z.T, doppler_ref)
    groups = local_pulses * channels * MIG // LANES
    per_group = LANES // (MIG * channels)
    load_halo.wait()
    load_halo_doppler.wait()
    h = jnp.concatenate(
        [halo_ref[pl.ds(j, sources, stride=2 * groups), :] for j in range(2 * groups)], axis=0
    ).T
    step = channels * MIG
    halo = dot_right(h[:step], halo_doppler_ref.at[0])
    for k in range(1, per_group):
        halo = halo + dot_right(h[k * step : (k + 1) * step], halo_doppler_ref.at[k])
    for c in range(channels):
        spectra[c, bins:, :] = halo[c * MIG : (c + 1) * MIG]
    load_mix.wait()
    mix_channels(spectra, mix_ref, unfolded, bins + MIG, 0)
    for copy in load_tables:
        copy.wait()
    migrate_rows(unfolded, cos_ref, sin_ref, shift_ref, focused, bins)
    for copy in load_final:
        copy.wait()
    stores = []
    piece = LANES // 2
    for k in range(bins // piece):
        at = slice(k * piece, (k + 1) * piece)
        real, imag = inverse_rows(focused, final_ref, twiddle_ref, at)
        image_ref[0, at, :] = real
        image_ref[1, at, :] = imag
        rows = pl.ds(k * piece, piece)
        copy = pltpu.make_async_copy(
            image_ref.at[:, rows], out_hbm.at[:, rows], store_sems.at[k]
        )
        copy.start()
        stores.append(copy)
    for copy in stores:
        copy.wait()


def fits(pulses, channels, length, devices):
    local_pulses = pulses // devices
    signals = local_pulses * channels
    bins = length // devices
    lead = length // LANES
    return (
        pulses == LANES
        and length % (LANES * devices) == 0
        and bins == 2 * LANES
        and channels == 4
        and 2 * lead == LANES
        and devices % 8 == 0
        and signals * MIG % LANES == 0
        and LANES % (MIG * channels) == 0
        and 2 * (signals * MIG // LANES) <= HALO_ROWS
        and channels * pulses <= 512
    )


def hbm():
    return pl.BlockSpec(memory_space=pltpu.HBM)


def vmem():
    return pl.BlockSpec(memory_space=pltpu.VMEM)


def blocked_local(
    raw_echoes, chirp_spectrum, reconstruction, delays, azimuth_rate, band_halfwidth, migration
):
    local_pulses, channels, _, length = raw_echoes.shape
    inner = lax.axis_size("rg")
    devices = lax.axis_size("az") * inner
    bins = length // devices
    lead = length // LANES
    pulses = local_pulses * devices
    signals = local_pulses * channels
    doppler_bins = channels * pulses
    leads = np.arange(lead)
    lanes = np.arange(LANES)

    first = left_matrix(*roots(leads, leads, lead, -1.0))
    first = first.transpose(0, 1, 3, 2).reshape(2 * lead, 2 * lead)
    turned = np.concatenate([lanes[0::2], lanes[1::2]])
    forward = right_matrix(*roots(lanes, turned, LANES, -1.0)).reshape(2 * LANES, 2 * LANES)
    inverse = right_matrix(*roots(turned, lanes, LANES, 1.0)).reshape(2 * LANES, 2 * LANES)
    last = left_matrix(*roots(leads, leads, lead, 1.0)) / length
    pair = np.zeros((devices, 2, 2, 2, 2, 2 * lead))
    by_device = last.reshape(2, devices, 2, 2 * lead).transpose(1, 0, 2, 3)
    for s in range(2):
        pair[:, s, :, :, s, :] = by_device
    pair = pair.reshape(devices * 8, 4 * lead)
    halo = np.zeros((devices, HALO_ROWS, 2 * lead))
    groups = signals * MIG // LANES
    for g in range(groups):
        halo[:-1, 2 * g : 2 * g + 2] = by_device[1:, :, 0]
    halo = halo.reshape(devices * HALO_ROWS, 2 * lead)
    twiddles = np.stack(roots(leads, lanes, length, -1.0)).astype(np.float32)

    sources = np.arange(devices)
    bins_f = doppler_of(np.arange(pulses))
    order_f = (np.arange(pulses)[:, None] == bins_f[None, :]).astype(ml_dtypes.bfloat16)
    order = (np.arange(local_pulses)[:, None] + sources[None, :] * local_pulses).reshape(-1)
    scale = 1.0 / math.sqrt(pulses)
    to_doppler = right_matrix(*roots(order, bins_f, pulses, -1.0)) * scale
    to_doppler = to_doppler.reshape(2 * pulses, 2 * pulses)
    per_group = local_pulses // groups
    halo_doppler = []
    for k in range(per_group):
        by_group = []
        for g in range(groups):
            at = sources * local_pulses + g * per_group + k
            by_group.append(
                (right_matrix(*roots(at, bins_f, pulses, -1.0)) * scale).reshape(
                    2 * devices, 2 * pulses
                )
            )
        halo_doppler.append(split_constant(np.concatenate(by_group, axis=0)))
    halo_doppler = np.stack(halo_doppler)
    final = right_matrix(*roots(lanes, lanes, LANES, 1.0)) / math.sqrt(doppler_bins)
    final = split_constant(final.reshape(2 * LANES, 2 * LANES))
    regroup = np.stack(roots(np.arange(8) % 4, lanes, doppler_bins, 1.0)).astype(np.float32)

    x = raw_echoes.reshape(signals, 2, lead, LANES).transpose(0, 2, 1, 3)
    x = x.reshape(signals, 2 * lead, LANES)
    chirp = chirp_spectrum.reshape(2, lead, LANES).transpose(1, 0, 2).reshape(2 * lead, LANES)
    block = signals * 4
    tables = (bins, doppler_bins)
    by_lane = (bins // LANES, LANES)
    operands = (
        x,
        chirp,
        azimuth_rate.reshape(by_lane),
        band_halfwidth.reshape(by_lane),
        migration.reshape(by_lane),
        split_constant(first),
        twiddles,
        split_constant(forward),
        split_constant(inverse),
        split_constant(pair),
        split_constant(halo),
        reconstruction.reshape(2, channels * channels, pulses),
        delays.reshape(1, channels),
        order_f,
    )
    received, halo_received, cosine, sine, shift, mix = pl.pallas_call(
        functools.partial(
            compress_kernel, (local_pulses, channels, lead, devices, inner, doppler_bins)
        ),
        out_shape=(
            jax.ShapeDtypeStruct((devices, block, LANES), jnp.float32),
            jax.ShapeDtypeStruct((devices, 2 * groups, LANES), jnp.float32),
            jax.ShapeDtypeStruct(tables, jnp.float32),
            jax.ShapeDtypeStruct(tables, jnp.float32),
            jax.ShapeDtypeStruct(tables, jnp.int32),
            jax.ShapeDtypeStruct((2, channels * channels, pulses), jnp.float32),
        ),
        in_specs=[hbm()] * len(operands),
        out_specs=(hbm(),) * 6,
        scratch_shapes=[pltpu.VMEM(value.shape, value.dtype) for value in operands]
        + [
            pltpu.VMEM((devices, block, LANES), jnp.float32),
            pltpu.VMEM((devices, 2 * groups, LANES), jnp.float32),
            pltpu.VMEM((3, bins, LANES), jnp.float32),
            pltpu.VMEM(tables, jnp.float32),
            pltpu.VMEM(tables, jnp.float32),
            pltpu.VMEM(tables, jnp.int32),
            pltpu.VMEM((2, channels * channels, pulses), jnp.float32),
            pltpu.SemaphoreType.DMA((len(operands) + local_pulses - 1,)),
            pltpu.SemaphoreType.DMA((4,)),
            pltpu.SemaphoreType.DMA((2,)),
            pltpu.SemaphoreType.DMA((3, devices)),
            pltpu.SemaphoreType.DMA((3, devices)),
        ],
        compiler_params=pltpu.CompilerParams(
            collective_id=0, has_side_effects=True, vmem_limit_bytes=KERNEL_VMEM
        ),
        name="compress_exchange",
    )(*operands)
    inputs = (
        received,
        halo_received.reshape(devices * 2 * groups, LANES),
        split_constant(to_doppler),
        halo_doppler,
        mix,
        shift,
        cosine,
        sine,
        final,
        regroup,
    )
    return pl.pallas_call(
        functools.partial(azimuth_kernel, (devices, local_pulses, channels, bins)),
        out_shape=jax.ShapeDtypeStruct((2, bins, doppler_bins), jnp.float32),
        in_specs=[hbm()] * len(inputs),
        out_specs=hbm(),
        scratch_shapes=[pltpu.VMEM(value.shape, value.dtype) for value in inputs]
        + [
            pltpu.VMEM((channels, bins + MIG, 2 * pulses), jnp.float32),
            pltpu.VMEM((bins + MIG, 2 * doppler_bins), jnp.float32),
            pltpu.VMEM((bins, 2 * doppler_bins), jnp.float32),
            pltpu.VMEM((2, bins, doppler_bins), jnp.float32),
            pltpu.SemaphoreType.DMA((len(inputs) - 1,)),
            pltpu.SemaphoreType.DMA((channels // 2 * local_pulses,)),
            pltpu.SemaphoreType.DMA((2 * bins // LANES,)),
        ],
        compiler_params=pltpu.CompilerParams(vmem_limit_bytes=KERNEL_VMEM),
        name="azimuth_focus",
    )(*inputs)


def local(raw_echoes, chirp_spectrum, reconstruction, *rest):
    local_pulses, channels, _, length = raw_echoes.shape
    devices = lax.axis_size("az") * lax.axis_size("rg")
    if fits(local_pulses * devices, channels, length, devices):
        return blocked_local(raw_echoes, chirp_spectrum, reconstruction, *rest)
    return plain_local(raw_echoes, chirp_spectrum, reconstruction, *rest)


def solution(mesh):
    in_specs = (
        P(("az", "rg"), None, None, None),
        P(),
        P(),
        P(),
        P(("az", "rg")),
        P(("az", "rg")),
        P(("az", "rg")),
    )
    out_specs = P(None, ("az", "rg"), None)
    return jax.shard_map(local, mesh=mesh, in_specs=in_specs, out_specs=out_specs, check_vma=False)
```

```python
import functools
import math

import jax
import jax.numpy as jnp
import ml_dtypes
import numpy as np
from jax import lax
from jax.experimental import pallas as pl
from jax.experimental.pallas import tpu as pltpu
from jax.sharding import PartitionSpec as P

MIG = 16
LANES = 128
HALO_ROWS = 8
KERNEL_VMEM = 62 * 1024 * 1024


highest = lax.Precision.HIGHEST
curvature = 32.0


def passed_along(value, axis, by):
    size = lax.axis_size(axis)
    pairs = [(i, i + by) for i in range(size) if 0 <= i + by < size]
    return lax.ppermute(value, axis, pairs)


def factor_pair(length):
    largest = 1
    for candidate in range(1, length + 1):
        if candidate * candidate > length:
            break
        if length % candidate == 0:
            largest = candidate
    return (largest, length // largest)


def dft_matrix(length, direction):
    indices = jnp.arange(length, dtype=jnp.int32)
    angles = (
        2.0 * math.pi / length * (indices[:, None] * indices[None, :] % length).astype(jnp.float32)
    )
    cosine = jnp.cos(angles)
    sines = direction * jnp.sin(angles)
    return jnp.stack(
        [jnp.stack([cosine, -sines], axis=1), jnp.stack([sines, cosine], axis=1)], axis=0
    )


def twiddle(lead_size, trail_size, length, direction):
    lead_index = jnp.arange(lead_size, dtype=jnp.int32)
    trail_index = jnp.arange(trail_size, dtype=jnp.int32)
    angles = (
        2.0
        * math.pi
        / length
        * (lead_index[:, None] * trail_index[None, :] % length).astype(jnp.float32)
    )
    return (jnp.cos(angles), direction * jnp.sin(angles))


def complex_mul(values, factor_real, factor_imag, part_axis):
    real_part = lax.index_in_dim(values, 0, part_axis, keepdims=True)
    imag_part = lax.index_in_dim(values, 1, part_axis, keepdims=True)
    return jnp.concatenate(
        [
            real_part * factor_real - imag_part * factor_imag,
            real_part * factor_imag + imag_part * factor_real,
        ],
        axis=part_axis,
    )


def range_focus(raw_echoes, chirp_spectrum):
    local_pulses, channels, _, length = raw_echoes.shape
    lead_size, trail_size = factor_pair(length)
    layout = raw_echoes.reshape(local_pulses, channels, 2, lead_size, trail_size)
    sectioned = jnp.einsum(
        "okci,pqcij->pqokj", dft_matrix(lead_size, -1.0), layout, precision=highest
    )
    twiddle_real, twiddle_imag = twiddle(lead_size, trail_size, length, -1.0)
    sectioned = complex_mul(sectioned, twiddle_real, twiddle_imag, 2)
    spectrum = jnp.einsum(
        "olcj,pqckj->pqolk", dft_matrix(trail_size, -1.0), sectioned, precision=highest
    )
    spectrum = spectrum.reshape(local_pulses, channels, 2, length)
    spectrum = complex_mul(spectrum, chirp_spectrum[0], -chirp_spectrum[1], 2)
    layout = spectrum.reshape(local_pulses, channels, 2, lead_size, trail_size)
    sectioned = jnp.einsum(
        "okci,pqcij->pqokj", dft_matrix(lead_size, 1.0), layout, precision=highest
    )
    twiddle_real, twiddle_imag = twiddle(lead_size, trail_size, length, 1.0)
    sectioned = complex_mul(sectioned, twiddle_real, twiddle_imag, 2)
    restored = jnp.einsum(
        "olcj,pqckj->qoplk", dft_matrix(trail_size, 1.0), sectioned, precision=highest
    )
    return restored.reshape(channels, 2, local_pulses, length) / length


def reconstruct(turned, mixing_real, mixing_imag):
    channels, _, local_pulses, blocks, bin_count = turned.shape
    pulse_total = blocks * local_pulses
    sectioned = jnp.einsum("okcm,qcimb->qobik", dft_matrix(blocks, -1.0), turned, precision=highest)
    twiddle_real, twiddle_imag = twiddle(local_pulses, blocks, pulse_total, -1.0)
    sectioned = complex_mul(sectioned, twiddle_real, twiddle_imag, 1)
    spectrum = jnp.einsum(
        "olci,qcbik->qoblk", dft_matrix(local_pulses, -1.0), sectioned, precision=highest
    )
    spectrum = spectrum.reshape(channels, 2, bin_count, pulse_total) / math.sqrt(pulse_total)
    spec_real = spectrum[:, 0]
    spec_imag = spectrum[:, 1]
    unfolded_real = jnp.einsum(
        "bcf,crf->rbf", mixing_real, spec_real, precision=highest
    ) - jnp.einsum("bcf,crf->rbf", mixing_imag, spec_imag, precision=highest)
    unfolded_imag = jnp.einsum(
        "bcf,crf->rbf", mixing_real, spec_imag, precision=highest
    ) + jnp.einsum("bcf,crf->rbf", mixing_imag, spec_real, precision=highest)
    unfolded = jnp.stack([unfolded_real, unfolded_imag], axis=0)
    return unfolded.reshape(2, bin_count, channels * pulse_total)


def azimuth_focus(unfolded, azimuth_rate, band_halfwidth, migration):
    bin_count = azimuth_rate.shape[0]
    length = unfolded.shape[2]
    doppler_index = jnp.arange(length, dtype=jnp.int32)
    centred = doppler_index - length * (doppler_index >= length // 2).astype(jnp.int32)
    band_square = band_halfwidth * band_halfwidth
    squared = jnp.minimum((centred * centred)[None, :], band_square[:, None])
    migration_shift = (migration[:, None] * squared + (band_square // 2)[:, None]) // band_square[
        :, None
    ]
    migrated = jnp.zeros((2, bin_count, length), jnp.float32)
    for offset in range(MIG + 1):
        window = unfolded[:, offset : offset + bin_count, :]
        migrated = jnp.where((migration_shift == offset)[None], window, migrated)
    relative = centred.astype(jnp.float32) / (length // 2)
    matched_phase = math.pi * curvature * azimuth_rate[:, None] * (relative * relative)[None, :]
    focused = complex_mul(migrated, jnp.cos(matched_phase), jnp.sin(matched_phase), 0)
    inside = jnp.abs(centred)[None, :] < band_halfwidth[:, None]
    focused = jnp.where(inside[None], focused, 0.0)
    lead_size, trail_size = factor_pair(length)
    layout = focused.reshape(2, bin_count, lead_size, trail_size)
    sectioned = jnp.einsum("okci,cbij->obkj", dft_matrix(lead_size, 1.0), layout, precision=highest)
    twiddle_real, twiddle_imag = twiddle(lead_size, trail_size, length, 1.0)
    sectioned = complex_mul(sectioned, twiddle_real, twiddle_imag, 0)
    focused_image = jnp.einsum(
        "olcj,cbkj->oblk", dft_matrix(trail_size, 1.0), sectioned, precision=highest
    )
    return focused_image.reshape(2, bin_count, length) / math.sqrt(length)


def plain_local(
    raw_echoes, chirp_spectrum, reconstruction, delays, azimuth_rate, band_halfwidth, migration
):
    compressed = range_focus(raw_echoes, chirp_spectrum)
    channels, _, local_pulses, length = compressed.shape
    azimuth_count = lax.axis_size("az")
    range_count = lax.axis_size("rg")
    bin_count = length // (azimuth_count * range_count)
    layout = compressed.reshape(channels, 2, local_pulses, azimuth_count, range_count, bin_count)
    layout = lax.all_to_all(layout, "rg", split_axis=4, concat_axis=4, tiled=True)
    layout = lax.all_to_all(layout, "az", split_axis=3, concat_axis=3, tiled=True)
    turned = layout.reshape(channels, 2, local_pulses, azimuth_count * range_count, bin_count)
    pulse_total = azimuth_count * range_count * local_pulses
    frequency = jnp.arange(pulse_total, dtype=jnp.int32)
    angles = (
        2.0
        * math.pi
        / pulse_total
        * (frequency[None, :] * delays[:, None] % pulse_total).astype(jnp.float32)
    )
    align_real = jnp.cos(angles)[None]
    align_imag = jnp.sin(angles)[None]
    mixing_real = reconstruction[0] * align_real - reconstruction[1] * align_imag
    mixing_imag = reconstruction[0] * align_imag + reconstruction[1] * align_real
    unfolded = reconstruct(turned, mixing_real, mixing_imag)
    margin_bins = passed_along(unfolded[:, :MIG, :], ("az", "rg"), -1)
    unfolded = jnp.concatenate([unfolded, margin_bins], axis=1)
    return azimuth_focus(unfolded, azimuth_rate, band_halfwidth, migration)


def split_constant(values):
    high = values.astype(ml_dtypes.bfloat16)
    low = (values - high.astype(np.float64)).astype(ml_dtypes.bfloat16)
    return np.stack([high, low])


def roots(rows, columns, length, direction):
    turns = (rows[:, None] * columns[None, :]) % length
    angles = 2.0 * np.pi / length * turns
    return np.cos(angles), direction * np.sin(angles)


def left_matrix(cosine, sine):
    return np.stack([np.stack([cosine, -sine], 1), np.stack([sine, cosine], 1)], 0)


def right_matrix(cosine, sine):
    return np.stack([np.stack([cosine, sine], 1), np.stack([-sine, cosine], 1)], 0)


def split(values):
    high = values.astype(jnp.bfloat16)
    low = (values - high.astype(jnp.float32)).astype(jnp.bfloat16)
    return high, low


def dot(a, b):
    return jnp.dot(a, b, preferred_element_type=jnp.float32)


def dot_right(values, matrix):
    high, low = split(values)
    rows = values.shape[0]
    both = dot(jnp.concatenate([high, low], axis=0), matrix[0])
    return both[:rows] + (both[rows:] + dot(high, matrix[1]))


def dot_left(matrix, values):
    high, low = split(values)
    return dot(matrix[0], high) + (dot(matrix[1], high) + dot(matrix[0], low))


def cos_sin_turns(turns):
    quarter = jnp.floor(turns * 4.0 + 0.5)
    theta = (turns - quarter * 0.25) * (2.0 * math.pi)
    square = theta * theta
    cosine = 1.0 + square * (
        -0.5 + square * (1.0 / 24 + square * (-1.0 / 720 + square * (1.0 / 40320)))
    )
    sine = theta * (
        1.0
        + square
        * (-1.0 / 6 + square * (1.0 / 120 + square * (-1.0 / 5040 + square * (1.0 / 362880))))
    )
    index = quarter.astype(jnp.int32)
    odd = (index & 1) == 1
    cos_negative = ((index + 1) & 2) == 2
    sin_negative = (index & 2) == 2
    cos_size = jnp.where(odd, sine, cosine)
    sin_size = jnp.where(odd, cosine, sine)
    return (
        jnp.where(cos_negative, -cos_size, cos_size),
        jnp.where(sin_negative, -sin_size, sin_size),
    )


def spread_rows(values):
    return jnp.concatenate(
        [
            jnp.broadcast_to(values[h : h + 1, :], (LANES, LANES)).T
            for h in range(values.shape[0])
        ],
        axis=0,
    )


def dot_exact(values, matrix):
    high = values.astype(jnp.bfloat16)
    rest = values - high.astype(jnp.float32)
    middle = rest.astype(jnp.bfloat16)
    low = (rest - middle.astype(jnp.float32)).astype(jnp.bfloat16)
    return dot(high, matrix) + dot(middle, matrix) + dot(low, matrix)


def doppler_of(lane):
    return (lane % (LANES // 4)) * 4 + lane // (LANES // 4)


def mix_channels(spectra, mix, unfolded, rows, shift):
    channels = spectra.shape[0]
    pulses = spectra.shape[2] // 2
    length = channels * pulses

    def mix_rows(index, carry):
        at = pl.ds(pl.multiple_of(index * 16, 16), 16)
        to = pl.ds(pl.multiple_of(index * 16 + shift, 8), 16)
        spec = [spectra[c, at, :] for c in range(channels)]
        for b in range(channels):
            total_r = total_i = None
            for c in range(channels):
                m = b * channels + c
                m_r, m_i = mix[0, m : m + 1, :], mix[1, m : m + 1, :]
                d_r, d_i = spec[c][:, :pulses], spec[c][:, pulses:]
                r = m_r * d_r - m_i * d_i
                i = m_r * d_i + m_i * d_r
                total_r = r if c == 0 else total_r + r
                total_i = i if c == 0 else total_i + i
            unfolded[to, b * pulses : (b + 1) * pulses] = total_r
            unfolded[to, length + b * pulses : length + (b + 1) * pulses] = total_i
        return carry

    lax.fori_loop(0, rows // 16, mix_rows, 0)


def migrate_rows(unfolded, cos_ref, sin_ref, shift_ref, focused, rows):
    length = shift_ref.shape[1]

    def focus_band(b, carry):
        lane = pl.multiple_of(b * LANES, LANES)
        columns = (pl.ds(lane, LANES), pl.ds(pl.multiple_of(length + lane, LANES), LANES))

        def windows(start):
            return [
                [unfolded[start + k : start + k + 8, column] for k in range(8)]
                for column in columns
            ]

        ahead = windows(0)
        for start in range(0, rows, 8):
            at = slice(start, start + 8)
            now, ahead = ahead, windows(start + 8)
            shift = shift_ref[at, columns[0]]
            bits = [(shift & (1 << level)) != 0 for level in range(5)]
            values = []
            for part, column in enumerate(columns):
                level_values = now[part] + ahead[part]
                for level in range(4):
                    level_values = [
                        jnp.where(bits[level], level_values[k + 1], level_values[k])
                        for k in range(0, len(level_values), 2)
                    ]
                last = unfolded[start + MIG : start + MIG + 8, column]
                values.append(jnp.where(bits[4], last, level_values[0]))
            real, imag = values
            cosine = cos_ref[at, columns[0]]
            sine = sin_ref[at, columns[0]]
            focused[at, columns[0]] = real * cosine - imag * sine
            focused[at, columns[1]] = real * sine + imag * cosine
        return carry

    lax.fori_loop(0, length // LANES, focus_band, 0)


def inverse_rows(focused, final_ref, twiddle_ref, at):
    group = LANES // 4
    rows = at.stop - at.start
    line = lax.broadcasted_iota(jnp.int32, (rows, LANES), 1) // group
    parts = []
    for part in range(2):
        base = part * 4 * LANES
        turned = []
        for b in range(4):
            value = focused[at, base + b * LANES : base + (b + 1) * LANES]
            turned.append(value if b == 0 else pltpu.roll(value, b * group, 1))
        grouped = []
        for j in range(4):
            value = turned[(0 - j) % 4]
            for g in range(1, 4):
                value = jnp.where(line == g, turned[(g - j) % 4], value)
            grouped.append(value if j == 0 else pltpu.roll(value, LANES - j * group, 1))
        parts.append(grouped)
    stacked = jnp.concatenate(
        [jnp.concatenate([parts[0][j], parts[1][j]], axis=1) for j in range(4)], axis=0
    )
    image = dot_right(stacked, final_ref)
    real, imag = [], []
    for j in range(4):
        r = image[j * rows : (j + 1) * rows, :LANES]
        i = image[j * rows : (j + 1) * rows, LANES:]
        if j > 0:
            t_r, t_i = twiddle_ref[0, j : j + 1, :], twiddle_ref[1, j : j + 1, :]
            r, i = r * t_r - i * t_i, r * t_i + i * t_r
        real.append(r)
        imag.append(i)
    a_r, a_i = real[0] + real[2], imag[0] + imag[2]
    b_r, b_i = real[0] - real[2], imag[0] - imag[2]
    c_r, c_i = real[1] + real[3], imag[1] + imag[3]
    d_r, d_i = imag[3] - imag[1], real[1] - real[3]
    return (
        jnp.concatenate([a_r + c_r, b_r + d_r, a_r - c_r, b_r - d_r], axis=1),
        jnp.concatenate([a_i + c_i, b_i + d_i, a_i - c_i, b_i - d_i], axis=1),
    )


def compress_kernel(
    sizes,
    x_hbm,
    chirp_hbm,
    rate_hbm,
    band_hbm,
    migration_hbm,
    first_hbm,
    twiddle_hbm,
    fwd_hbm,
    inv_hbm,
    last_hbm,
    halo_hbm,
    reconstruction_hbm,
    delays_hbm,
    order_hbm,
    recv_ref,
    cos_hbm,
    sin_hbm,
    shift_hbm,
    mix_hbm,
    x_ref,
    chirp_ref,
    rate_ref,
    band_ref,
    migration_ref,
    first_ref,
    twiddle_ref,
    fwd_ref,
    inv_ref,
    last_ref,
    halo_ref,
    reconstruction_ref,
    delays_ref,
    order_ref,
    send_ref,
    rows_ref,
    cos_ref,
    sin_ref,
    shift_ref,
    mix_ref,
    load_sems,
    store_sems,
    local_sem,
    send_sems,
    recv_sems,
):
    pulses, channels, lead, devices, inner, length = sizes
    mine = lax.axis_index("az") * inner + lax.axis_index("rg")
    barrier = pltpu.get_barrier_semaphore()

    def place(index):
        return (lax.div(index, inner), lax.rem(index, inner))

    def greet(k, carry):
        pl.semaphore_signal(
            barrier,
            inc=1,
            device_id=place(lax.rem(mine + k, devices)),
            device_id_type=pl.DeviceIdType.MESH,
        )
        return carry

    loads = []

    def start_load(source, target):
        copy = pltpu.make_async_copy(source, target, load_sems.at[len(loads)])
        copy.start()
        loads.append(copy)
        return copy

    def pulse_load(p):
        at = pl.ds(p * channels, channels)
        return start_load(x_hbm.at[at], x_ref.at[at])

    load_x = [pulse_load(0)]
    load_first = start_load(first_hbm, first_ref)
    load_twiddle = start_load(twiddle_hbm, twiddle_ref)
    load_fwd = start_load(fwd_hbm, fwd_ref)
    load_chirp = start_load(chirp_hbm, chirp_ref)
    load_inv = start_load(inv_hbm, inv_ref)
    load_last = start_load(last_hbm, last_ref)
    load_x += [pulse_load(p) for p in range(1, pulses)]
    load_halo = start_load(halo_hbm, halo_ref)
    load_rate = start_load(rate_hbm, rate_ref)
    load_band = start_load(band_hbm, band_ref)
    load_migration = start_load(migration_hbm, migration_ref)
    load_reconstruction = start_load(reconstruction_hbm, reconstruction_ref)
    load_delays = start_load(delays_hbm, delays_ref)
    load_order = start_load(order_hbm, order_ref)
    lax.fori_loop(1, devices, greet, 0)

    rows = pulses * channels * 4 + HALO_ROWS
    cut = channels * 4

    def remote(chunk, i):
        far = lax.div(i + 1, 2)
        step = devices // 2 + far - 2 * far * lax.rem(i, 2)
        target = lax.rem(mine + step, devices)
        at = pl.ds(0, cut) if chunk == 0 else pl.ds(cut, rows - cut)
        return pltpu.make_async_remote_copy(
            src_ref=send_ref.at[target, at],
            dst_ref=recv_ref.at[mine, at],
            send_sem=send_sems.at[chunk, step],
            recv_sem=recv_sems.at[chunk, step],
            device_id=place(target),
            device_id_type=pl.DeviceIdType.MESH,
        )

    def send(chunk):
        def body(i, carry):
            remote(chunk, i).start()
            return carry

        lax.fori_loop(0, devices - 1, body, 0)

    lane = lax.broadcasted_iota(jnp.int32, (2 * lead, LANES), 1)
    groups = pulses * channels * MIG // LANES
    per_group = LANES // MIG
    pairs = channels // 2
    packs = [jnp.zeros((2 * lead, LANES), jnp.float32) for _ in range(groups)]
    for p in range(pulses):
        load_x[p].wait()
        if p == 0:
            load_first.wait()
        x = jnp.concatenate([x_ref[p * channels + c] for c in range(channels)], axis=1)
        y = dot_left(first_ref, x)
        if p == 0:
            load_twiddle.wait()
            load_fwd.wait()
            load_chirp.wait()
            load_inv.wait()
            tw_r = jnp.concatenate([twiddle_ref[0]] * channels, axis=0)
            tw_i = jnp.concatenate([twiddle_ref[1]] * channels, axis=0)
            chirp = jnp.concatenate(
                [chirp_ref[pl.ds(part, lead, stride=2), :] for part in range(2)], axis=0
            ).T
            top, bottom = chirp[:lead], chirp[lead:]
            left = lane[:lead] < lead
            chirp_r = jnp.where(left, top, pltpu.roll(bottom, lead, 1))
            chirp_i = jnp.where(left, pltpu.roll(top, lead, 1), bottom)
            chirp_r = jnp.concatenate([chirp_r] * channels, axis=0)
            chirp_i = jnp.concatenate([chirp_i] * channels, axis=0)
        y = jnp.concatenate([y[:, c * LANES : (c + 1) * LANES] for c in range(channels)], axis=0)
        y = y.reshape(channels, 2, lead, LANES)
        y_r = y[:, 0].reshape(channels * lead, LANES)
        y_i = y[:, 1].reshape(channels * lead, LANES)
        y = jnp.concatenate([y_r * tw_r - y_i * tw_i, y_r * tw_i + y_i * tw_r], axis=1)
        s = dot_right(y, fwd_ref)
        s_r, s_i = s[:, :LANES], s[:, LANES:]
        s = jnp.concatenate(
            [s_r * chirp_r + s_i * chirp_i, s_i * chirp_r - s_r * chirp_i], axis=1
        )
        t = dot_right(s, inv_ref)
        t_r, t_i = t[:, :LANES], t[:, LANES:]
        z_r = t_r * tw_r + t_i * tw_i
        z_i = t_i * tw_r - t_r * tw_i
        z = [
            jnp.concatenate(
                [z_r[c * lead : (c + 1) * lead], z_i[c * lead : (c + 1) * lead]], axis=0
            )
            for c in range(channels)
        ]
        stacked = jnp.concatenate(
            [jnp.concatenate([z[2 * k], z[2 * k + 1]], axis=0) for k in range(pairs)], axis=1
        )
        if p == 0:
            load_last.wait()
        w = dot_left(last_ref, stacked)
        for k in range(pairs):
            row = (p * pairs + k) * 8
            send_ref[:, row : row + 8, :] = w[:, k * LANES : (k + 1) * LANES].reshape(
                devices, 8, LANES
            )
        for c in range(channels):
            signal = p * channels + c
            g, where = signal // per_group, signal % per_group
            moved = z[c] if where == 0 else pltpu.roll(z[c], where * MIG, 1)
            packs[g] = jnp.where(lane // MIG == where, moved, packs[g])
        if p == 0:
            pl.semaphore_wait(barrier, devices - 1)
            send(0)
    load_halo.wait()
    w = dot_left(halo_ref, jnp.concatenate(packs, axis=1))
    row = lax.broadcasted_iota(jnp.int32, (devices * HALO_ROWS, LANES), 0) % HALO_ROWS
    total = w[:, :LANES]
    for g in range(1, groups):
        total = jnp.where(row // 2 == g, w[:, g * LANES : (g + 1) * LANES], total)
    send_ref[:, pulses * channels * 4 :, :] = total.reshape(devices, HALO_ROWS, LANES)
    send(1)
    own = pltpu.make_async_copy(send_ref.at[mine], recv_ref.at[mine], local_sem)
    own.start()

    load_reconstruction.wait()
    load_delays.wait()
    load_order.wait()
    bins_f = pulses * devices
    shape = (channels * channels, bins_f)
    row = lax.broadcasted_iota(jnp.int32, shape, 0) % channels
    frequency = doppler_of(lax.broadcasted_iota(jnp.int32, shape, 1))
    delay = jnp.zeros_like(row)
    for c in range(channels):
        one = jnp.broadcast_to(delays_ref[0:1, c : c + 1], row.shape)
        delay = jnp.where(row == c, one, delay)
    turns = lax.rem(frequency * delay, bins_f).astype(jnp.float32) * (1.0 / bins_f)
    align_r, align_i = cos_sin_turns(turns)
    rec_r = dot_exact(reconstruction_ref[0], order_ref[...])
    rec_i = dot_exact(reconstruction_ref[1], order_ref[...])
    mix_ref[0] = rec_r * align_r - rec_i * align_i
    mix_ref[1] = rec_r * align_i + rec_i * align_r

    load_rate.wait()
    load_band.wait()
    load_migration.wait()
    rows_ref[0] = spread_rows(rate_ref[...])
    rows_ref[1] = spread_rows(band_ref[...].astype(jnp.float32))
    rows_ref[2] = spread_rows(migration_ref[...].astype(jnp.float32))
    bins = rows_ref.shape[1]

    def tables(index, carry):
        at = pl.ds(pl.multiple_of(index * 8, 8), 8)
        rate = rows_ref[0, at, :]
        band = rows_ref[1, at, :].astype(jnp.int32)
        move = rows_ref[2, at, :].astype(jnp.int32)
        band_square = band * band
        for start in range(0, length, LANES):
            doppler = doppler_of(lax.broadcasted_iota(jnp.int32, (8, LANES), 1)) + start
            centred = jnp.where(doppler >= length // 2, doppler - length, doppler)
            relative = centred.astype(jnp.float32) * (2.0 / length)
            cosine, sine = cos_sin_turns(rate * (relative * relative * (curvature / 2.0)))
            inside = jnp.abs(centred) < band
            columns = slice(start, start + LANES)
            cos_ref[at, columns] = jnp.where(inside, cosine, 0.0)
            sin_ref[at, columns] = jnp.where(inside, sine, 0.0)
            reach = move * jnp.minimum(centred * centred, band_square) + (band_square >> 1)
            shift = jnp.zeros((8, LANES), jnp.int32)
            bound = band_square
            for offset in range(1, MIG + 1):
                shift = jnp.where(reach >= bound, offset, shift)
                bound = bound + band_square
            shift_ref[at, columns] = shift
        return carry

    lax.fori_loop(0, bins // 8, tables, 0)
    stores = []
    for source, target in (
        (cos_ref, cos_hbm),
        (sin_ref, sin_hbm),
        (shift_ref, shift_hbm),
        (mix_ref, mix_hbm),
    ):
        copy = pltpu.make_async_copy(source, target, store_sems.at[len(stores)])
        copy.start()
        stores.append(copy)
    for copy in stores:
        copy.wait()
    own.wait()

    def finish(i, carry):
        for chunk in range(2):
            copy = remote(chunk, i)
            copy.wait_send()
            copy.wait_recv()
        return carry

    lax.fori_loop(0, devices - 1, finish, 0)


def azimuth_kernel(
    sizes,
    recv_hbm,
    doppler_hbm,
    halo_doppler_hbm,
    mix_hbm,
    shift_hbm,
    cos_hbm,
    sin_hbm,
    final_hbm,
    twiddle_hbm,
    out_hbm,
    recv_ref,
    doppler_ref,
    halo_doppler_ref,
    mix_ref,
    shift_ref,
    cos_ref,
    sin_ref,
    final_ref,
    twiddle_ref,
    spectra,
    unfolded,
    focused,
    image_ref,
    load_sems,
    recv_sems,
    store_sems,
):
    sources, local_pulses, channels, bins = sizes
    block = local_pulses * channels * 4 + HALO_ROWS
    arrivals = []

    def arrive(row):
        at = pl.ds(row, 8)
        copy = pltpu.make_async_copy(
            recv_hbm.at[:, at], recv_ref.at[:, at], recv_sems.at[len(arrivals)]
        )
        copy.start()
        arrivals.append(copy)

    loads = []

    def load(source, target):
        copy = pltpu.make_async_copy(source, target, load_sems.at[len(loads)])
        copy.start()
        loads.append(copy)
        return copy

    load_doppler = load(doppler_hbm, doppler_ref)
    for pair in range(channels // 2):
        for p in range(local_pulses):
            arrive((p * (channels // 2) + pair) * 8)
    arrive(local_pulses * channels * 4)
    load_halo_doppler = load(halo_doppler_hbm, halo_doppler_ref)
    load_mix = load(mix_hbm, mix_ref)
    load_tables = [
        load(shift_hbm, shift_ref),
        load(cos_hbm, cos_ref),
        load(sin_hbm, sin_ref),
    ]
    load_final = [load(final_hbm, final_ref), load(twiddle_hbm, twiddle_ref)]

    flat = recv_ref.reshape(sources * block, LANES)

    def rows_of(start):
        return flat[pl.ds(start, sources, stride=block), :]

    for pair in range(channels // 2):
        for p in range(local_pulses):
            arrivals[pair * local_pulses + p].wait()
        turned = []
        for c in (2 * pair, 2 * pair + 1):
            for half in range(bins // LANES):
                z = jnp.concatenate(
                    [
                        rows_of(p * channels * 4 + c * 4 + part * 2 + half)
                        for part in range(2)
                        for p in range(local_pulses)
                    ],
                    axis=0,
                )
                turned.append(z.T)
        if pair == 0:
            load_doppler.wait()
        result = dot_right(jnp.concatenate(turned, axis=0), doppler_ref)
        spectra[2 * pair, :bins, :] = result[:bins]
        spectra[2 * pair + 1, :bins, :] = result[bins:]
    groups = local_pulses * channels * MIG // LANES
    per_group = LANES // (MIG * channels)
    arrivals[-1].wait()
    load_halo_doppler.wait()
    h = jnp.concatenate(
        [rows_of(local_pulses * channels * 4 + j) for j in range(2 * groups)], axis=0
    ).T
    step = channels * MIG
    halo = dot_right(h[:step], halo_doppler_ref.at[0])
    for k in range(1, per_group):
        halo = halo + dot_right(h[k * step : (k + 1) * step], halo_doppler_ref.at[k])
    for c in range(channels):
        spectra[c, bins:, :] = halo[c * MIG : (c + 1) * MIG]
    load_mix.wait()
    mix_channels(spectra, mix_ref, unfolded, bins + MIG, 0)
    for copy in load_tables:
        copy.wait()
    migrate_rows(unfolded, cos_ref, sin_ref, shift_ref, focused, bins)
    for copy in load_final:
        copy.wait()
    stores = []
    for k in range(bins // LANES):
        at = slice(k * LANES, (k + 1) * LANES)
        real, imag = inverse_rows(focused, final_ref, twiddle_ref, at)
        image_ref[0, at, :] = real
        image_ref[1, at, :] = imag
        rows = pl.ds(k * LANES, LANES)
        copy = pltpu.make_async_copy(
            image_ref.at[:, rows], out_hbm.at[:, rows], store_sems.at[k]
        )
        copy.start()
        stores.append(copy)
    for copy in stores:
        copy.wait()


def fits(pulses, channels, length, devices):
    local_pulses = pulses // devices
    signals = local_pulses * channels
    bins = length // devices
    lead = length // LANES
    return (
        pulses == LANES
        and length % (LANES * devices) == 0
        and bins == 2 * LANES
        and channels == 4
        and 2 * lead == LANES
        and devices % 8 == 0
        and signals * MIG % LANES == 0
        and LANES % (MIG * channels) == 0
        and 2 * (signals * MIG // LANES) <= HALO_ROWS
        and channels * pulses <= 512
    )


def hbm():
    return pl.BlockSpec(memory_space=pltpu.HBM)


def vmem():
    return pl.BlockSpec(memory_space=pltpu.VMEM)


def blocked_local(
    raw_echoes, chirp_spectrum, reconstruction, delays, azimuth_rate, band_halfwidth, migration
):
    local_pulses, channels, _, length = raw_echoes.shape
    inner = lax.axis_size("rg")
    devices = lax.axis_size("az") * inner
    bins = length // devices
    lead = length // LANES
    pulses = local_pulses * devices
    signals = local_pulses * channels
    doppler_bins = channels * pulses
    leads = np.arange(lead)
    lanes = np.arange(LANES)

    first = left_matrix(*roots(leads, leads, lead, -1.0))
    first = first.transpose(0, 1, 3, 2).reshape(2 * lead, 2 * lead)
    turned = np.concatenate([lanes[0::2], lanes[1::2]])
    forward = right_matrix(*roots(lanes, turned, LANES, -1.0)).reshape(2 * LANES, 2 * LANES)
    inverse = right_matrix(*roots(turned, lanes, LANES, 1.0)).reshape(2 * LANES, 2 * LANES)
    last = left_matrix(*roots(leads, leads, lead, 1.0)) / length
    pair = np.zeros((devices, 2, 2, 2, 2, 2 * lead))
    by_device = last.reshape(2, devices, 2, 2 * lead).transpose(1, 0, 2, 3)
    for s in range(2):
        pair[:, s, :, :, s, :] = by_device
    pair = pair.reshape(devices * 8, 4 * lead)
    halo = np.zeros((devices, HALO_ROWS, 2 * lead))
    groups = signals * MIG // LANES
    for g in range(groups):
        halo[:-1, 2 * g : 2 * g + 2] = by_device[1:, :, 0]
    halo = halo.reshape(devices * HALO_ROWS, 2 * lead)
    twiddles = np.stack(roots(leads, lanes, length, -1.0)).astype(np.float32)

    sources = np.arange(devices)
    bins_f = doppler_of(np.arange(pulses))
    order_f = (np.arange(pulses)[:, None] == bins_f[None, :]).astype(ml_dtypes.bfloat16)
    order = (np.arange(local_pulses)[:, None] + sources[None, :] * local_pulses).reshape(-1)
    scale = 1.0 / math.sqrt(pulses)
    to_doppler = right_matrix(*roots(order, bins_f, pulses, -1.0)) * scale
    to_doppler = to_doppler.reshape(2 * pulses, 2 * pulses)
    per_group = local_pulses // groups
    halo_doppler = []
    for k in range(per_group):
        by_group = []
        for g in range(groups):
            at = sources * local_pulses + g * per_group + k
            by_group.append(
                (right_matrix(*roots(at, bins_f, pulses, -1.0)) * scale).reshape(
                    2 * devices, 2 * pulses
                )
            )
        halo_doppler.append(split_constant(np.concatenate(by_group, axis=0)))
    halo_doppler = np.stack(halo_doppler)
    final = right_matrix(*roots(lanes, lanes, LANES, 1.0)) / math.sqrt(doppler_bins)
    final = split_constant(final.reshape(2 * LANES, 2 * LANES))
    regroup = np.stack(roots(np.arange(8) % 4, lanes, doppler_bins, 1.0)).astype(np.float32)

    x = raw_echoes.reshape(signals, 2, lead, LANES).transpose(0, 2, 1, 3)
    x = x.reshape(signals, 2 * lead, LANES)
    chirp = chirp_spectrum.reshape(2, lead, LANES).transpose(1, 0, 2).reshape(2 * lead, LANES)
    block = signals * 4 + HALO_ROWS
    tables = (bins, doppler_bins)
    by_lane = (bins // LANES, LANES)
    operands = (
        x,
        chirp,
        azimuth_rate.reshape(by_lane),
        band_halfwidth.reshape(by_lane),
        migration.reshape(by_lane),
        split_constant(first),
        twiddles,
        split_constant(forward),
        split_constant(inverse),
        split_constant(pair),
        split_constant(halo),
        reconstruction.reshape(2, channels * channels, pulses),
        delays.reshape(1, channels),
        order_f,
    )
    received, cosine, sine, shift, mix = pl.pallas_call(
        functools.partial(
            compress_kernel, (local_pulses, channels, lead, devices, inner, doppler_bins)
        ),
        out_shape=(
            jax.ShapeDtypeStruct((devices, block, LANES), jnp.float32),
            jax.ShapeDtypeStruct(tables, jnp.float32),
            jax.ShapeDtypeStruct(tables, jnp.float32),
            jax.ShapeDtypeStruct(tables, jnp.int32),
            jax.ShapeDtypeStruct((2, channels * channels, pulses), jnp.float32),
        ),
        in_specs=[hbm()] * len(operands),
        out_specs=(hbm(),) * 5,
        scratch_shapes=[pltpu.VMEM(value.shape, value.dtype) for value in operands]
        + [
            pltpu.VMEM((devices, block, LANES), jnp.float32),
            pltpu.VMEM((3, bins, LANES), jnp.float32),
            pltpu.VMEM(tables, jnp.float32),
            pltpu.VMEM(tables, jnp.float32),
            pltpu.VMEM(tables, jnp.int32),
            pltpu.VMEM((2, channels * channels, pulses), jnp.float32),
            pltpu.SemaphoreType.DMA((len(operands) + local_pulses - 1,)),
            pltpu.SemaphoreType.DMA((4,)),
            pltpu.SemaphoreType.DMA,
            pltpu.SemaphoreType.DMA((2, devices)),
            pltpu.SemaphoreType.DMA((2, devices)),
        ],
        compiler_params=pltpu.CompilerParams(
            collective_id=0, has_side_effects=True, vmem_limit_bytes=KERNEL_VMEM
        ),
        name="compress_exchange",
    )(*operands)
    inputs = (
        received,
        split_constant(to_doppler),
        halo_doppler,
        mix,
        shift,
        cosine,
        sine,
        final,
        regroup,
    )
    return pl.pallas_call(
        functools.partial(azimuth_kernel, (devices, local_pulses, channels, bins)),
        out_shape=jax.ShapeDtypeStruct((2, bins, doppler_bins), jnp.float32),
        in_specs=[hbm()] * len(inputs),
        out_specs=hbm(),
        scratch_shapes=[pltpu.VMEM(value.shape, value.dtype) for value in inputs]
        + [
            pltpu.VMEM((channels, bins + MIG, 2 * pulses), jnp.float32),
            pltpu.VMEM((bins + MIG, 2 * doppler_bins), jnp.float32),
            pltpu.VMEM((bins, 2 * doppler_bins), jnp.float32),
            pltpu.VMEM((2, bins, doppler_bins), jnp.float32),
            pltpu.SemaphoreType.DMA((len(inputs) - 1,)),
            pltpu.SemaphoreType.DMA((channels // 2 * local_pulses + 1,)),
            pltpu.SemaphoreType.DMA((bins // LANES,)),
        ],
        compiler_params=pltpu.CompilerParams(vmem_limit_bytes=KERNEL_VMEM),
        name="azimuth_focus",
    )(*inputs)


def local(raw_echoes, chirp_spectrum, reconstruction, *rest):
    local_pulses, channels, _, length = raw_echoes.shape
    devices = lax.axis_size("az") * lax.axis_size("rg")
    if fits(local_pulses * devices, channels, length, devices):
        return blocked_local(raw_echoes, chirp_spectrum, reconstruction, *rest)
    return plain_local(raw_echoes, chirp_spectrum, reconstruction, *rest)


def solution(mesh):
    in_specs = (
        P(("az", "rg"), None, None, None),
        P(),
        P(),
        P(),
        P(("az", "rg")),
        P(("az", "rg")),
        P(("az", "rg")),
    )
    out_specs = P(None, ("az", "rg"), None)
    return jax.shard_map(local, mesh=mesh, in_specs=in_specs, out_specs=out_specs, check_vma=False)
```

```python
import functools
import math

import jax
import jax.numpy as jnp
import ml_dtypes
import numpy as np
from jax import lax
from jax.experimental import pallas as pl
from jax.experimental.pallas import tpu as pltpu
from jax.sharding import PartitionSpec as P

MIG = 16
LANES = 128
HALO_ROWS = 8
KERNEL_VMEM = 62 * 1024 * 1024


highest = lax.Precision.HIGHEST
curvature = 32.0


def passed_along(value, axis, by):
    size = lax.axis_size(axis)
    pairs = [(i, i + by) for i in range(size) if 0 <= i + by < size]
    return lax.ppermute(value, axis, pairs)


def factor_pair(length):
    largest = 1
    for candidate in range(1, length + 1):
        if candidate * candidate > length:
            break
        if length % candidate == 0:
            largest = candidate
    return (largest, length // largest)


def dft_matrix(length, direction):
    indices = jnp.arange(length, dtype=jnp.int32)
    angles = (
        2.0 * math.pi / length * (indices[:, None] * indices[None, :] % length).astype(jnp.float32)
    )
    cosine = jnp.cos(angles)
    sines = direction * jnp.sin(angles)
    return jnp.stack(
        [jnp.stack([cosine, -sines], axis=1), jnp.stack([sines, cosine], axis=1)], axis=0
    )


def twiddle(lead_size, trail_size, length, direction):
    lead_index = jnp.arange(lead_size, dtype=jnp.int32)
    trail_index = jnp.arange(trail_size, dtype=jnp.int32)
    angles = (
        2.0
        * math.pi
        / length
        * (lead_index[:, None] * trail_index[None, :] % length).astype(jnp.float32)
    )
    return (jnp.cos(angles), direction * jnp.sin(angles))


def complex_mul(values, factor_real, factor_imag, part_axis):
    real_part = lax.index_in_dim(values, 0, part_axis, keepdims=True)
    imag_part = lax.index_in_dim(values, 1, part_axis, keepdims=True)
    return jnp.concatenate(
        [
            real_part * factor_real - imag_part * factor_imag,
            real_part * factor_imag + imag_part * factor_real,
        ],
        axis=part_axis,
    )


def range_focus(raw_echoes, chirp_spectrum):
    local_pulses, channels, _, length = raw_echoes.shape
    lead_size, trail_size = factor_pair(length)
    layout = raw_echoes.reshape(local_pulses, channels, 2, lead_size, trail_size)
    sectioned = jnp.einsum(
        "okci,pqcij->pqokj", dft_matrix(lead_size, -1.0), layout, precision=highest
    )
    twiddle_real, twiddle_imag = twiddle(lead_size, trail_size, length, -1.0)
    sectioned = complex_mul(sectioned, twiddle_real, twiddle_imag, 2)
    spectrum = jnp.einsum(
        "olcj,pqckj->pqolk", dft_matrix(trail_size, -1.0), sectioned, precision=highest
    )
    spectrum = spectrum.reshape(local_pulses, channels, 2, length)
    spectrum = complex_mul(spectrum, chirp_spectrum[0], -chirp_spectrum[1], 2)
    layout = spectrum.reshape(local_pulses, channels, 2, lead_size, trail_size)
    sectioned = jnp.einsum(
        "okci,pqcij->pqokj", dft_matrix(lead_size, 1.0), layout, precision=highest
    )
    twiddle_real, twiddle_imag = twiddle(lead_size, trail_size, length, 1.0)
    sectioned = complex_mul(sectioned, twiddle_real, twiddle_imag, 2)
    restored = jnp.einsum(
        "olcj,pqckj->qoplk", dft_matrix(trail_size, 1.0), sectioned, precision=highest
    )
    return restored.reshape(channels, 2, local_pulses, length) / length


def reconstruct(turned, mixing_real, mixing_imag):
    channels, _, local_pulses, blocks, bin_count = turned.shape
    pulse_total = blocks * local_pulses
    sectioned = jnp.einsum("okcm,qcimb->qobik", dft_matrix(blocks, -1.0), turned, precision=highest)
    twiddle_real, twiddle_imag = twiddle(local_pulses, blocks, pulse_total, -1.0)
    sectioned = complex_mul(sectioned, twiddle_real, twiddle_imag, 1)
    spectrum = jnp.einsum(
        "olci,qcbik->qoblk", dft_matrix(local_pulses, -1.0), sectioned, precision=highest
    )
    spectrum = spectrum.reshape(channels, 2, bin_count, pulse_total) / math.sqrt(pulse_total)
    spec_real = spectrum[:, 0]
    spec_imag = spectrum[:, 1]
    unfolded_real = jnp.einsum(
        "bcf,crf->rbf", mixing_real, spec_real, precision=highest
    ) - jnp.einsum("bcf,crf->rbf", mixing_imag, spec_imag, precision=highest)
    unfolded_imag = jnp.einsum(
        "bcf,crf->rbf", mixing_real, spec_imag, precision=highest
    ) + jnp.einsum("bcf,crf->rbf", mixing_imag, spec_real, precision=highest)
    unfolded = jnp.stack([unfolded_real, unfolded_imag], axis=0)
    return unfolded.reshape(2, bin_count, channels * pulse_total)


def azimuth_focus(unfolded, azimuth_rate, band_halfwidth, migration):
    bin_count = azimuth_rate.shape[0]
    length = unfolded.shape[2]
    doppler_index = jnp.arange(length, dtype=jnp.int32)
    centred = doppler_index - length * (doppler_index >= length // 2).astype(jnp.int32)
    band_square = band_halfwidth * band_halfwidth
    squared = jnp.minimum((centred * centred)[None, :], band_square[:, None])
    migration_shift = (migration[:, None] * squared + (band_square // 2)[:, None]) // band_square[
        :, None
    ]
    migrated = jnp.zeros((2, bin_count, length), jnp.float32)
    for offset in range(MIG + 1):
        window = unfolded[:, offset : offset + bin_count, :]
        migrated = jnp.where((migration_shift == offset)[None], window, migrated)
    relative = centred.astype(jnp.float32) / (length // 2)
    matched_phase = math.pi * curvature * azimuth_rate[:, None] * (relative * relative)[None, :]
    focused = complex_mul(migrated, jnp.cos(matched_phase), jnp.sin(matched_phase), 0)
    inside = jnp.abs(centred)[None, :] < band_halfwidth[:, None]
    focused = jnp.where(inside[None], focused, 0.0)
    lead_size, trail_size = factor_pair(length)
    layout = focused.reshape(2, bin_count, lead_size, trail_size)
    sectioned = jnp.einsum("okci,cbij->obkj", dft_matrix(lead_size, 1.0), layout, precision=highest)
    twiddle_real, twiddle_imag = twiddle(lead_size, trail_size, length, 1.0)
    sectioned = complex_mul(sectioned, twiddle_real, twiddle_imag, 0)
    focused_image = jnp.einsum(
        "olcj,cbkj->oblk", dft_matrix(trail_size, 1.0), sectioned, precision=highest
    )
    return focused_image.reshape(2, bin_count, length) / math.sqrt(length)


def plain_local(
    raw_echoes, chirp_spectrum, reconstruction, delays, azimuth_rate, band_halfwidth, migration
):
    compressed = range_focus(raw_echoes, chirp_spectrum)
    channels, _, local_pulses, length = compressed.shape
    azimuth_count = lax.axis_size("az")
    range_count = lax.axis_size("rg")
    bin_count = length // (azimuth_count * range_count)
    layout = compressed.reshape(channels, 2, local_pulses, azimuth_count, range_count, bin_count)
    layout = lax.all_to_all(layout, "rg", split_axis=4, concat_axis=4, tiled=True)
    layout = lax.all_to_all(layout, "az", split_axis=3, concat_axis=3, tiled=True)
    turned = layout.reshape(channels, 2, local_pulses, azimuth_count * range_count, bin_count)
    pulse_total = azimuth_count * range_count * local_pulses
    frequency = jnp.arange(pulse_total, dtype=jnp.int32)
    angles = (
        2.0
        * math.pi
        / pulse_total
        * (frequency[None, :] * delays[:, None] % pulse_total).astype(jnp.float32)
    )
    align_real = jnp.cos(angles)[None]
    align_imag = jnp.sin(angles)[None]
    mixing_real = reconstruction[0] * align_real - reconstruction[1] * align_imag
    mixing_imag = reconstruction[0] * align_imag + reconstruction[1] * align_real
    unfolded = reconstruct(turned, mixing_real, mixing_imag)
    margin_bins = passed_along(unfolded[:, :MIG, :], ("az", "rg"), -1)
    unfolded = jnp.concatenate([unfolded, margin_bins], axis=1)
    return azimuth_focus(unfolded, azimuth_rate, band_halfwidth, migration)


def split_constant(values):
    high = values.astype(ml_dtypes.bfloat16)
    low = (values - high.astype(np.float64)).astype(ml_dtypes.bfloat16)
    return np.stack([high, low])


def roots(rows, columns, length, direction):
    turns = (rows[:, None] * columns[None, :]) % length
    angles = 2.0 * np.pi / length * turns
    return np.cos(angles), direction * np.sin(angles)


def left_matrix(cosine, sine):
    return np.stack([np.stack([cosine, -sine], 1), np.stack([sine, cosine], 1)], 0)


def right_matrix(cosine, sine):
    return np.stack([np.stack([cosine, sine], 1), np.stack([-sine, cosine], 1)], 0)


def split(values):
    high = values.astype(jnp.bfloat16)
    low = (values - high.astype(jnp.float32)).astype(jnp.bfloat16)
    return high, low


def dot(a, b):
    return jnp.dot(a, b, preferred_element_type=jnp.float32)


def dot_right(values, matrix):
    high, low = split(values)
    return dot(high, matrix[0]) + (dot(low, matrix[0]) + dot(high, matrix[1]))


def dot_left(matrix, values):
    high, low = split(values)
    return dot(matrix[0], high) + (dot(matrix[1], high) + dot(matrix[0], low))


def cos_sin_turns(turns):
    quarter = jnp.floor(turns * 4.0 + 0.5)
    theta = (turns - quarter * 0.25) * (2.0 * math.pi)
    square = theta * theta
    cosine = 1.0 + square * (
        -0.5 + square * (1.0 / 24 + square * (-1.0 / 720 + square * (1.0 / 40320)))
    )
    sine = theta * (
        1.0
        + square
        * (-1.0 / 6 + square * (1.0 / 120 + square * (-1.0 / 5040 + square * (1.0 / 362880))))
    )
    index = quarter.astype(jnp.int32)
    odd = (index & 1) == 1
    cos_negative = ((index + 1) & 2) == 2
    sin_negative = (index & 2) == 2
    cos_size = jnp.where(odd, sine, cosine)
    sin_size = jnp.where(odd, cosine, sine)
    return (
        jnp.where(cos_negative, -cos_size, cos_size),
        jnp.where(sin_negative, -sin_size, sin_size),
    )


def spread_rows(values):
    return jnp.concatenate(
        [
            jnp.broadcast_to(values[h : h + 1, :], (LANES, LANES)).T
            for h in range(values.shape[0])
        ],
        axis=0,
    )


def dot_exact(values, matrix):
    high = values.astype(jnp.bfloat16)
    rest = values - high.astype(jnp.float32)
    middle = rest.astype(jnp.bfloat16)
    low = (rest - middle.astype(jnp.float32)).astype(jnp.bfloat16)
    return dot(high, matrix) + dot(middle, matrix) + dot(low, matrix)


def doppler_of(lane):
    return (lane % (LANES // 4)) * 4 + lane // (LANES // 4)


def mix_channels(spectra, mix, unfolded, rows, shift):
    channels = spectra.shape[0]
    pulses = spectra.shape[2] // 2
    length = channels * pulses

    def mix_rows(index, carry):
        at = pl.ds(pl.multiple_of(index * 16, 16), 16)
        to = pl.ds(pl.multiple_of(index * 16 + shift, 8), 16)
        spec = [spectra[c, at, :] for c in range(channels)]
        for b in range(channels):
            total_r = total_i = None
            for c in range(channels):
                m = b * channels + c
                m_r, m_i = mix[0, m : m + 1, :], mix[1, m : m + 1, :]
                d_r, d_i = spec[c][:, :pulses], spec[c][:, pulses:]
                r = m_r * d_r - m_i * d_i
                i = m_r * d_i + m_i * d_r
                total_r = r if c == 0 else total_r + r
                total_i = i if c == 0 else total_i + i
            unfolded[to, b * pulses : (b + 1) * pulses] = total_r
            unfolded[to, length + b * pulses : length + (b + 1) * pulses] = total_i
        return carry

    lax.fori_loop(0, rows // 16, mix_rows, 0)


def migrate_rows(unfolded, cos_ref, sin_ref, shift_ref, focused, rows):
    length = shift_ref.shape[1]

    def focus_band(b, carry):
        lane = pl.multiple_of(b * LANES, LANES)
        columns = (pl.ds(lane, LANES), pl.ds(pl.multiple_of(length + lane, LANES), LANES))

        def windows(start):
            return [
                [unfolded[start + k : start + k + 8, column] for k in range(8)]
                for column in columns
            ]

        ahead = windows(0)
        for start in range(0, rows, 8):
            at = slice(start, start + 8)
            now, ahead = ahead, windows(start + 8)
            shift = shift_ref[at, columns[0]]
            bits = [(shift & (1 << level)) != 0 for level in range(5)]
            values = []
            for part, column in enumerate(columns):
                level_values = now[part] + ahead[part]
                for level in range(4):
                    level_values = [
                        jnp.where(bits[level], level_values[k + 1], level_values[k])
                        for k in range(0, len(level_values), 2)
                    ]
                last = unfolded[start + MIG : start + MIG + 8, column]
                values.append(jnp.where(bits[4], last, level_values[0]))
            real, imag = values
            cosine = cos_ref[at, columns[0]]
            sine = sin_ref[at, columns[0]]
            focused[at, columns[0]] = real * cosine - imag * sine
            focused[at, columns[1]] = real * sine + imag * cosine
        return carry

    lax.fori_loop(0, length // LANES, focus_band, 0)


def inverse_rows(focused, final_ref, twiddle_ref, at):
    group = LANES // 4
    rows = at.stop - at.start
    line = lax.broadcasted_iota(jnp.int32, (rows, LANES), 1) // group
    parts = []
    for part in range(2):
        base = part * 4 * LANES
        turned = []
        for b in range(4):
            value = focused[at, base + b * LANES : base + (b + 1) * LANES]
            turned.append(value if b == 0 else pltpu.roll(value, b * group, 1))
        grouped = []
        for j in range(4):
            value = turned[(0 - j) % 4]
            for g in range(1, 4):
                value = jnp.where(line == g, turned[(g - j) % 4], value)
            grouped.append(value if j == 0 else pltpu.roll(value, LANES - j * group, 1))
        parts.append(grouped)
    stacked = jnp.concatenate(
        [jnp.concatenate([parts[0][j], parts[1][j]], axis=1) for j in range(4)], axis=0
    )
    image = dot_right(stacked, final_ref)
    real, imag = [], []
    for j in range(4):
        r = image[j * rows : (j + 1) * rows, :LANES]
        i = image[j * rows : (j + 1) * rows, LANES:]
        if j > 0:
            t_r, t_i = twiddle_ref[0, j : j + 1, :], twiddle_ref[1, j : j + 1, :]
            r, i = r * t_r - i * t_i, r * t_i + i * t_r
        real.append(r)
        imag.append(i)
    a_r, a_i = real[0] + real[2], imag[0] + imag[2]
    b_r, b_i = real[0] - real[2], imag[0] - imag[2]
    c_r, c_i = real[1] + real[3], imag[1] + imag[3]
    d_r, d_i = imag[3] - imag[1], real[1] - real[3]
    return (
        jnp.concatenate([a_r + c_r, b_r + d_r, a_r - c_r, b_r - d_r], axis=1),
        jnp.concatenate([a_i + c_i, b_i + d_i, a_i - c_i, b_i - d_i], axis=1),
    )


def compress_kernel(
    sizes,
    x_hbm,
    chirp_hbm,
    rate_hbm,
    band_hbm,
    migration_hbm,
    first_hbm,
    twiddle_hbm,
    fwd_hbm,
    inv_hbm,
    last_hbm,
    halo_hbm,
    reconstruction_hbm,
    delays_hbm,
    order_hbm,
    recv_ref,
    cos_hbm,
    sin_hbm,
    shift_hbm,
    mix_hbm,
    x_ref,
    chirp_ref,
    rate_ref,
    band_ref,
    migration_ref,
    first_ref,
    twiddle_ref,
    fwd_ref,
    inv_ref,
    last_ref,
    halo_ref,
    reconstruction_ref,
    delays_ref,
    order_ref,
    send_ref,
    rows_ref,
    cos_ref,
    sin_ref,
    shift_ref,
    mix_ref,
    load_sems,
    store_sems,
    local_sem,
    send_sems,
    recv_sems,
):
    pulses, channels, lead, devices, inner, length = sizes
    mine = lax.axis_index("az") * inner + lax.axis_index("rg")
    barrier = pltpu.get_barrier_semaphore()

    def place(index):
        return (lax.div(index, inner), lax.rem(index, inner))

    def greet(k, carry):
        pl.semaphore_signal(
            barrier,
            inc=1,
            device_id=place(lax.rem(mine + k, devices)),
            device_id_type=pl.DeviceIdType.MESH,
        )
        return carry

    loads = []

    def start_load(source, target):
        copy = pltpu.make_async_copy(source, target, load_sems.at[len(loads)])
        copy.start()
        loads.append(copy)
        return copy

    def pulse_load(p):
        at = pl.ds(p * channels, channels)
        return start_load(x_hbm.at[at], x_ref.at[at])

    load_x = [pulse_load(0)]
    load_first = start_load(first_hbm, first_ref)
    load_twiddle = start_load(twiddle_hbm, twiddle_ref)
    load_fwd = start_load(fwd_hbm, fwd_ref)
    load_chirp = start_load(chirp_hbm, chirp_ref)
    load_inv = start_load(inv_hbm, inv_ref)
    load_last = start_load(last_hbm, last_ref)
    load_x += [pulse_load(p) for p in range(1, pulses)]
    load_halo = start_load(halo_hbm, halo_ref)
    load_rate = start_load(rate_hbm, rate_ref)
    load_band = start_load(band_hbm, band_ref)
    load_migration = start_load(migration_hbm, migration_ref)
    load_reconstruction = start_load(reconstruction_hbm, reconstruction_ref)
    load_delays = start_load(delays_hbm, delays_ref)
    load_order = start_load(order_hbm, order_ref)
    lax.fori_loop(1, devices, greet, 0)

    rows = pulses * channels * 4 + HALO_ROWS
    cut = channels * 4

    def remote(chunk, i):
        far = lax.div(i + 1, 2)
        step = devices // 2 + far - 2 * far * lax.rem(i, 2)
        target = lax.rem(mine + step, devices)
        at = pl.ds(0, cut) if chunk == 0 else pl.ds(cut, rows - cut)
        return pltpu.make_async_remote_copy(
            src_ref=send_ref.at[target, at],
            dst_ref=recv_ref.at[mine, at],
            send_sem=send_sems.at[chunk, step],
            recv_sem=recv_sems.at[chunk, step],
            device_id=place(target),
            device_id_type=pl.DeviceIdType.MESH,
        )

    def send(chunk):
        def body(i, carry):
            remote(chunk, i).start()
            return carry

        lax.fori_loop(0, devices - 1, body, 0)

    lane = lax.broadcasted_iota(jnp.int32, (2 * lead, LANES), 1)
    groups = pulses * channels * MIG // LANES
    per_group = LANES // MIG
    pairs = channels // 2
    packs = [jnp.zeros((2 * lead, LANES), jnp.float32) for _ in range(groups)]
    for p in range(pulses):
        load_x[p].wait()
        if p == 0:
            load_first.wait()
        x = jnp.concatenate([x_ref[p * channels + c] for c in range(channels)], axis=1)
        y = dot_left(first_ref, x)
        if p == 0:
            load_twiddle.wait()
            load_fwd.wait()
            load_chirp.wait()
            load_inv.wait()
            tw_r = jnp.concatenate([twiddle_ref[0]] * channels, axis=0)
            tw_i = jnp.concatenate([twiddle_ref[1]] * channels, axis=0)
            chirp = jnp.concatenate(
                [chirp_ref[pl.ds(part, lead, stride=2), :] for part in range(2)], axis=0
            ).T
            top, bottom = chirp[:lead], chirp[lead:]
            left = lane[:lead] < lead
            chirp_r = jnp.where(left, top, pltpu.roll(bottom, lead, 1))
            chirp_i = jnp.where(left, pltpu.roll(top, lead, 1), bottom)
            chirp_r = jnp.concatenate([chirp_r] * channels, axis=0)
            chirp_i = jnp.concatenate([chirp_i] * channels, axis=0)
        y = jnp.concatenate([y[:, c * LANES : (c + 1) * LANES] for c in range(channels)], axis=0)
        y = y.reshape(channels, 2, lead, LANES)
        y_r = y[:, 0].reshape(channels * lead, LANES)
        y_i = y[:, 1].reshape(channels * lead, LANES)
        y = jnp.concatenate([y_r * tw_r - y_i * tw_i, y_r * tw_i + y_i * tw_r], axis=1)
        s = dot_right(y, fwd_ref)
        s_r, s_i = s[:, :LANES], s[:, LANES:]
        s = jnp.concatenate(
            [s_r * chirp_r + s_i * chirp_i, s_i * chirp_r - s_r * chirp_i], axis=1
        )
        t = dot_right(s, inv_ref)
        t_r, t_i = t[:, :LANES], t[:, LANES:]
        z_r = t_r * tw_r + t_i * tw_i
        z_i = t_i * tw_r - t_r * tw_i
        z = [
            jnp.concatenate(
                [z_r[c * lead : (c + 1) * lead], z_i[c * lead : (c + 1) * lead]], axis=0
            )
            for c in range(channels)
        ]
        stacked = jnp.concatenate(
            [jnp.concatenate([z[2 * k], z[2 * k + 1]], axis=0) for k in range(pairs)], axis=1
        )
        if p == 0:
            load_last.wait()
        w = dot_left(last_ref, stacked)
        for k in range(pairs):
            row = (p * pairs + k) * 8
            send_ref[:, row : row + 8, :] = w[:, k * LANES : (k + 1) * LANES].reshape(
                devices, 8, LANES
            )
        for c in range(channels):
            signal = p * channels + c
            g, where = signal // per_group, signal % per_group
            moved = z[c] if where == 0 else pltpu.roll(z[c], where * MIG, 1)
            packs[g] = jnp.where(lane // MIG == where, moved, packs[g])
        if p == 0:
            pl.semaphore_wait(barrier, devices - 1)
            send(0)
    load_halo.wait()
    w = dot_left(halo_ref, jnp.concatenate(packs, axis=1))
    row = lax.broadcasted_iota(jnp.int32, (devices * HALO_ROWS, LANES), 0) % HALO_ROWS
    total = w[:, :LANES]
    for g in range(1, groups):
        total = jnp.where(row // 2 == g, w[:, g * LANES : (g + 1) * LANES], total)
    send_ref[:, pulses * channels * 4 :, :] = total.reshape(devices, HALO_ROWS, LANES)
    send(1)
    own = pltpu.make_async_copy(send_ref.at[mine], recv_ref.at[mine], local_sem)
    own.start()

    load_reconstruction.wait()
    load_delays.wait()
    load_order.wait()
    bins_f = pulses * devices
    shape = (channels * channels, bins_f)
    row = lax.broadcasted_iota(jnp.int32, shape, 0) % channels
    frequency = doppler_of(lax.broadcasted_iota(jnp.int32, shape, 1))
    delay = jnp.zeros_like(row)
    for c in range(channels):
        one = jnp.broadcast_to(delays_ref[0:1, c : c + 1], row.shape)
        delay = jnp.where(row == c, one, delay)
    turns = lax.rem(frequency * delay, bins_f).astype(jnp.float32) * (1.0 / bins_f)
    align_r, align_i = cos_sin_turns(turns)
    rec_r = dot_exact(reconstruction_ref[0], order_ref[...])
    rec_i = dot_exact(reconstruction_ref[1], order_ref[...])
    mix_ref[0] = rec_r * align_r - rec_i * align_i
    mix_ref[1] = rec_r * align_i + rec_i * align_r

    load_rate.wait()
    load_band.wait()
    load_migration.wait()
    rows_ref[0] = spread_rows(rate_ref[...])
    rows_ref[1] = spread_rows(band_ref[...].astype(jnp.float32))
    rows_ref[2] = spread_rows(migration_ref[...].astype(jnp.float32))
    bins = rows_ref.shape[1]

    def tables(index, carry):
        at = pl.ds(pl.multiple_of(index * 8, 8), 8)
        rate = rows_ref[0, at, :]
        band = rows_ref[1, at, :].astype(jnp.int32)
        move = rows_ref[2, at, :].astype(jnp.int32)
        band_square = band * band
        for start in range(0, length, LANES):
            doppler = doppler_of(lax.broadcasted_iota(jnp.int32, (8, LANES), 1)) + start
            centred = jnp.where(doppler >= length // 2, doppler - length, doppler)
            relative = centred.astype(jnp.float32) * (2.0 / length)
            cosine, sine = cos_sin_turns(rate * (relative * relative * (curvature / 2.0)))
            inside = jnp.abs(centred) < band
            columns = slice(start, start + LANES)
            cos_ref[at, columns] = jnp.where(inside, cosine, 0.0)
            sin_ref[at, columns] = jnp.where(inside, sine, 0.0)
            reach = move * jnp.minimum(centred * centred, band_square) + (band_square >> 1)
            shift = jnp.zeros((8, LANES), jnp.int32)
            bound = band_square
            for offset in range(1, MIG + 1):
                shift = jnp.where(reach >= bound, offset, shift)
                bound = bound + band_square
            shift_ref[at, columns] = shift
        return carry

    lax.fori_loop(0, bins // 8, tables, 0)
    stores = []
    for source, target in (
        (cos_ref, cos_hbm),
        (sin_ref, sin_hbm),
        (shift_ref, shift_hbm),
        (mix_ref, mix_hbm),
    ):
        copy = pltpu.make_async_copy(source, target, store_sems.at[len(stores)])
        copy.start()
        stores.append(copy)
    for copy in stores:
        copy.wait()
    own.wait()

    def finish(i, carry):
        for chunk in range(2):
            copy = remote(chunk, i)
            copy.wait_send()
            copy.wait_recv()
        return carry

    lax.fori_loop(0, devices - 1, finish, 0)


def azimuth_kernel(
    sizes,
    recv_hbm,
    doppler_hbm,
    halo_doppler_hbm,
    mix_hbm,
    shift_hbm,
    cos_hbm,
    sin_hbm,
    final_hbm,
    twiddle_hbm,
    out_hbm,
    recv_ref,
    doppler_ref,
    halo_doppler_ref,
    mix_ref,
    shift_ref,
    cos_ref,
    sin_ref,
    final_ref,
    twiddle_ref,
    spectra,
    unfolded,
    focused,
    image_ref,
    load_sems,
    store_sems,
):
    sources, local_pulses, channels, bins = sizes
    block = local_pulses * channels * 4 + HALO_ROWS
    loads = []

    def load(source, target):
        copy = pltpu.make_async_copy(source, target, load_sems.at[len(loads)])
        copy.start()
        loads.append(copy)
        return copy

    load_doppler = load(doppler_hbm, doppler_ref)
    load_recv = load(recv_hbm, recv_ref)
    load_halo_doppler = load(halo_doppler_hbm, halo_doppler_ref)
    load_mix = load(mix_hbm, mix_ref)
    load_tables = [
        load(shift_hbm, shift_ref),
        load(cos_hbm, cos_ref),
        load(sin_hbm, sin_ref),
    ]
    load_final = [load(final_hbm, final_ref), load(twiddle_hbm, twiddle_ref)]

    flat = recv_ref.reshape(sources * block, LANES)

    def rows_of(start):
        return flat[pl.ds(start, sources, stride=block), :]

    load_doppler.wait()
    load_recv.wait()
    for c in range(channels):
        for half in range(bins // LANES):
            z = jnp.concatenate(
                [
                    rows_of(p * channels * 4 + c * 4 + part * 2 + half)
                    for part in range(2)
                    for p in range(local_pulses)
                ],
                axis=0,
            )
            spectra[c, half * LANES : (half + 1) * LANES, :] = dot_right(z.T, doppler_ref)
    groups = local_pulses * channels * MIG // LANES
    per_group = LANES // (MIG * channels)
    load_halo_doppler.wait()
    h = jnp.concatenate(
        [rows_of(local_pulses * channels * 4 + j) for j in range(2 * groups)], axis=0
    ).T
    step = channels * MIG
    halo = dot_right(h[:step], halo_doppler_ref.at[0])
    for k in range(1, per_group):
        halo = halo + dot_right(h[k * step : (k + 1) * step], halo_doppler_ref.at[k])
    for c in range(channels):
        spectra[c, bins:, :] = halo[c * MIG : (c + 1) * MIG]
    load_mix.wait()
    mix_channels(spectra, mix_ref, unfolded, bins + MIG, 0)
    for copy in load_tables:
        copy.wait()
    migrate_rows(unfolded, cos_ref, sin_ref, shift_ref, focused, bins)
    for copy in load_final:
        copy.wait()
    stores = []
    piece = LANES // 2
    for k in range(bins // piece):
        at = slice(k * piece, (k + 1) * piece)
        real, imag = inverse_rows(focused, final_ref, twiddle_ref, at)
        image_ref[0, at, :] = real
        image_ref[1, at, :] = imag
        rows = pl.ds(k * piece, piece)
        copy = pltpu.make_async_copy(
            image_ref.at[:, rows], out_hbm.at[:, rows], store_sems.at[k]
        )
        copy.start()
        stores.append(copy)
    for copy in stores:
        copy.wait()


def fits(pulses, channels, length, devices):
    local_pulses = pulses // devices
    signals = local_pulses * channels
    bins = length // devices
    lead = length // LANES
    return (
        pulses == LANES
        and length % (LANES * devices) == 0
        and bins == 2 * LANES
        and channels == 4
        and 2 * lead == LANES
        and devices % 8 == 0
        and signals * MIG % LANES == 0
        and LANES % (MIG * channels) == 0
        and 2 * (signals * MIG // LANES) <= HALO_ROWS
        and channels * pulses <= 512
    )


def hbm():
    return pl.BlockSpec(memory_space=pltpu.HBM)


def vmem():
    return pl.BlockSpec(memory_space=pltpu.VMEM)


def blocked_local(
    raw_echoes, chirp_spectrum, reconstruction, delays, azimuth_rate, band_halfwidth, migration
):
    local_pulses, channels, _, length = raw_echoes.shape
    inner = lax.axis_size("rg")
    devices = lax.axis_size("az") * inner
    bins = length // devices
    lead = length // LANES
    pulses = local_pulses * devices
    signals = local_pulses * channels
    doppler_bins = channels * pulses
    leads = np.arange(lead)
    lanes = np.arange(LANES)

    first = left_matrix(*roots(leads, leads, lead, -1.0))
    first = first.transpose(0, 1, 3, 2).reshape(2 * lead, 2 * lead)
    turned = np.concatenate([lanes[0::2], lanes[1::2]])
    forward = right_matrix(*roots(lanes, turned, LANES, -1.0)).reshape(2 * LANES, 2 * LANES)
    inverse = right_matrix(*roots(turned, lanes, LANES, 1.0)).reshape(2 * LANES, 2 * LANES)
    last = left_matrix(*roots(leads, leads, lead, 1.0)) / length
    pair = np.zeros((devices, 2, 2, 2, 2, 2 * lead))
    by_device = last.reshape(2, devices, 2, 2 * lead).transpose(1, 0, 2, 3)
    for s in range(2):
        pair[:, s, :, :, s, :] = by_device
    pair = pair.reshape(devices * 8, 4 * lead)
    halo = np.zeros((devices, HALO_ROWS, 2 * lead))
    groups = signals * MIG // LANES
    for g in range(groups):
        halo[:-1, 2 * g : 2 * g + 2] = by_device[1:, :, 0]
    halo = halo.reshape(devices * HALO_ROWS, 2 * lead)
    twiddles = np.stack(roots(leads, lanes, length, -1.0)).astype(np.float32)

    sources = np.arange(devices)
    bins_f = doppler_of(np.arange(pulses))
    order_f = (np.arange(pulses)[:, None] == bins_f[None, :]).astype(ml_dtypes.bfloat16)
    order = (np.arange(local_pulses)[:, None] + sources[None, :] * local_pulses).reshape(-1)
    scale = 1.0 / math.sqrt(pulses)
    to_doppler = right_matrix(*roots(order, bins_f, pulses, -1.0)) * scale
    to_doppler = to_doppler.reshape(2 * pulses, 2 * pulses)
    per_group = local_pulses // groups
    halo_doppler = []
    for k in range(per_group):
        by_group = []
        for g in range(groups):
            at = sources * local_pulses + g * per_group + k
            by_group.append(
                (right_matrix(*roots(at, bins_f, pulses, -1.0)) * scale).reshape(
                    2 * devices, 2 * pulses
                )
            )
        halo_doppler.append(split_constant(np.concatenate(by_group, axis=0)))
    halo_doppler = np.stack(halo_doppler)
    final = right_matrix(*roots(lanes, lanes, LANES, 1.0)) / math.sqrt(doppler_bins)
    final = split_constant(final.reshape(2 * LANES, 2 * LANES))
    regroup = np.stack(roots(np.arange(8) % 4, lanes, doppler_bins, 1.0)).astype(np.float32)

    x = raw_echoes.reshape(signals, 2, lead, LANES).transpose(0, 2, 1, 3)
    x = x.reshape(signals, 2 * lead, LANES)
    chirp = chirp_spectrum.reshape(2, lead, LANES).transpose(1, 0, 2).reshape(2 * lead, LANES)
    block = signals * 4 + HALO_ROWS
    tables = (bins, doppler_bins)
    by_lane = (bins // LANES, LANES)
    operands = (
        x,
        chirp,
        azimuth_rate.reshape(by_lane),
        band_halfwidth.reshape(by_lane),
        migration.reshape(by_lane),
        split_constant(first),
        twiddles,
        split_constant(forward),
        split_constant(inverse),
        split_constant(pair),
        split_constant(halo),
        reconstruction.reshape(2, channels * channels, pulses),
        delays.reshape(1, channels),
        order_f,
    )
    received, cosine, sine, shift, mix = pl.pallas_call(
        functools.partial(
            compress_kernel, (local_pulses, channels, lead, devices, inner, doppler_bins)
        ),
        out_shape=(
            jax.ShapeDtypeStruct((devices, block, LANES), jnp.float32),
            jax.ShapeDtypeStruct(tables, jnp.float32),
            jax.ShapeDtypeStruct(tables, jnp.float32),
            jax.ShapeDtypeStruct(tables, jnp.int32),
            jax.ShapeDtypeStruct((2, channels * channels, pulses), jnp.float32),
        ),
        in_specs=[hbm()] * len(operands),
        out_specs=(hbm(),) * 5,
        scratch_shapes=[pltpu.VMEM(value.shape, value.dtype) for value in operands]
        + [
            pltpu.VMEM((devices, block, LANES), jnp.float32),
            pltpu.VMEM((3, bins, LANES), jnp.float32),
            pltpu.VMEM(tables, jnp.float32),
            pltpu.VMEM(tables, jnp.float32),
            pltpu.VMEM(tables, jnp.int32),
            pltpu.VMEM((2, channels * channels, pulses), jnp.float32),
            pltpu.SemaphoreType.DMA((len(operands) + local_pulses - 1,)),
            pltpu.SemaphoreType.DMA((4,)),
            pltpu.SemaphoreType.DMA,
            pltpu.SemaphoreType.DMA((2, devices)),
            pltpu.SemaphoreType.DMA((2, devices)),
        ],
        compiler_params=pltpu.CompilerParams(
            collective_id=0, has_side_effects=True, vmem_limit_bytes=KERNEL_VMEM
        ),
        name="compress_exchange",
    )(*operands)
    inputs = (
        received,
        split_constant(to_doppler),
        halo_doppler,
        mix,
        shift,
        cosine,
        sine,
        final,
        regroup,
    )
    return pl.pallas_call(
        functools.partial(azimuth_kernel, (devices, local_pulses, channels, bins)),
        out_shape=jax.ShapeDtypeStruct((2, bins, doppler_bins), jnp.float32),
        in_specs=[hbm()] * len(inputs),
        out_specs=hbm(),
        scratch_shapes=[pltpu.VMEM(value.shape, value.dtype) for value in inputs]
        + [
            pltpu.VMEM((channels, bins + MIG, 2 * pulses), jnp.float32),
            pltpu.VMEM((bins + MIG, 2 * doppler_bins), jnp.float32),
            pltpu.VMEM((bins, 2 * doppler_bins), jnp.float32),
            pltpu.VMEM((2, bins, doppler_bins), jnp.float32),
            pltpu.SemaphoreType.DMA((len(inputs),)),
            pltpu.SemaphoreType.DMA((2 * bins // LANES,)),
        ],
        compiler_params=pltpu.CompilerParams(vmem_limit_bytes=KERNEL_VMEM),
        name="azimuth_focus",
    )(*inputs)


def local(raw_echoes, chirp_spectrum, reconstruction, *rest):
    local_pulses, channels, _, length = raw_echoes.shape
    devices = lax.axis_size("az") * lax.axis_size("rg")
    if fits(local_pulses * devices, channels, length, devices):
        return blocked_local(raw_echoes, chirp_spectrum, reconstruction, *rest)
    return plain_local(raw_echoes, chirp_spectrum, reconstruction, *rest)


def solution(mesh):
    in_specs = (
        P(("az", "rg"), None, None, None),
        P(),
        P(),
        P(),
        P(("az", "rg")),
        P(("az", "rg")),
        P(("az", "rg")),
    )
    out_specs = P(None, ("az", "rg"), None)
    return jax.shard_map(local, mesh=mesh, in_specs=in_specs, out_specs=out_specs, check_vma=False)
```
